512 devices in a mesh: replica: 32 (over z, core), fsdp: 16 (over y, x).
Axes of the slice: x: 4, y: 4, z: 16, core: 2. Of those that a mesh axis runs over, the one named last changes fastest.
Arguments:
- weights: bfloat16 [3, 32, 28672], P(None, None, 'fsdp'), may hold values from -4 to 4
- local_weights: bfloat16 [32, 3, 32, 28672], P('replica', None, None, 'fsdp'), may hold values from -11 to 11
- carried_error: float32 [32, 3, 32, 28672], P('replica', None, None, 'fsdp'), may hold values from -4 to 4
- momentum: float32 [3, 32, 28672], P(None, None, 'fsdp'), may hold values from -4 to 4
- initial_factor: float32 [3, 32, 16], replicated, may hold values from -5 to 5
Outputs:
- next_weights: bfloat16 [3, 32, 28672], P(None, None, 'fsdp')
- next_error: float32 [32, 3, 32, 28672], P('replica', None, None, 'fsdp')
- next_momentum: float32 [3, 32, 28672], P(None, None, 'fsdp')
- following_factor: float32 [3, 32, 16], replicated
The draws below stay inside these ranges and needn't reach their ends.
All inputs are finite; a program needn't handle non-finite values.
Results may differ from the reference program's by a relative error of at most 0.001.
Values sent between devices are 32-bit elements; how exact they have to be, the bound alone decides.
No kernel may reach another device: no remote copies, remote signals or barrier semaphores. Data moves between devices by JAX's collectives and lax.ppermute only.
A program may use at most 64 MiB of HBM per device.

```python
import math
import jax
import jax.numpy as jnp
from jax import lax

FF = 28672
COLS = 32
RANK = 16
REPLICAS = 32
N_REPLICA = 32
N_FSDP = 16


def base_draw(key):
    return jnp.clip(jax.random.normal(key, (3, COLS, FF), jnp.float32), -4.0, 4.0)


def column_ramp(low_end):
    shard_width = FF // N_FSDP
    position = jnp.arange(FF, dtype=jnp.int32)
    within = (position % shard_width).astype(jnp.float32) / shard_width
    across = (position // shard_width).astype(jnp.float32) / N_FSDP
    fraction = 0.5 * within + 0.5 * across
    return jnp.exp(math.log(low_end) * (1.0 - fraction)).reshape(1, 1, FF)


def draw_weights(key, part):
    base_weights = base_draw(key)
    return base_weights.astype(jnp.bfloat16)


def draw_local_weights(key, part):
    base_weights = base_draw(key)
    key = jax.random.fold_in(key, 23)
    key_common, key_own, key_rows, key_cols = jax.random.split(key, 4)
    common = jnp.clip(jax.random.normal(key_common, (3, COLS, FF), jnp.float32), -4.0, 4.0)
    own_drift = jnp.clip(jax.random.normal(key_own, (REPLICAS, 3, COLS, FF), jnp.float32), -4.0, 4.0)
    col_scale = column_ramp(0.1) * jnp.exp(jax.random.uniform(key_cols, (3, 1, FF), jnp.float32, math.log(0.5), 0.0))
    row_scale = jnp.exp(jax.random.uniform(key_rows, (3, COLS, 1), jnp.float32, math.log(0.6), math.log(1.6)))
    drift = (0.6 * common[None] + 0.5 * own_drift) * (row_scale * col_scale)[None]
    return (base_weights[None] - drift).astype(jnp.bfloat16)


def levels(rng, extent, pieces, smallest, top_value):
    def one(dim, parts):
        draws = jax.random.uniform(jax.random.fold_in(jax.random.fold_in(rng, 6), dim), (parts,), jnp.float32, smallest / len(pieces), top_value / len(pieces))
        return jnp.repeat(jnp.exp(draws), extent[dim] // parts).reshape((-1,) + (1,) * (len(extent) - dim - 1))

    level = one(*pieces[0])
    for cut in pieces[1:]:
        level = level * one(*cut)
    return level


def centred(key, shape, scale, limit, shards=(), kind=jnp.bfloat16):
    array = jax.random.normal(key, shape, jnp.float32) * scale
    if len(shards) > 0:
        array = levels(key, shape, shards, -0.22, 0.18) * array
    return jnp.clip(array, min=-limit, max=limit).astype(kind)


def setup_inputs(seed: int = 0) -> dict:
    keys = jax.random.split(jax.random.key(seed), 6)
    return {
        "weights": draw_weights(jax.random.fold_in(keys[5], 71), 0),
        "local_weights": draw_local_weights(jax.random.fold_in(keys[5], 71), 0),
        "carried_error": centred(keys[2], (REPLICAS, 3, COLS, FF), 0.3, 4.0, ((0, 32), (3, 16)), jnp.float32),
        "momentum": centred(keys[3], (3, COLS, FF), 0.3, 4.0, ((2, 16),), jnp.float32),
        "initial_factor": centred(keys[4], (3, COLS, RANK), 1.0, 5.0, (), jnp.float32),
    }


def reference(weights, local_weights, carried_error, momentum, initial_factor):
    highest_precision = lax.Precision.HIGHEST
    weights_wide = weights.astype(jnp.float32)
    corrected_drift = weights_wide[None] - local_weights.astype(jnp.float32) + carried_error
    factor_reduced = jnp.einsum('nwz,tnwu->nzu', initial_factor, corrected_drift, precision=highest_precision)
    gram_reduced = jnp.einsum('vxq,vbq->vxb', factor_reduced, factor_reduced, precision=highest_precision)
    triangle = jnp.linalg.cholesky(gram_reduced)
    normalized_rows = lax.linalg.triangular_solve(triangle, factor_reduced, left_side=True, lower=True)
    following_factor = jnp.einsum('pbsw,bhw->bsh', corrected_drift, normalized_rows, precision=highest_precision) / N_REPLICA
    approximate_update = jnp.einsum('evi,eid->evd', following_factor, normalized_rows, precision=highest_precision)
    next_error = corrected_drift - approximate_update[None]
    next_momentum = 0.9 * momentum + approximate_update
    next_weights = (weights_wide - 0.7 * (approximate_update + 0.9 * next_momentum)).astype(jnp.bfloat16)
    return (next_weights, next_error, next_momentum, following_factor)
```

```python
import jax
import jax.numpy as jnp
from jax import lax
from jax.experimental import pallas as pl
from jax.experimental.pallas import tpu as pltpu
from jax.sharding import PartitionSpec as P

CHIPS = 16
BLOCK = 128
BLOCKS = 14
WIDTH = BLOCK * BLOCKS
MATS = 3
COLS = 32
RANK = 16
HALF = MATS * COLS // 2
HIGHEST = lax.Precision.HIGHEST
VMEM = pl.BlockSpec(memory_space=pltpu.VMEM)
SMEM = pl.BlockSpec(memory_space=pltpu.SMEM)
HBM = pl.BlockSpec(memory_space=pl.ANY)
PARAMS = pltpu.CompilerParams(vmem_limit_bytes=32 * 1024 * 1024)


def slot_of(distance):
    up = distance + 1
    return (up & 3) * 4 + ((up >> 2) & 3)


def pack_kernel(ids, w, lw, ce, keep, send):
    z, core = ids[0], ids[1]
    mine = pl.multiple_of(16 * core, 16)
    other = pl.multiple_of(16 - 16 * core, 16)
    for block in range(CHIPS):
        slot = slot_of((block - z) & 15)
        if block >= BLOCKS:
            keep[slot] = jnp.zeros((HALF, BLOCK), jnp.float32)
            send[slot] = jnp.zeros((HALF, BLOCK), jnp.float32)
            continue
        lanes = slice(block * BLOCK, (block + 1) * BLOCK)
        for mat in range(MATS):
            rows = slice(16 * mat, 16 * mat + 16)
            for start, out in ((mine, keep), (other, send)):
                part = pl.ds(start, 16)
                out[slot, rows] = (
                    w[mat, part, lanes].astype(jnp.float32)
                    - lw[mat, part, lanes].astype(jnp.float32)
                    + ce[mat, part, lanes]
                )


def factor_kernel(ids, qt, own, sib, inner, factor):
    first = ids[1] == 0
    inner[...] = jnp.zeros_like(inner)
    for mat in range(MATS):
        rows = slice(16 * mat, 16 * mat + 16)
        mine, other = own[rows], sib[rows]
        drift = jnp.concatenate(
            [jnp.where(first, mine, other), jnp.where(first, other, mine)], axis=0
        )
        projected = jnp.dot(
            qt[mat], drift, precision=HIGHEST, preferred_element_type=jnp.float32
        )
        both = jnp.concatenate([projected, drift], axis=0)
        inner[rows, 0 : RANK + COLS] = lax.dot_general(
            projected,
            both,
            (((1,), (1,)), ((), ())),
            precision=HIGHEST,
            preferred_element_type=jnp.float32,
        )
        factor[8 * mat : 8 * mat + 8] = jnp.where(first, projected[0:8], projected[8:16])


def final_kernel(
    islands, ids, inner, fown, fsib, w, lw, ce, mom,
    out_w, out_e, out_m, out_f, fac, buf_w, buf_e, buf_m, sems,
):
    z, core = ids[0], ids[1]
    mine = pl.multiple_of(8 * core, 8)
    other = pl.multiple_of(8 - 8 * core, 8)
    for block in range(BLOCKS):
        slot = slot_of((z - block) & 15)
        lanes = slice(block * BLOCK, (block + 1) * BLOCK)
        for mat in range(MATS):
            rows = slice(8 * mat, 8 * mat + 8)
            fac[mat, pl.ds(mine, 8), lanes] = fown[slot, rows]
            fac[mat, pl.ds(other, 8), lanes] = fsib[slot, rows]

    shape = (MATS, RANK, BLOCK)
    row = lax.broadcasted_iota(jnp.int32, shape, 1)
    lane = lax.broadcasted_iota(jnp.int32, shape, 2)
    table = inner[...].reshape(shape)
    table = jnp.where(lane == row + (RANK + COLS), 1.0, table)
    for step in range(RANK):
        scale = lax.rsqrt(table[:, step : step + 1, step : step + 1])
        pivot = table[:, step : step + 1, :] * scale
        column = table[:, :, step : step + 1] * scale
        table = jnp.where(
            row == step, pivot, jnp.where(row > step, table - column * pivot, table)
        )
    for mat in range(MATS):
        small = table[mat, :, RANK : RANK + COLS] * (1.0 / islands)
        out_f[mat] = small
        inverse = table[mat, :, RANK + COLS : 2 * RANK + COLS]
        mixed = lax.dot_general(
            small, inverse, (((0,), (0,)), ((), ())),
            precision=HIGHEST, preferred_element_type=jnp.float32,
        )
        for tile in range(7):
            lanes = slice(tile * 256, (tile + 1) * 256)
            approx = jnp.dot(
                mixed, fac[mat, :, lanes],
                precision=HIGHEST, preferred_element_type=jnp.float32,
            )
            wide = w[mat, :, lanes].astype(jnp.float32)
            drift = wide - lw[mat, :, lanes].astype(jnp.float32) + ce[mat, :, lanes]
            momentum = 0.9 * mom[mat, :, lanes] + approx
            buf_e[mat, :, lanes] = drift - approx
            buf_m[mat, :, lanes] = momentum
            buf_w[mat, :, lanes] = (wide - 0.7 * (approx + 0.9 * momentum)).astype(jnp.bfloat16)
        for kind, (buf, out) in enumerate(((buf_w, out_w), (buf_e, out_e), (buf_m, out_m))):
            pltpu.make_async_copy(buf.at[mat], out.at[mat], sems.at[kind, mat]).start()
    for mat in range(MATS):
        for kind, (buf, out) in enumerate(((buf_w, out_w), (buf_e, out_e), (buf_m, out_m))):
            pltpu.make_async_copy(buf.at[mat], out.at[mat], sems.at[kind, mat]).wait()


def sibling(x):
    return lax.ppermute(x, "replica", [(i, i ^ 1) for i in range(2 * CHIPS)])


def along_z(x, distance):
    return lax.ppermute(
        x, "replica", [(i, (i + 2 * distance) % (2 * CHIPS)) for i in range(2 * CHIPS)]
    )


def along_x(x, distance):
    return lax.ppermute(x, "fsdp", [(i, (i & 12) + ((i + distance) & 3)) for i in range(16)])


def along_y(x, distance):
    return lax.ppermute(x, "fsdp", [(i, (i + 4 * distance) & 15) for i in range(16)])


def sum_of_four(x, move, distances):
    return x + (move(x, distances[0]) + move(x, distances[1])) + move(x, distances[2])


def local(weights, local_weights, carried_error, momentum, initial_factor):
    f32 = jnp.float32
    index = lax.axis_index("replica")
    ids = jnp.stack([index >> 1, index & 1]).astype(jnp.int32)
    lw, ce = local_weights[0], carried_error[0]
    keep, send = pl.pallas_call(
        pack_kernel,
        out_shape=[jax.ShapeDtypeStruct((CHIPS, HALF, BLOCK), f32)] * 2,
        in_specs=[SMEM, VMEM, VMEM, VMEM],
        out_specs=[VMEM, VMEM],
        compiler_params=PARAMS,
        name="pack",
    )(ids, weights, lw, ce)
    got = sibling(send)
    shares = [keep[4 * a : 4 * a + 4] + got[4 * a : 4 * a + 4] for a in range(4)]
    part = shares[1] + (along_z(shares[2], 1) + along_z(shares[0], -1)) + along_z(shares[3], 2)
    own = part[0] + (along_z(part[1], 4) + along_z(part[3], 12)) + along_z(part[2], 8)
    qt = jnp.swapaxes(initial_factor, 1, 2)
    inner, factor = pl.pallas_call(
        factor_kernel,
        out_shape=[
            jax.ShapeDtypeStruct((HALF, BLOCK), f32),
            jax.ShapeDtypeStruct((HALF // 2, BLOCK), f32),
        ],
        in_specs=[SMEM, VMEM, VMEM, VMEM],
        out_specs=[VMEM, VMEM],
        compiler_params=PARAMS,
        name="factor",
    )(ids, qt, own, sibling(own))

    four = jnp.stack([factor, along_z(factor, 4), along_z(factor, 8), along_z(factor, 12)])
    fown = jnp.concatenate([along_z(four, -1), four, along_z(four, 1), along_z(four, 2)])
    fsib = sibling(fown)

    inner = sum_of_four(inner, along_x, (1, 3, 2))
    inner = sum_of_four(inner, along_y, (1, 3, 2))
    inner = sum_of_four(inner, along_z, (4, 12, 8))
    inner = sum_of_four(inner, along_z, (1, -1, 2))

    shape = (MATS, COLS, WIDTH)
    next_weights, next_error, next_momentum, following = pl.pallas_call(
        lambda *refs: final_kernel(lax.axis_size("replica"), *refs),
        out_shape=[
            jax.ShapeDtypeStruct(shape, jnp.bfloat16),
            jax.ShapeDtypeStruct(shape, f32),
            jax.ShapeDtypeStruct(shape, f32),
            jax.ShapeDtypeStruct((MATS, RANK, COLS), f32),
        ],
        in_specs=[SMEM] + [VMEM] * 7,
        out_specs=[HBM, HBM, HBM, VMEM],
        scratch_shapes=[
            pltpu.VMEM((MATS, RANK, WIDTH), f32),
            pltpu.VMEM(shape, jnp.bfloat16),
            pltpu.VMEM(shape, f32),
            pltpu.VMEM(shape, f32),
            pltpu.SemaphoreType.DMA((3, 3)),
        ],
        compiler_params=PARAMS,
        name="final",
    )(ids, inner, fown, fsib, weights, lw, ce, momentum)
    return (next_weights, next_error[None], next_momentum, jnp.swapaxes(following, 1, 2))


def solution(mesh):
    return jax.shard_map(
        local,
        mesh=mesh,
        in_specs=(
            P(None, None, "fsdp"),
            P("replica", None, None, "fsdp"),
            P("replica", None, None, "fsdp"),
            P(None, None, "fsdp"),
            P(),
        ),
        out_specs=(
            P(None, None, "fsdp"),
            P("replica", None, None, "fsdp"),
            P(None, None, "fsdp"),
            P(),
        ),
        check_vma=False,
    )
```

```python
import jax
import jax.numpy as jnp
from jax import lax
from jax.experimental import pallas as pl
from jax.experimental.pallas import tpu as pltpu
from jax.sharding import PartitionSpec as P

CHIPS = 16
BLOCK = 128
SIDE = BLOCK // 2
BLOCKS = 14
WIDTH = BLOCK * BLOCKS
MATS = 3
COLS = 32
RANK = 16
SHARE = MATS * COLS // 2
FROWS = SHARE // 2
PAIR = RANK + COLS
HIGHEST = lax.Precision.HIGHEST
VMEM = pl.BlockSpec(memory_space=pltpu.VMEM)
SMEM = pl.BlockSpec(memory_space=pltpu.SMEM)
HBM = pl.BlockSpec(memory_space=pl.ANY)
PARAMS = pltpu.CompilerParams(vmem_limit_bytes=32 * 1024 * 1024)
PACK_PARAMS = pltpu.CompilerParams(vmem_limit_bytes=56 * 1024 * 1024)


def swap_sides(x):
    return pltpu.roll(x, SIDE, 1)


def left_side(rows):
    return lax.broadcasted_iota(jnp.int32, (rows, BLOCK), 1) < SIDE


def pack_kernel(core_ref, w_hbm, lw_hbm, ce_hbm, keep, send, drift, w, lw, ce, sems):
    core = core_ref[0]
    copies = [
        [
            pltpu.make_async_copy(src.at[mat], dst.at[mat], sems.at[kind, mat])
            for kind, (src, dst) in enumerate(((ce_hbm, ce), (w_hbm, w), (lw_hbm, lw)))
        ]
        for mat in range(MATS)
    ]
    for group in copies:
        for copy in group:
            copy.start()
    left = left_side(16)
    for out in (keep, send):
        out[BLOCKS:CHIPS] = jnp.zeros((CHIPS - BLOCKS, SHARE, BLOCK), jnp.float32)
    for mat in range(MATS):
        for copy in copies[mat]:
            copy.wait()
        for block in range(BLOCKS):
            lanes = slice(block * BLOCK, (block + 1) * BLOCK)
            value = (
                w[mat, :, lanes].astype(jnp.float32)
                - lw[mat, :, lanes].astype(jnp.float32)
                + ce[mat, :, lanes]
            )
            drift[mat, :, lanes] = value
    for block in range(BLOCKS):
        lanes = slice(block * BLOCK, (block + 1) * BLOCK)
        keep[block, 0:COLS] = drift[2 * core, :, lanes]
        send[block, 0:COLS] = drift[2 - 2 * core, :, lanes]
        top, bottom = drift[1, 0:16, lanes], drift[1, 16:32, lanes]
        first = jnp.where(left, top, swap_sides(bottom))
        second = jnp.where(left, swap_sides(top), bottom)
        keep[block, COLS:SHARE] = jnp.where(core == 0, first, second)
        send[block, COLS:SHARE] = jnp.where(core == 0, second, first)


def products(factor, drift):
    return lax.dot_general(
        factor,
        jnp.concatenate([factor, drift], axis=0),
        (((1,), (1,)), ((), ())),
        precision=HIGHEST,
        preferred_element_type=jnp.float32,
    )


def factor_kernel(core_ref, qt, got, inner, factor):
    core = core_ref[0]
    total = jnp.sum(got[...], axis=0)
    left = left_side(16)
    whole = total[0:COLS]
    half = total[COLS:SHARE]
    half = jnp.concatenate(
        [jnp.where(left, half, 0.0), jnp.where(left, swap_sides(half), 0.0)], axis=0
    )
    whole_factor = jnp.dot(
        qt[2 * core], whole, precision=HIGHEST, preferred_element_type=jnp.float32
    )
    half_factor = jnp.dot(qt[1], half, precision=HIGHEST, preferred_element_type=jnp.float32)
    factor[0:RANK] = whole_factor
    factor[RANK:FROWS] = half_factor[0:8] + swap_sides(half_factor[8:16])
    inner[...] = jnp.zeros_like(inner)
    inner[:, 0:PAIR] = products(whole_factor, whole)
    inner[:, PAIR : 2 * PAIR] = products(half_factor, half)


def final_kernel(
    islands, core_ref, own, sib, w, mom, drift,
    out_w, out_e, out_m, out_f, fac, buf_w, buf_e, buf_m, sems,
):
    first = core_ref[0] == 0
    left = left_side(8)
    for block in range(BLOCKS):
        lanes = slice(block * BLOCK, (block + 1) * BLOCK)
        mine, other = own[block, 0:FROWS], sib[block, 0:FROWS]
        low, high = jnp.where(first, mine, other), jnp.where(first, other, mine)
        fac[0, :, lanes] = low[0:RANK]
        fac[2, :, lanes] = high[0:RANK]
        low, high = low[RANK:FROWS], high[RANK:FROWS]
        fac[1, 0:8, lanes] = jnp.where(left, low, swap_sides(high))
        fac[1, 8:16, lanes] = jnp.where(left, swap_sides(low), high)

    mine = jnp.sum(own[:, FROWS : FROWS + RANK], axis=0)
    other = jnp.sum(sib[:, FROWS : FROWS + RANK], axis=0)
    middle = pltpu.roll(mine + other, BLOCK - PAIR, 1)
    table = jnp.stack([jnp.where(first, mine, other), middle, jnp.where(first, other, mine)])
    shape = (MATS, RANK, BLOCK)
    row = lax.broadcasted_iota(jnp.int32, shape, 1)
    lane = lax.broadcasted_iota(jnp.int32, shape, 2)
    table = jnp.where(lane < PAIR, table, jnp.where(lane == row + PAIR, 1.0, 0.0))
    for step in range(RANK):
        scale = lax.rsqrt(table[:, step : step + 1, step : step + 1])
        pivot = table[:, step : step + 1, :] * scale
        column = table[:, :, step : step + 1] * scale
        table = jnp.where(
            row == step, pivot, jnp.where(row > step, table - column * pivot, table)
        )
    for mat in range(MATS):
        small = table[mat, :, RANK:PAIR] * (1.0 / islands)
        out_f[mat] = small
        inverse = table[mat, :, PAIR : PAIR + RANK]
        mixed = lax.dot_general(
            small, inverse, (((0,), (0,)), ((), ())),
            precision=HIGHEST, preferred_element_type=jnp.float32,
        )
        for tile in range(7):
            lanes = slice(tile * 256, (tile + 1) * 256)
            approx = jnp.dot(
                mixed, fac[mat, :, lanes],
                precision=HIGHEST, preferred_element_type=jnp.float32,
            )
            wide = w[mat, :, lanes].astype(jnp.float32)
            momentum = 0.9 * mom[mat, :, lanes] + approx
            buf_e[mat, :, lanes] = drift[mat, :, lanes] - approx
            buf_m[mat, :, lanes] = momentum
            buf_w[mat, :, lanes] = (wide - 0.7 * (approx + 0.9 * momentum)).astype(jnp.bfloat16)
        for kind, (buf, out) in enumerate(((buf_w, out_w), (buf_e, out_e), (buf_m, out_m))):
            pltpu.make_async_copy(buf.at[mat], out.at[mat], sems.at[kind, mat]).start()
    for mat in range(MATS):
        for kind, (buf, out) in enumerate(((buf_w, out_w), (buf_e, out_e), (buf_m, out_m))):
            pltpu.make_async_copy(buf.at[mat], out.at[mat], sems.at[kind, mat]).wait()


def sibling(x):
    return lax.ppermute(x, "replica", [(i, i ^ 1) for i in range(2 * CHIPS)])


def exchange_z(x):
    groups = [[2 * chip + core for chip in range(CHIPS)] for core in range(2)]
    return lax.all_to_all(x, "replica", 0, 0, axis_index_groups=groups, tiled=True)


def local(weights, local_weights, carried_error, momentum, initial_factor):
    f32 = jnp.float32
    core = (lax.axis_index("replica") & 1).astype(jnp.int32).reshape(1)
    shape = (MATS, COLS, WIDTH)
    keep, send, drift = pl.pallas_call(
        pack_kernel,
        out_shape=[jax.ShapeDtypeStruct((CHIPS, SHARE, BLOCK), f32)] * 2
        + [jax.ShapeDtypeStruct(shape, f32)],
        in_specs=[SMEM, HBM, HBM, HBM],
        out_specs=[VMEM] * 3,
        scratch_shapes=[
            pltpu.VMEM(shape, jnp.bfloat16),
            pltpu.VMEM(shape, jnp.bfloat16),
            pltpu.VMEM(shape, f32),
            pltpu.SemaphoreType.DMA((3, 3)),
        ],
        compiler_params=PACK_PARAMS,
        name="pack",
    )(core, weights, local_weights[0], carried_error[0])
    shares = exchange_z(keep + sibling(send))
    inner, factor = pl.pallas_call(
        factor_kernel,
        out_shape=[
            jax.ShapeDtypeStruct((RANK, BLOCK), f32),
            jax.ShapeDtypeStruct((FROWS, BLOCK), f32),
        ],
        in_specs=[SMEM, VMEM, VMEM],
        out_specs=[VMEM, VMEM],
        compiler_params=PARAMS,
        name="factor",
    )(core, jnp.swapaxes(initial_factor, 1, 2), shares)

    inner = lax.all_to_all(
        jnp.broadcast_to(inner, (16, RANK, BLOCK)), "fsdp", 0, 0, tiled=True
    )
    inner = jnp.sum(inner, axis=0)
    rows = FROWS + RANK
    own = exchange_z(
        jnp.broadcast_to(jnp.concatenate([factor, inner]), (CHIPS, rows, BLOCK))
    )
    sib = sibling(own)

    next_weights, next_error, next_momentum, following = pl.pallas_call(
        lambda *refs: final_kernel(lax.axis_size("replica"), *refs),
        out_shape=[
            jax.ShapeDtypeStruct(shape, jnp.bfloat16),
            jax.ShapeDtypeStruct(shape, f32),
            jax.ShapeDtypeStruct(shape, f32),
            jax.ShapeDtypeStruct((MATS, RANK, COLS), f32),
        ],
        in_specs=[SMEM] + [VMEM] * 5,
        out_specs=[HBM, HBM, HBM, VMEM],
        scratch_shapes=[
            pltpu.VMEM((MATS, RANK, WIDTH), f32),
            pltpu.VMEM(shape, jnp.bfloat16),
            pltpu.VMEM(shape, f32),
            pltpu.VMEM(shape, f32),
            pltpu.SemaphoreType.DMA((3, 3)),
        ],
        compiler_params=PARAMS,
        name="final",
    )(core, own, sib, weights, momentum, drift)
    return (next_weights, next_error[None], next_momentum, jnp.swapaxes(following, 1, 2))


def solution(mesh):
    return jax.shard_map(
        local,
        mesh=mesh,
        in_specs=(
            P(None, None, "fsdp"),
            P("replica", None, None, "fsdp"),
            P("replica", None, None, "fsdp"),
            P(None, None, "fsdp"),
            P(),
        ),
        out_specs=(
            P(None, None, "fsdp"),
            P("replica", None, None, "fsdp"),
            P(None, None, "fsdp"),
            P(),
        ),
        check_vma=False,
    )
```

```python
import jax
import jax.numpy as jnp
from jax import lax
from jax.experimental import pallas as pl
from jax.experimental.pallas import tpu as pltpu
from jax.sharding import PartitionSpec as P

CHIPS = 16
BLOCK = 128
SIDE = BLOCK // 2
BLOCKS = 14
WIDTH = BLOCK * BLOCKS
MATS = 3
COLS = 32
RANK = 16
SHARE = MATS * COLS // 2
FROWS = SHARE // 2
PAIR = RANK + COLS
HIGHEST = lax.Precision.HIGHEST
VMEM = pl.BlockSpec(memory_space=pltpu.VMEM)
SMEM = pl.BlockSpec(memory_space=pltpu.SMEM)
HBM = pl.BlockSpec(memory_space=pl.ANY)
PARAMS = pltpu.CompilerParams(vmem_limit_bytes=32 * 1024 * 1024)
PACK_PARAMS = pltpu.CompilerParams(vmem_limit_bytes=56 * 1024 * 1024)


def slot_of(block):
    return (block & 3) * 4 + (block >> 2)


def swap_sides(x):
    return pltpu.roll(x, SIDE, 1)


def left_side(rows):
    return lax.broadcasted_iota(jnp.int32, (rows, BLOCK), 1) < SIDE


def pack_kernel(core_ref, w_hbm, lw_hbm, ce_hbm, keep, send, drift, w, lw, ce, sems):
    core = core_ref[0]
    copies = [
        [
            pltpu.make_async_copy(src.at[mat], dst.at[mat], sems.at[kind, mat])
            for kind, (src, dst) in enumerate(((ce_hbm, ce), (w_hbm, w), (lw_hbm, lw)))
        ]
        for mat in range(MATS)
    ]
    for group in copies:
        for copy in group:
            copy.start()
    left = left_side(16)
    for out in (keep, send):
        for block in range(BLOCKS, CHIPS):
            out[slot_of(block)] = jnp.zeros((SHARE, BLOCK), jnp.float32)
    for mat in range(MATS):
        for copy in copies[mat]:
            copy.wait()
        for block in range(BLOCKS):
            lanes = slice(block * BLOCK, (block + 1) * BLOCK)
            value = (
                w[mat, :, lanes].astype(jnp.float32)
                - lw[mat, :, lanes].astype(jnp.float32)
                + ce[mat, :, lanes]
            )
            drift[mat, :, lanes] = value
    for block in range(BLOCKS):
        lanes = slice(block * BLOCK, (block + 1) * BLOCK)
        slot = slot_of(block)
        keep[slot, 0:COLS] = drift[2 * core, :, lanes]
        send[slot, 0:COLS] = drift[2 - 2 * core, :, lanes]
        top, bottom = drift[1, 0:16, lanes], drift[1, 16:32, lanes]
        first = jnp.where(left, top, swap_sides(bottom))
        second = jnp.where(left, swap_sides(top), bottom)
        keep[slot, COLS:SHARE] = jnp.where(core == 0, first, second)
        send[slot, COLS:SHARE] = jnp.where(core == 0, second, first)


def products(factor, drift):
    return lax.dot_general(
        factor,
        jnp.concatenate([factor, drift], axis=0),
        (((1,), (1,)), ((), ())),
        precision=HIGHEST,
        preferred_element_type=jnp.float32,
    )


def factor_kernel(core_ref, qt, got, inner, factor):
    core = core_ref[0]
    total = jnp.sum(got[...], axis=0)
    left = left_side(16)
    whole = total[0:COLS]
    half = total[COLS:SHARE]
    half = jnp.concatenate(
        [jnp.where(left, half, 0.0), jnp.where(left, swap_sides(half), 0.0)], axis=0
    )
    whole_factor = jnp.dot(
        qt[2 * core], whole, precision=HIGHEST, preferred_element_type=jnp.float32
    )
    half_factor = jnp.dot(qt[1], half, precision=HIGHEST, preferred_element_type=jnp.float32)
    factor[0:RANK] = whole_factor
    factor[RANK:FROWS] = half_factor[0:8] + swap_sides(half_factor[8:16])
    inner[...] = jnp.zeros_like(inner)
    inner[:, 0:PAIR] = products(whole_factor, whole)
    inner[:, PAIR : 2 * PAIR] = products(half_factor, half)


def final_kernel(
    islands, core_ref, own, sib, w, mom, drift,
    out_w, out_e, out_m, out_f, fac, buf_w, buf_e, buf_m, sems,
):
    first = core_ref[0] == 0
    left = left_side(8)
    for block in range(BLOCKS):
        lanes = slice(block * BLOCK, (block + 1) * BLOCK)
        low, rows = block & 3, slice((block >> 2) * FROWS, (block >> 2) * FROWS + FROWS)
        mine, other = own[low, rows], sib[low, rows]
        low, high = jnp.where(first, mine, other), jnp.where(first, other, mine)
        fac[0, :, lanes] = low[0:RANK]
        fac[2, :, lanes] = high[0:RANK]
        low, high = low[RANK:FROWS], high[RANK:FROWS]
        fac[1, 0:8, lanes] = jnp.where(left, low, swap_sides(high))
        fac[1, 8:16, lanes] = jnp.where(left, swap_sides(low), high)

    mine = jnp.sum(own[:, 4 * FROWS : 4 * FROWS + RANK], axis=0)
    other = jnp.sum(sib[:, 4 * FROWS : 4 * FROWS + RANK], axis=0)
    middle = pltpu.roll(mine + other, BLOCK - PAIR, 1)
    table = jnp.stack([jnp.where(first, mine, other), middle, jnp.where(first, other, mine)])
    shape = (MATS, RANK, BLOCK)
    row = lax.broadcasted_iota(jnp.int32, shape, 1)
    lane = lax.broadcasted_iota(jnp.int32, shape, 2)
    table = jnp.where(lane < PAIR, table, jnp.where(lane == row + PAIR, 1.0, 0.0))
    for step in range(RANK):
        scale = lax.rsqrt(table[:, step : step + 1, step : step + 1])
        pivot = table[:, step : step + 1, :] * scale
        column = table[:, :, step : step + 1] * scale
        table = jnp.where(
            row == step, pivot, jnp.where(row > step, table - column * pivot, table)
        )
    for mat in range(MATS):
        small = table[mat, :, RANK:PAIR] * (1.0 / islands)
        out_f[mat] = small
        inverse = table[mat, :, PAIR : PAIR + RANK]
        mixed = lax.dot_general(
            small, inverse, (((0,), (0,)), ((), ())),
            precision=HIGHEST, preferred_element_type=jnp.float32,
        )
        for tile in range(7):
            lanes = slice(tile * 256, (tile + 1) * 256)
            approx = jnp.dot(
                mixed, fac[mat, :, lanes],
                precision=HIGHEST, preferred_element_type=jnp.float32,
            )
            wide = w[mat, :, lanes].astype(jnp.float32)
            momentum = 0.9 * mom[mat, :, lanes] + approx
            buf_e[mat, :, lanes] = drift[mat, :, lanes] - approx
            buf_m[mat, :, lanes] = momentum
            buf_w[mat, :, lanes] = (wide - 0.7 * (approx + 0.9 * momentum)).astype(jnp.bfloat16)
        for kind, (buf, out) in enumerate(((buf_w, out_w), (buf_e, out_e), (buf_m, out_m))):
            pltpu.make_async_copy(buf.at[mat], out.at[mat], sems.at[kind, mat]).start()
    for mat in range(MATS):
        for kind, (buf, out) in enumerate(((buf_w, out_w), (buf_e, out_e), (buf_m, out_m))):
            pltpu.make_async_copy(buf.at[mat], out.at[mat], sems.at[kind, mat]).wait()


def sibling(x):
    return lax.ppermute(x, "replica", [(i, i ^ 1) for i in range(2 * CHIPS)])


def near(x):
    groups = [
        [2 * (4 * high + low) + core for low in range(4)] for high in range(4) for core in range(2)
    ]
    return lax.all_to_all(x, "replica", 0, 0, axis_index_groups=groups, tiled=True)


def far(x):
    groups = [
        [2 * (4 * high + low) + core for high in range(4)] for low in range(4) for core in range(2)
    ]
    return lax.all_to_all(x, "replica", 0, 0, axis_index_groups=groups, tiled=True)


def along_x(x):
    groups = [[4 * y + i for i in range(4)] for y in range(4)]
    return lax.all_to_all(x, "fsdp", 0, 0, axis_index_groups=groups, tiled=True)


def along_y(x):
    groups = [[4 * i + x for i in range(4)] for x in range(4)]
    return lax.all_to_all(x, "fsdp", 0, 0, axis_index_groups=groups, tiled=True)


def to_four(x):
    return jnp.broadcast_to(x, (4,) + x.shape)


def local(weights, local_weights, carried_error, momentum, initial_factor):
    f32 = jnp.float32
    core = (lax.axis_index("replica") & 1).astype(jnp.int32).reshape(1)
    shape = (MATS, COLS, WIDTH)
    keep, send, drift = pl.pallas_call(
        pack_kernel,
        out_shape=[jax.ShapeDtypeStruct((CHIPS, SHARE, BLOCK), f32)] * 2
        + [jax.ShapeDtypeStruct(shape, f32)],
        in_specs=[SMEM, HBM, HBM, HBM],
        out_specs=[VMEM] * 3,
        scratch_shapes=[
            pltpu.VMEM(shape, jnp.bfloat16),
            pltpu.VMEM(shape, jnp.bfloat16),
            pltpu.VMEM(shape, f32),
            pltpu.SemaphoreType.DMA((3, 3)),
        ],
        compiler_params=PACK_PARAMS,
        name="pack",
    )(core, weights, local_weights[0], carried_error[0])
    shares = (keep + sibling(send)).reshape(4, 4, SHARE, BLOCK)
    shares = far(jnp.sum(near(shares), axis=0))
    inner, factor = pl.pallas_call(
        factor_kernel,
        out_shape=[
            jax.ShapeDtypeStruct((RANK, BLOCK), f32),
            jax.ShapeDtypeStruct((FROWS, BLOCK), f32),
        ],
        in_specs=[SMEM, VMEM, VMEM],
        out_specs=[VMEM, VMEM],
        compiler_params=PARAMS,
        name="factor",
    )(core, jnp.swapaxes(initial_factor, 1, 2), shares)

    inner = jnp.sum(along_x(to_four(inner)), axis=0)
    inner = jnp.sum(along_y(to_four(inner)), axis=0)
    rows = far(to_four(jnp.concatenate([factor, inner])))
    factor = rows[:, :FROWS].reshape(4 * FROWS, BLOCK)
    inner = jnp.sum(rows[:, FROWS:], axis=0)
    own = near(to_four(jnp.concatenate([factor, inner])))
    sib = sibling(own)

    next_weights, next_error, next_momentum, following = pl.pallas_call(
        lambda *refs: final_kernel(lax.axis_size("replica"), *refs),
        out_shape=[
            jax.ShapeDtypeStruct(shape, jnp.bfloat16),
            jax.ShapeDtypeStruct(shape, f32),
            jax.ShapeDtypeStruct(shape, f32),
            jax.ShapeDtypeStruct((MATS, RANK, COLS), f32),
        ],
        in_specs=[SMEM] + [VMEM] * 5,
        out_specs=[HBM, HBM, HBM, VMEM],
        scratch_shapes=[
            pltpu.VMEM((MATS, RANK, WIDTH), f32),
            pltpu.VMEM(shape, jnp.bfloat16),
            pltpu.VMEM(shape, f32),
            pltpu.VMEM(shape, f32),
            pltpu.SemaphoreType.DMA((3, 3)),
        ],
        compiler_params=PARAMS,
        name="final",
    )(core, own, sib, weights, momentum, drift)
    return (next_weights, next_error[None], next_momentum, jnp.swapaxes(following, 1, 2))


def solution(mesh):
    return jax.shard_map(
        local,
        mesh=mesh,
        in_specs=(
            P(None, None, "fsdp"),
            P("replica", None, None, "fsdp"),
            P("replica", None, None, "fsdp"),
            P(None, None, "fsdp"),
            P(),
        ),
        out_specs=(
            P(None, None, "fsdp"),
            P("replica", None, None, "fsdp"),
            P(None, None, "fsdp"),
            P(),
        ),
        check_vma=False,
    )
```

```python
import jax
import jax.numpy as jnp
from jax import lax
from jax.experimental import pallas as pl
from jax.experimental.pallas import tpu as pltpu
from jax.sharding import PartitionSpec as P

CHIPS = 16
BLOCK = 128
SIDE = BLOCK // 2
BLOCKS = 14
WIDTH = BLOCK * BLOCKS
MATS = 3
COLS = 32
RANK = 16
SHARE = MATS * COLS // 2
FROWS = SHARE // 2
MROWS = 8
GROWS = FROWS + MROWS
PAIR = RANK + COLS
HIGHEST = lax.Precision.HIGHEST
VMEM = pl.BlockSpec(memory_space=pltpu.VMEM)
SMEM = pl.BlockSpec(memory_space=pltpu.SMEM)
HBM = pl.BlockSpec(memory_space=pl.ANY)
PARAMS = pltpu.CompilerParams(vmem_limit_bytes=32 * 1024 * 1024)
PACK_PARAMS = pltpu.CompilerParams(vmem_limit_bytes=56 * 1024 * 1024)


def swap_sides(x):
    return pltpu.roll(x, SIDE, 1)


def left_side(rows):
    return lax.broadcasted_iota(jnp.int32, (rows, BLOCK), 1) < SIDE


def pack_kernel(core_ref, w_hbm, lw_hbm, ce_hbm, keep, send, drift, w, lw, ce, sems):
    core = core_ref[0]
    copies = [
        [
            pltpu.make_async_copy(src.at[mat], dst.at[mat], sems.at[kind, mat])
            for kind, (src, dst) in enumerate(((ce_hbm, ce), (w_hbm, w), (lw_hbm, lw)))
        ]
        for mat in range(MATS)
    ]
    for group in copies:
        for copy in group:
            copy.start()
    left = left_side(16)
    for out in (keep, send):
        out[BLOCKS:CHIPS] = jnp.zeros((CHIPS - BLOCKS, SHARE, BLOCK), jnp.float32)
    for mat in range(MATS):
        for copy in copies[mat]:
            copy.wait()
        for block in range(BLOCKS):
            lanes = slice(block * BLOCK, (block + 1) * BLOCK)
            value = (
                w[mat, :, lanes].astype(jnp.float32)
                - lw[mat, :, lanes].astype(jnp.float32)
                + ce[mat, :, lanes]
            )
            drift[mat, :, lanes] = value
    for block in range(BLOCKS):
        lanes = slice(block * BLOCK, (block + 1) * BLOCK)
        keep[block, 0:COLS] = drift[2 * core, :, lanes]
        send[block, 0:COLS] = drift[2 - 2 * core, :, lanes]
        top, bottom = drift[1, 0:16, lanes], drift[1, 16:32, lanes]
        first = jnp.where(left, top, swap_sides(bottom))
        second = jnp.where(left, swap_sides(top), bottom)
        keep[block, COLS:SHARE] = jnp.where(core == 0, first, second)
        send[block, COLS:SHARE] = jnp.where(core == 0, second, first)


def outer(a, b):
    return lax.dot_general(
        a, b, (((1,), (1,)), ((), ())), precision=HIGHEST, preferred_element_type=jnp.float32
    )


def factor_kernel(core_ref, qt, got, inner, factor):
    core = core_ref[0]
    total = jnp.sum(got[...], axis=0)
    left = left_side(16)
    whole = total[0:COLS]
    half = total[COLS:SHARE]
    half = jnp.concatenate(
        [jnp.where(left, half, 0.0), jnp.where(left, swap_sides(half), 0.0)], axis=0
    )
    whole_factor = jnp.dot(
        qt[2 * core], whole, precision=HIGHEST, preferred_element_type=jnp.float32
    )
    half_factor = jnp.dot(qt[1], half, precision=HIGHEST, preferred_element_type=jnp.float32)
    factor[0:RANK] = whole_factor
    factor[RANK:FROWS] = half_factor[0:8] + swap_sides(half_factor[8:16])
    whole, half = outer(whole_factor, whole), outer(half_factor, half)
    inner[...] = jnp.concatenate([whole[0:8], whole[8:16], half[0:8], half[8:16]], axis=1)


def final_kernel(
    islands, core_ref, qt, own, sib, w, mom, drift,
    out_w, out_e, out_m, out_f, fac, buf_w, buf_e, buf_m, sems,
):
    first = core_ref[0] == 0
    left = left_side(8)
    for block in range(BLOCKS):
        lanes = slice(block * BLOCK, (block + 1) * BLOCK)
        mine, other = own[block, 0:FROWS], sib[block, 0:FROWS]
        low, high = jnp.where(first, mine, other), jnp.where(first, other, mine)
        fac[0, :, lanes] = low[0:RANK]
        fac[2, :, lanes] = high[0:RANK]
        low, high = low[RANK:FROWS], high[RANK:FROWS]
        fac[1, 0:8, lanes] = jnp.where(left, low, swap_sides(high))
        fac[1, 8:16, lanes] = jnp.where(left, swap_sides(low), high)

    mine = jnp.sum(own[:, FROWS:GROWS], axis=0)
    other = jnp.sum(sib[:, FROWS:GROWS], axis=0)
    middle = pltpu.roll(mine + other, SIDE, 1)
    table = []
    for mat, rows in enumerate(
        (jnp.where(first, mine, other), middle, jnp.where(first, other, mine))
    ):
        rows = jnp.concatenate([rows[:, 0:COLS], rows[:, COLS : 2 * COLS]], axis=0)
        gram = outer(qt[mat], rows)
        rest = jnp.zeros((RANK, BLOCK - PAIR), jnp.float32)
        table.append(jnp.concatenate([gram, rows, rest], axis=1))
    table = jnp.stack(table)
    shape = (MATS, RANK, BLOCK)
    row = lax.broadcasted_iota(jnp.int32, shape, 1)
    lane = lax.broadcasted_iota(jnp.int32, shape, 2)
    table = jnp.where(lane == row + PAIR, 1.0, table)
    for step in range(RANK):
        scale = lax.rsqrt(table[:, step : step + 1, step : step + 1])
        pivot = table[:, step : step + 1, :] * scale
        column = table[:, :, step : step + 1] * scale
        table = jnp.where(
            row == step, pivot, jnp.where(row > step, table - column * pivot, table)
        )
    for mat in range(MATS):
        small = table[mat, :, RANK:PAIR] * (1.0 / islands)
        out_f[mat] = small
        inverse = table[mat, :, PAIR : PAIR + RANK]
        mixed = lax.dot_general(
            small, inverse, (((0,), (0,)), ((), ())),
            precision=HIGHEST, preferred_element_type=jnp.float32,
        )
        for tile in range(7):
            lanes = slice(tile * 256, (tile + 1) * 256)
            approx = jnp.dot(
                mixed, fac[mat, :, lanes],
                precision=HIGHEST, preferred_element_type=jnp.float32,
            )
            wide = w[mat, :, lanes].astype(jnp.float32)
            momentum = 0.9 * mom[mat, :, lanes] + approx
            buf_e[mat, :, lanes] = drift[mat, :, lanes] - approx
            buf_m[mat, :, lanes] = momentum
            buf_w[mat, :, lanes] = (wide - 0.7 * (approx + 0.9 * momentum)).astype(jnp.bfloat16)
        for kind, (buf, out) in enumerate(((buf_w, out_w), (buf_e, out_e), (buf_m, out_m))):
            pltpu.make_async_copy(buf.at[mat], out.at[mat], sems.at[kind, mat]).start()
    for mat in range(MATS):
        for kind, (buf, out) in enumerate(((buf_w, out_w), (buf_e, out_e), (buf_m, out_m))):
            pltpu.make_async_copy(buf.at[mat], out.at[mat], sems.at[kind, mat]).wait()


def sibling(x):
    return lax.ppermute(x, "replica", [(i, i ^ 1) for i in range(2 * CHIPS)])


def exchange_z(x):
    groups = [[2 * chip + core for chip in range(CHIPS)] for core in range(2)]
    return lax.all_to_all(x, "replica", 0, 0, axis_index_groups=groups, tiled=True)


def local(weights, local_weights, carried_error, momentum, initial_factor):
    f32 = jnp.float32
    core = (lax.axis_index("replica") & 1).astype(jnp.int32).reshape(1)
    shape = (MATS, COLS, WIDTH)
    keep, send, drift = pl.pallas_call(
        pack_kernel,
        out_shape=[pltpu.VMEM((CHIPS, SHARE, BLOCK), f32)] * 2 + [pltpu.VMEM(shape, f32)],
        in_specs=[SMEM, HBM, HBM, HBM],
        out_specs=[VMEM] * 3,
        scratch_shapes=[
            pltpu.VMEM(shape, jnp.bfloat16),
            pltpu.VMEM(shape, jnp.bfloat16),
            pltpu.VMEM(shape, f32),
            pltpu.SemaphoreType.DMA((3, 3)),
        ],
        compiler_params=PACK_PARAMS,
        name="pack",
    )(core, weights, local_weights[0], carried_error[0])
    qt = jnp.swapaxes(initial_factor, 1, 2)
    shares = exchange_z(keep + sibling(send))
    inner, factor = pl.pallas_call(
        factor_kernel,
        out_shape=[
            jax.ShapeDtypeStruct((MROWS, BLOCK), f32),
            jax.ShapeDtypeStruct((FROWS, BLOCK), f32),
        ],
        in_specs=[SMEM, VMEM, VMEM],
        out_specs=[VMEM, VMEM],
        compiler_params=PARAMS,
        name="factor",
    )(core, qt, shares)

    inner = lax.all_to_all(
        jnp.broadcast_to(inner, (16, MROWS, BLOCK)), "fsdp", 0, 0, tiled=True
    )
    inner = jnp.sum(inner, axis=0)
    own = exchange_z(
        jnp.broadcast_to(jnp.concatenate([factor, inner]), (CHIPS, GROWS, BLOCK))
    )
    sib = sibling(own)

    next_weights, next_error, next_momentum, following = pl.pallas_call(
        lambda *refs: final_kernel(lax.axis_size("replica"), *refs),
        out_shape=[
            jax.ShapeDtypeStruct(shape, jnp.bfloat16),
            jax.ShapeDtypeStruct(shape, f32),
            jax.ShapeDtypeStruct(shape, f32),
            jax.ShapeDtypeStruct((MATS, RANK, COLS), f32),
        ],
        in_specs=[SMEM] + [VMEM] * 6,
        out_specs=[HBM, HBM, HBM, VMEM],
        scratch_shapes=[
            pltpu.VMEM((MATS, RANK, WIDTH), f32),
            pltpu.VMEM(shape, jnp.bfloat16),
            pltpu.VMEM(shape, f32),
            pltpu.VMEM(shape, f32),
            pltpu.SemaphoreType.DMA((3, 3)),
        ],
        compiler_params=PARAMS,
        name="final",
    )(core, qt, own, sib, weights, momentum, drift)
    return (next_weights, next_error[None], next_momentum, jnp.swapaxes(following, 1, 2))


def solution(mesh):
    return jax.shard_map(
        local,
        mesh=mesh,
        in_specs=(
            P(None, None, "fsdp"),
            P("replica", None, None, "fsdp"),
            P("replica", None, None, "fsdp"),
            P(None, None, "fsdp"),
            P(),
        ),
        out_specs=(
            P(None, None, "fsdp"),
            P("replica", None, None, "fsdp"),
            P(None, None, "fsdp"),
            P(),
        ),
        check_vma=False,
    )
```

```python
import jax
import jax.numpy as jnp
from jax import lax
from jax.experimental import pallas as pl
from jax.experimental.pallas import tpu as pltpu
from jax.sharding import PartitionSpec as P

CHIPS = 16
BLOCK = 128
SIDE = BLOCK // 2
BLOCKS = 14
WIDTH = BLOCK * BLOCKS
MATS = 3
COLS = 32
RANK = 16
SHARE = MATS * COLS // 2
FROWS = SHARE // 2
MROWS = 8
GROWS = FROWS + MROWS
PAIR = RANK + COLS
HIGHEST = lax.Precision.HIGHEST
VMEM = pl.BlockSpec(memory_space=pltpu.VMEM)
SMEM = pl.BlockSpec(memory_space=pltpu.SMEM)
HBM = pl.BlockSpec(memory_space=pl.ANY)
PARAMS = pltpu.CompilerParams(vmem_limit_bytes=32 * 1024 * 1024)
PACK_PARAMS = pltpu.CompilerParams(vmem_limit_bytes=56 * 1024 * 1024)


def slot_of(block, chip):
    return ((block ^ chip) & 1) * 8 + (block >> 1)


def swap_sides(x):
    return pltpu.roll(x, SIDE, 1)


def left_side(rows):
    return lax.broadcasted_iota(jnp.int32, (rows, BLOCK), 1) < SIDE


def pack_kernel(ids, w_hbm, lw_hbm, ce_hbm, keep, send, drift, w, lw, ce, sems):
    core, chip = ids[0], ids[1]
    copies = [
        [
            pltpu.make_async_copy(src.at[mat], dst.at[mat], sems.at[kind, mat])
            for kind, (src, dst) in enumerate(((ce_hbm, ce), (w_hbm, w), (lw_hbm, lw)))
        ]
        for mat in range(MATS)
    ]
    for group in copies:
        for copy in group:
            copy.start()
    left = left_side(16)
    for out in (keep, send):
        for block in range(BLOCKS, CHIPS):
            out[slot_of(block, chip)] = jnp.zeros((SHARE, BLOCK), jnp.float32)
    for mat in range(MATS):
        for copy in copies[mat]:
            copy.wait()
        for block in range(BLOCKS):
            lanes = slice(block * BLOCK, (block + 1) * BLOCK)
            value = (
                w[mat, :, lanes].astype(jnp.float32)
                - lw[mat, :, lanes].astype(jnp.float32)
                + ce[mat, :, lanes]
            )
            drift[mat, :, lanes] = value
    for block in range(BLOCKS):
        lanes = slice(block * BLOCK, (block + 1) * BLOCK)
        slot = slot_of(block, chip)
        keep[slot, 0:COLS] = drift[2 * core, :, lanes]
        send[slot, 0:COLS] = drift[2 - 2 * core, :, lanes]
        top, bottom = drift[1, 0:16, lanes], drift[1, 16:32, lanes]
        first = jnp.where(left, top, swap_sides(bottom))
        second = jnp.where(left, swap_sides(top), bottom)
        keep[slot, COLS:SHARE] = jnp.where(core == 0, first, second)
        send[slot, COLS:SHARE] = jnp.where(core == 0, second, first)


def outer(a, b):
    return lax.dot_general(
        a, b, (((1,), (1,)), ((), ())), precision=HIGHEST, preferred_element_type=jnp.float32
    )


def factor_kernel(ids, qt, got, inner, factor):
    core = ids[0]
    total = jnp.sum(got[...], axis=0)
    left = left_side(16)
    whole = total[0:COLS]
    half = total[COLS:SHARE]
    half = jnp.concatenate(
        [jnp.where(left, half, 0.0), jnp.where(left, swap_sides(half), 0.0)], axis=0
    )
    whole_factor = jnp.dot(
        qt[2 * core], whole, precision=HIGHEST, preferred_element_type=jnp.float32
    )
    half_factor = jnp.dot(qt[1], half, precision=HIGHEST, preferred_element_type=jnp.float32)
    factor[0:RANK] = whole_factor
    factor[RANK:FROWS] = half_factor[0:8] + swap_sides(half_factor[8:16])
    whole, half = outer(whole_factor, whole), outer(half_factor, half)
    inner[...] = jnp.concatenate([whole[0:8], whole[8:16], half[0:8], half[8:16]], axis=1)


def split(x):
    high = x.astype(jnp.bfloat16)
    rest = x - high.astype(jnp.float32)
    middle = rest.astype(jnp.bfloat16)
    return high, middle, (rest - middle.astype(jnp.float32)).astype(jnp.bfloat16)


def final_kernel(
    islands, ids, qt, own, sib, w, mom, drift,
    out_w, out_e, out_m, out_f, fac, buf_w, buf_e, buf_m, sems,
):
    first = ids[0] == 0

    mine = jnp.sum(own[:, FROWS:GROWS], axis=0)
    other = jnp.sum(sib[:, FROWS:GROWS], axis=0)
    middle = pltpu.roll(mine + other, SIDE, 1)
    table = []
    for mat, rows in enumerate(
        (jnp.where(first, mine, other), middle, jnp.where(first, other, mine))
    ):
        rows = jnp.concatenate([rows[:, 0:COLS], rows[:, COLS : 2 * COLS]], axis=0)
        gram = outer(qt[mat], rows)
        rest = jnp.zeros((RANK, BLOCK - PAIR), jnp.float32)
        table.append(jnp.concatenate([gram, rows, rest], axis=1))
    table = jnp.stack(table)
    row = lax.broadcasted_iota(jnp.int32, table.shape, 1)
    small = table
    for step in range(RANK):
        scale = lax.rsqrt(table[:, step : step + 1, step : step + 1])
        pivot = table[:, step : step + 1, :] * scale
        column = table[:, :, step : step + 1] * scale
        here = row == step
        small = jnp.where(here, pivot, small)
        table = jnp.where(here, pivot * scale, table - column * pivot)

    left = left_side(8)
    for block in range(BLOCKS):
        lanes = slice(block * BLOCK, (block + 1) * BLOCK)
        mine, other = own[block, 0:FROWS], sib[block, 0:FROWS]
        low, high = jnp.where(first, mine, other), jnp.where(first, other, mine)
        low_half, high_half = low[RANK:FROWS], high[RANK:FROWS]
        half = jnp.concatenate(
            [
                jnp.where(left, low_half, swap_sides(high_half)),
                jnp.where(left, swap_sides(low_half), high_half),
            ],
            axis=0,
        )
        for mat, value in enumerate((low[0:RANK], half, high[0:RANK])):
            top, mid, last = split(value)
            for place, part in enumerate((top, mid, last, top, mid, top)):
                fac[mat, place * RANK : place * RANK + RANK, lanes] = part

    for mat in range(MATS):
        out_f[mat] = small[mat, :, RANK:PAIR] * (1.0 / islands)
        top, mid, last = split(table[mat, :, RANK:PAIR] * (1.0 / islands))
        parts = [x.astype(jnp.float32) for x in (top, top, top, mid, mid, last)]
        mixed = jnp.transpose(jnp.concatenate(parts, axis=0)).astype(jnp.bfloat16)
        for tile in range(7):
            lanes = slice(tile * 256, (tile + 1) * 256)
            approx = jnp.dot(mixed, fac[mat, :, lanes], preferred_element_type=jnp.float32)
            wide = w[mat, :, lanes].astype(jnp.float32)
            momentum = 0.9 * mom[mat, :, lanes] + approx
            buf_e[mat, :, lanes] = drift[mat, :, lanes] - approx
            buf_m[mat, :, lanes] = momentum
            buf_w[mat, :, lanes] = (wide - 0.7 * (approx + 0.9 * momentum)).astype(jnp.bfloat16)
        for kind, (buf, out) in enumerate(((buf_w, out_w), (buf_e, out_e), (buf_m, out_m))):
            pltpu.make_async_copy(buf.at[mat], out.at[mat], sems.at[kind, mat]).start()
    for mat in range(MATS):
        for kind, (buf, out) in enumerate(((buf_w, out_w), (buf_e, out_e), (buf_m, out_m))):
            pltpu.make_async_copy(buf.at[mat], out.at[mat], sems.at[kind, mat]).wait()


def sibling(x):
    return lax.ppermute(x, "replica", [(i, i ^ 1) for i in range(2 * CHIPS)])


def neighbour(x, step):
    pairs = [
        (2 * chip + core, 2 * ((chip + (step if chip % 2 == 0 else -step)) % CHIPS) + core)
        for chip in range(CHIPS)
        for core in range(2)
    ]
    return lax.ppermute(x, "replica", pairs)


def exchange_parity(x):
    groups = [
        [2 * chip + core for chip in range(parity, CHIPS, 2)]
        for parity in range(2)
        for core in range(2)
    ]
    return lax.all_to_all(x, "replica", 0, 0, axis_index_groups=groups, tiled=True)


def exchange_z(x):
    groups = [[2 * chip + core for chip in range(CHIPS)] for core in range(2)]
    return lax.all_to_all(x, "replica", 0, 0, axis_index_groups=groups, tiled=True)


def local(weights, local_weights, carried_error, momentum, initial_factor):
    f32 = jnp.float32
    index = lax.axis_index("replica")
    ids = jnp.stack([index & 1, index >> 1]).astype(jnp.int32)
    shape = (MATS, COLS, WIDTH)
    keep, send, drift = pl.pallas_call(
        pack_kernel,
        out_shape=[pltpu.VMEM((CHIPS, SHARE, BLOCK), f32)] * 2 + [pltpu.VMEM(shape, f32)],
        in_specs=[SMEM, HBM, HBM, HBM],
        out_specs=[VMEM] * 3,
        scratch_shapes=[
            pltpu.VMEM(shape, jnp.bfloat16),
            pltpu.VMEM(shape, jnp.bfloat16),
            pltpu.VMEM(shape, f32),
            pltpu.SemaphoreType.DMA((3, 3)),
        ],
        compiler_params=PACK_PARAMS,
        name="pack",
    )(ids, weights, local_weights[0], carried_error[0])
    qt = jnp.swapaxes(initial_factor, 1, 2)
    got = sibling(send)
    halves = [
        neighbour(keep[first : first + 4] + got[first : first + 4], step)
        for first, step in ((8, 1), (12, -1))
    ]
    shares = exchange_parity(keep[0:8] + got[0:8] + jnp.concatenate(halves))
    inner, factor = pl.pallas_call(
        factor_kernel,
        out_shape=[
            jax.ShapeDtypeStruct((MROWS, BLOCK), f32),
            jax.ShapeDtypeStruct((FROWS, BLOCK), f32),
        ],
        in_specs=[SMEM, VMEM, VMEM],
        out_specs=[VMEM, VMEM],
        compiler_params=PARAMS,
        name="factor",
    )(ids, qt, shares)

    inner = lax.all_to_all(
        jnp.broadcast_to(inner, (16, MROWS, BLOCK)), "fsdp", 0, 0, tiled=True
    )
    inner = jnp.sum(inner, axis=0)
    own = exchange_z(
        jnp.broadcast_to(jnp.concatenate([factor, inner]), (CHIPS, GROWS, BLOCK))
    )
    sib = sibling(own)

    next_weights, next_error, next_momentum, following = pl.pallas_call(
        lambda *refs: final_kernel(lax.axis_size("replica"), *refs),
        out_shape=[
            jax.ShapeDtypeStruct(shape, jnp.bfloat16),
            jax.ShapeDtypeStruct(shape, f32),
            jax.ShapeDtypeStruct(shape, f32),
            jax.ShapeDtypeStruct((MATS, RANK, COLS), f32),
        ],
        in_specs=[SMEM] + [VMEM] * 6,
        out_specs=[HBM, HBM, HBM, VMEM],
        scratch_shapes=[
            pltpu.VMEM((MATS, 6 * RANK, WIDTH), jnp.bfloat16),
            pltpu.VMEM(shape, jnp.bfloat16),
            pltpu.VMEM(shape, f32),
            pltpu.VMEM(shape, f32),
            pltpu.SemaphoreType.DMA((3, 3)),
        ],
        compiler_params=PARAMS,
        name="final",
    )(ids, qt, own, sib, weights, momentum, drift)
    return (next_weights, next_error[None], next_momentum, jnp.swapaxes(following, 1, 2))


def solution(mesh):
    return jax.shard_map(
        local,
        mesh=mesh,
        in_specs=(
            P(None, None, "fsdp"),
            P("replica", None, None, "fsdp"),
            P("replica", None, None, "fsdp"),
            P(None, None, "fsdp"),
            P(),
        ),
        out_specs=(
            P(None, None, "fsdp"),
            P("replica", None, None, "fsdp"),
            P(None, None, "fsdp"),
            P(),
        ),
        check_vma=False,
    )
```

```python
import jax
import jax.numpy as jnp
from jax import lax
from jax.experimental import pallas as pl
from jax.experimental.pallas import tpu as pltpu
from jax.sharding import PartitionSpec as P

CHIPS = 16
BLOCK = 128
SIDE = BLOCK // 2
BLOCKS = 14
WIDTH = BLOCK * BLOCKS
MATS = 3
COLS = 32
RANK = 16
SHARE = MATS * COLS // 2
FROWS = SHARE // 2
MROWS = 8
GROWS = FROWS + MROWS
PAIR = RANK + COLS
HIGHEST = lax.Precision.HIGHEST
VMEM = pl.BlockSpec(memory_space=pltpu.VMEM)
SMEM = pl.BlockSpec(memory_space=pltpu.SMEM)
HBM = pl.BlockSpec(memory_space=pl.ANY)
PARAMS = pltpu.CompilerParams(vmem_limit_bytes=32 * 1024 * 1024)
PACK_PARAMS = pltpu.CompilerParams(vmem_limit_bytes=56 * 1024 * 1024)


def slot_of(block):
    return (block & 1) * 8 + (block >> 1)


def swap_sides(x):
    return pltpu.roll(x, SIDE, 1)


def left_side(rows):
    return lax.broadcasted_iota(jnp.int32, (rows, BLOCK), 1) < SIDE


def pack_kernel(ids, w_hbm, lw_hbm, ce_hbm, keep, send, drift, w, lw, ce, sems):
    core = ids[0]
    copies = [
        [
            pltpu.make_async_copy(src.at[mat], dst.at[mat], sems.at[kind, mat])
            for kind, (src, dst) in enumerate(((ce_hbm, ce), (w_hbm, w), (lw_hbm, lw)))
        ]
        for mat in range(MATS)
    ]
    for group in copies:
        for copy in group:
            copy.start()
    left = left_side(16)
    for out in (keep, send):
        for block in range(BLOCKS, CHIPS):
            out[slot_of(block)] = jnp.zeros((SHARE, BLOCK), jnp.float32)
    for mat in range(MATS):
        for copy in copies[mat]:
            copy.wait()
        for block in range(BLOCKS):
            lanes = slice(block * BLOCK, (block + 1) * BLOCK)
            value = (
                w[mat, :, lanes].astype(jnp.float32)
                - lw[mat, :, lanes].astype(jnp.float32)
                + ce[mat, :, lanes]
            )
            drift[mat, :, lanes] = value
    for block in range(BLOCKS):
        lanes = slice(block * BLOCK, (block + 1) * BLOCK)
        slot = slot_of(block)
        keep[slot, 0:COLS] = drift[2 * core, :, lanes]
        send[slot, 0:COLS] = drift[2 - 2 * core, :, lanes]
        top, bottom = drift[1, 0:16, lanes], drift[1, 16:32, lanes]
        first = jnp.where(left, top, swap_sides(bottom))
        second = jnp.where(left, swap_sides(top), bottom)
        keep[slot, COLS:SHARE] = jnp.where(core == 0, first, second)
        send[slot, COLS:SHARE] = jnp.where(core == 0, second, first)


def outer(a, b):
    return lax.dot_general(
        a, b, (((1,), (1,)), ((), ())), precision=HIGHEST, preferred_element_type=jnp.float32
    )


def factor_kernel(ids, qt, got, inner, factor):
    core = ids[0]
    total = jnp.sum(got[...], axis=0)
    left = left_side(16)
    whole = total[0:COLS]
    half = total[COLS:SHARE]
    half = jnp.concatenate(
        [jnp.where(left, half, 0.0), jnp.where(left, swap_sides(half), 0.0)], axis=0
    )
    whole_factor = jnp.dot(
        qt[2 * core], whole, precision=HIGHEST, preferred_element_type=jnp.float32
    )
    half_factor = jnp.dot(qt[1], half, precision=HIGHEST, preferred_element_type=jnp.float32)
    factor[0:RANK] = whole_factor
    factor[RANK:FROWS] = half_factor[0:8] + swap_sides(half_factor[8:16])
    whole, half = outer(whole_factor, whole), outer(half_factor, half)
    inner[...] = jnp.concatenate([whole[0:8], whole[8:16], half[0:8], half[8:16]], axis=1)


def split(x):
    high = x.astype(jnp.bfloat16)
    rest = x - high.astype(jnp.float32)
    middle = rest.astype(jnp.bfloat16)
    return high, middle, (rest - middle.astype(jnp.float32)).astype(jnp.bfloat16)


def final_kernel(
    islands, ids, qt, own, sib, w, mom, drift,
    out_w, out_e, out_m, out_f, fac, buf_w, buf_e, buf_m, sems,
):
    first = ids[0] == 0

    rows = slice(8 * FROWS, 8 * FROWS + MROWS)
    mine = own[0, rows] + own[1, rows]
    other = sib[0, rows] + sib[1, rows]
    middle = pltpu.roll(mine + other, SIDE, 1)
    table = []
    for mat, rows in enumerate(
        (jnp.where(first, mine, other), middle, jnp.where(first, other, mine))
    ):
        rows = jnp.concatenate([rows[:, 0:COLS], rows[:, COLS : 2 * COLS]], axis=0)
        gram = outer(qt[mat], rows)
        rest = jnp.zeros((RANK, BLOCK - PAIR), jnp.float32)
        table.append(jnp.concatenate([gram, rows, rest], axis=1))
    table = jnp.stack(table)
    row = lax.broadcasted_iota(jnp.int32, table.shape, 1)
    small = table
    for step in range(RANK):
        scale = lax.rsqrt(table[:, step : step + 1, step : step + 1])
        pivot = table[:, step : step + 1, :] * scale
        column = table[:, :, step : step + 1] * scale
        here = row == step
        small = jnp.where(here, pivot, small)
        table = jnp.where(here, pivot * scale, table - column * pivot)

    left = left_side(8)
    for block in range(BLOCKS):
        lanes = slice(block * BLOCK, (block + 1) * BLOCK)
        rows = slice((block >> 1) * FROWS, (block >> 1) * FROWS + FROWS)
        mine, other = own[block & 1, rows], sib[block & 1, rows]
        low, high = jnp.where(first, mine, other), jnp.where(first, other, mine)
        low_half, high_half = low[RANK:FROWS], high[RANK:FROWS]
        half = jnp.concatenate(
            [
                jnp.where(left, low_half, swap_sides(high_half)),
                jnp.where(left, swap_sides(low_half), high_half),
            ],
            axis=0,
        )
        for mat, value in enumerate((low[0:RANK], half, high[0:RANK])):
            top, mid, last = split(value)
            for place, part in enumerate((top, mid, last, top, mid, top)):
                fac[mat, place * RANK : place * RANK + RANK, lanes] = part

    for mat in range(MATS):
        out_f[mat] = small[mat, :, RANK:PAIR] * (1.0 / islands)
        top, mid, last = split(table[mat, :, RANK:PAIR] * (1.0 / islands))
        parts = [x.astype(jnp.float32) for x in (top, top, top, mid, mid, last)]
        mixed = jnp.transpose(jnp.concatenate(parts, axis=0)).astype(jnp.bfloat16)
        for tile in range(7):
            lanes = slice(tile * 256, (tile + 1) * 256)
            approx = jnp.dot(mixed, fac[mat, :, lanes], preferred_element_type=jnp.float32)
            wide = w[mat, :, lanes].astype(jnp.float32)
            momentum = 0.9 * mom[mat, :, lanes] + approx
            buf_e[mat, :, lanes] = drift[mat, :, lanes] - approx
            buf_m[mat, :, lanes] = momentum
            buf_w[mat, :, lanes] = (wide - 0.7 * (approx + 0.9 * momentum)).astype(jnp.bfloat16)
        for kind, (buf, out) in enumerate(((buf_w, out_w), (buf_e, out_e), (buf_m, out_m))):
            pltpu.make_async_copy(buf.at[mat], out.at[mat], sems.at[kind, mat]).start()
    for mat in range(MATS):
        for kind, (buf, out) in enumerate(((buf_w, out_w), (buf_e, out_e), (buf_m, out_m))):
            pltpu.make_async_copy(buf.at[mat], out.at[mat], sems.at[kind, mat]).wait()


def sibling(x):
    return lax.ppermute(x, "replica", [(i, i ^ 1) for i in range(2 * CHIPS)])


def exchange_pair(x):
    groups = [
        [2 * chip + core, 2 * chip + 2 + core] for chip in range(0, CHIPS, 2) for core in range(2)
    ]
    return lax.all_to_all(x, "replica", 0, 0, axis_index_groups=groups, tiled=True)


def exchange_parity(x):
    groups = [
        [2 * chip + core for chip in range(parity, CHIPS, 2)]
        for parity in range(2)
        for core in range(2)
    ]
    return lax.all_to_all(x, "replica", 0, 0, axis_index_groups=groups, tiled=True)


def local(weights, local_weights, carried_error, momentum, initial_factor):
    f32 = jnp.float32
    ids = (lax.axis_index("replica") & 1).astype(jnp.int32).reshape(1)
    shape = (MATS, COLS, WIDTH)
    keep, send, drift = pl.pallas_call(
        pack_kernel,
        out_shape=[pltpu.VMEM((CHIPS, SHARE, BLOCK), f32)] * 2 + [pltpu.VMEM(shape, f32)],
        in_specs=[SMEM, HBM, HBM, HBM],
        out_specs=[VMEM] * 3,
        scratch_shapes=[
            pltpu.VMEM(shape, jnp.bfloat16),
            pltpu.VMEM(shape, jnp.bfloat16),
            pltpu.VMEM(shape, f32),
            pltpu.SemaphoreType.DMA((3, 3)),
        ],
        compiler_params=PACK_PARAMS,
        name="pack",
    )(ids, weights, local_weights[0], carried_error[0])
    qt = jnp.swapaxes(initial_factor, 1, 2)
    shares = exchange_pair((keep + sibling(send)).reshape(2, 8, SHARE, BLOCK))
    shares = exchange_parity(jnp.sum(shares, axis=0))
    inner, factor = pl.pallas_call(
        factor_kernel,
        out_shape=[
            jax.ShapeDtypeStruct((MROWS, BLOCK), f32),
            jax.ShapeDtypeStruct((FROWS, BLOCK), f32),
        ],
        in_specs=[SMEM, VMEM, VMEM],
        out_specs=[VMEM, VMEM],
        compiler_params=PARAMS,
        name="factor",
    )(ids, qt, shares)

    inner = lax.all_to_all(
        jnp.broadcast_to(inner, (16, MROWS, BLOCK)), "fsdp", 0, 0, tiled=True
    )
    inner = jnp.sum(inner, axis=0)
    rows = exchange_parity(
        jnp.broadcast_to(jnp.concatenate([factor, inner]), (8, GROWS, BLOCK))
    )
    factor = rows[:, :FROWS].reshape(8 * FROWS, BLOCK)
    inner = jnp.sum(rows[:, FROWS:], axis=0)
    own = exchange_pair(
        jnp.broadcast_to(jnp.concatenate([factor, inner]), (2, 8 * FROWS + MROWS, BLOCK))
    )
    sib = sibling(own)

    next_weights, next_error, next_momentum, following = pl.pallas_call(
        lambda *refs: final_kernel(lax.axis_size("replica"), *refs),
        out_shape=[
            jax.ShapeDtypeStruct(shape, jnp.bfloat16),
            jax.ShapeDtypeStruct(shape, f32),
            jax.ShapeDtypeStruct(shape, f32),
            jax.ShapeDtypeStruct((MATS, RANK, COLS), f32),
        ],
        in_specs=[SMEM] + [VMEM] * 6,
        out_specs=[HBM, HBM, HBM, VMEM],
        scratch_shapes=[
            pltpu.VMEM((MATS, 6 * RANK, WIDTH), jnp.bfloat16),
            pltpu.VMEM(shape, jnp.bfloat16),
            pltpu.VMEM(shape, f32),
            pltpu.VMEM(shape, f32),
            pltpu.SemaphoreType.DMA((3, 3)),
        ],
        compiler_params=PARAMS,
        name="final",
    )(ids, qt, own, sib, weights, momentum, drift)
    return (next_weights, next_error[None], next_momentum, jnp.swapaxes(following, 1, 2))


def solution(mesh):
    return jax.shard_map(
        local,
        mesh=mesh,
        in_specs=(
            P(None, None, "fsdp"),
            P("replica", None, None, "fsdp"),
            P("replica", None, None, "fsdp"),
            P(None, None, "fsdp"),
            P(),
        ),
        out_specs=(
            P(None, None, "fsdp"),
            P("replica", None, None, "fsdp"),
            P(None, None, "fsdp"),
            P(),
        ),
        check_vma=False,
    )
```

```python
import jax
import jax.numpy as jnp
from jax import lax
from jax.experimental import pallas as pl
from jax.experimental.pallas import tpu as pltpu
from jax.sharding import PartitionSpec as P

CHIPS = 16
BLOCK = 128
SIDE = BLOCK // 2
BLOCKS = 14
WIDTH = BLOCK * BLOCKS
MATS = 3
COLS = 32
RANK = 16
SHARE = MATS * COLS // 2
FROWS = SHARE // 2
MROWS = 8
GROWS = FROWS + MROWS
PAIR = RANK + COLS
HIGHEST = lax.Precision.HIGHEST
VMEM = pl.BlockSpec(memory_space=pltpu.VMEM)
SMEM = pl.BlockSpec(memory_space=pltpu.SMEM)
HBM = pl.BlockSpec(memory_space=pl.ANY)
PARAMS = pltpu.CompilerParams(vmem_limit_bytes=32 * 1024 * 1024)
PACK_PARAMS = pltpu.CompilerParams(vmem_limit_bytes=56 * 1024 * 1024)


def swap_sides(x):
    return pltpu.roll(x, SIDE, 1)


def left_side(rows):
    return lax.broadcasted_iota(jnp.int32, (rows, BLOCK), 1) < SIDE


def pack_kernel(ids, w_hbm, lw_hbm, ce_hbm, keep, send, drift, w, lw, ce, sems):
    core = ids[0]
    copies = [
        [
            pltpu.make_async_copy(src.at[mat], dst.at[mat], sems.at[kind, mat])
            for kind, (src, dst) in enumerate(((ce_hbm, ce), (w_hbm, w), (lw_hbm, lw)))
        ]
        for mat in range(MATS)
    ]
    for group in copies:
        for copy in group:
            copy.start()
    left = left_side(16)
    for out in (keep, send):
        out[BLOCKS:CHIPS] = jnp.zeros((CHIPS - BLOCKS, SHARE, BLOCK), jnp.float32)
    for mat in range(MATS):
        for copy in copies[mat]:
            copy.wait()
        for block in range(BLOCKS):
            lanes = slice(block * BLOCK, (block + 1) * BLOCK)
            value = (
                w[mat, :, lanes].astype(jnp.float32)
                - lw[mat, :, lanes].astype(jnp.float32)
                + ce[mat, :, lanes]
            )
            drift[mat, :, lanes] = value
    for block in range(BLOCKS):
        lanes = slice(block * BLOCK, (block + 1) * BLOCK)
        keep[block, 0:COLS] = drift[2 * core, :, lanes]
        send[block, 0:COLS] = drift[2 - 2 * core, :, lanes]
        top, bottom = drift[1, 0:16, lanes], drift[1, 16:32, lanes]
        first = jnp.where(left, top, swap_sides(bottom))
        second = jnp.where(left, swap_sides(top), bottom)
        keep[block, COLS:SHARE] = jnp.where(core == 0, first, second)
        send[block, COLS:SHARE] = jnp.where(core == 0, second, first)


def outer(a, b):
    return lax.dot_general(
        a, b, (((1,), (1,)), ((), ())), precision=HIGHEST, preferred_element_type=jnp.float32
    )


def factor_kernel(ids, qt, got, inner, factor):
    core = ids[0]
    total = jnp.sum(got[...], axis=0)
    left = left_side(16)
    whole = total[0:COLS]
    half = total[COLS:SHARE]
    half = jnp.concatenate(
        [jnp.where(left, half, 0.0), jnp.where(left, swap_sides(half), 0.0)], axis=0
    )
    whole_factor = jnp.dot(
        qt[2 * core], whole, precision=HIGHEST, preferred_element_type=jnp.float32
    )
    half_factor = jnp.dot(qt[1], half, precision=HIGHEST, preferred_element_type=jnp.float32)
    factor[0:RANK] = whole_factor
    factor[RANK:FROWS] = half_factor[0:8] + swap_sides(half_factor[8:16])
    whole, half = outer(whole_factor, whole), outer(half_factor, half)
    inner[...] = jnp.concatenate([whole[0:8], whole[8:16], half[0:8], half[8:16]], axis=1)


def split(x):
    high = x.astype(jnp.bfloat16)
    rest = x - high.astype(jnp.float32)
    middle = rest.astype(jnp.bfloat16)
    return high, middle, (rest - middle.astype(jnp.float32)).astype(jnp.bfloat16)


def final_kernel(
    islands, ids, qt, own, sib, w, mom, drift,
    out_w, out_e, out_m, out_f, fac, buf_w, buf_e, buf_m, sems,
):
    first = ids[0] == 0

    mine = jnp.sum(own[:, FROWS:GROWS], axis=0)
    other = jnp.sum(sib[:, FROWS:GROWS], axis=0)
    middle = pltpu.roll(mine + other, SIDE, 1)
    table = []
    for mat, rows in enumerate(
        (jnp.where(first, mine, other), middle, jnp.where(first, other, mine))
    ):
        rows = jnp.concatenate([rows[:, 0:COLS], rows[:, COLS : 2 * COLS]], axis=0)
        gram = outer(qt[mat], rows)
        rest = jnp.zeros((RANK, BLOCK - PAIR), jnp.float32)
        table.append(jnp.concatenate([gram, rows, rest], axis=1))
    table = jnp.stack(table)
    row = lax.broadcasted_iota(jnp.int32, table.shape, 1)
    small = table
    for step in range(RANK):
        spread = jnp.broadcast_to(table[:, :, step : step + 1], table.shape)
        pivot = spread[:, step : step + 1, :]
        line = table[:, step : step + 1, :]
        scaled = line * (1.0 / pivot)
        here = row == step
        small = jnp.where(here, line * lax.rsqrt(pivot), small)
        table = jnp.where(here, scaled, table - spread * scaled)

    left = left_side(8)
    for block in range(BLOCKS):
        lanes = slice(block * BLOCK, (block + 1) * BLOCK)
        mine, other = own[block, 0:FROWS], sib[block, 0:FROWS]
        low, high = jnp.where(first, mine, other), jnp.where(first, other, mine)
        low_half, high_half = low[RANK:FROWS], high[RANK:FROWS]
        half = jnp.concatenate(
            [
                jnp.where(left, low_half, swap_sides(high_half)),
                jnp.where(left, swap_sides(low_half), high_half),
            ],
            axis=0,
        )
        for mat, value in enumerate((low[0:RANK], half, high[0:RANK])):
            top, mid, last = split(value)
            for place, part in enumerate((top, mid, last, top, mid, top)):
                fac[mat, place * RANK : place * RANK + RANK, lanes] = part

    for mat in range(MATS):
        out_f[mat] = small[mat, :, RANK:PAIR] * (1.0 / islands)
        top, mid, last = split(table[mat, :, RANK:PAIR] * (1.0 / islands))
        parts = [x.astype(jnp.float32) for x in (top, top, top, mid, mid, last)]
        mixed = jnp.transpose(jnp.concatenate(parts, axis=0)).astype(jnp.bfloat16)
        for tile in range(7):
            lanes = slice(tile * 256, (tile + 1) * 256)
            approx = jnp.dot(mixed, fac[mat, :, lanes], preferred_element_type=jnp.float32)
            wide = w[mat, :, lanes].astype(jnp.float32)
            momentum = 0.9 * mom[mat, :, lanes] + approx
            buf_e[mat, :, lanes] = drift[mat, :, lanes] - approx
            buf_m[mat, :, lanes] = momentum
            buf_w[mat, :, lanes] = (wide - 0.7 * (approx + 0.9 * momentum)).astype(jnp.bfloat16)
        for kind, (buf, out) in enumerate(((buf_w, out_w), (buf_e, out_e), (buf_m, out_m))):
            pltpu.make_async_copy(buf.at[mat], out.at[mat], sems.at[kind, mat]).start()
    for mat in range(MATS):
        for kind, (buf, out) in enumerate(((buf_w, out_w), (buf_e, out_e), (buf_m, out_m))):
            pltpu.make_async_copy(buf.at[mat], out.at[mat], sems.at[kind, mat]).wait()


def sibling(x):
    return lax.ppermute(x, "replica", [(i, i ^ 1) for i in range(2 * CHIPS)])


def exchange_z(x):
    groups = [[2 * chip + core for chip in range(CHIPS)] for core in range(2)]
    return lax.all_to_all(x, "replica", 0, 0, axis_index_groups=groups, tiled=True)


def local(weights, local_weights, carried_error, momentum, initial_factor):
    f32 = jnp.float32
    ids = (lax.axis_index("replica") & 1).astype(jnp.int32).reshape(1)
    shape = (MATS, COLS, WIDTH)
    keep, send, drift = pl.pallas_call(
        pack_kernel,
        out_shape=[pltpu.VMEM((CHIPS, SHARE, BLOCK), f32)] * 2 + [pltpu.VMEM(shape, f32)],
        in_specs=[SMEM, HBM, HBM, HBM],
        out_specs=[VMEM] * 3,
        scratch_shapes=[
            pltpu.VMEM(shape, jnp.bfloat16),
            pltpu.VMEM(shape, jnp.bfloat16),
            pltpu.VMEM(shape, f32),
            pltpu.SemaphoreType.DMA((3, 3)),
        ],
        compiler_params=PACK_PARAMS,
        name="pack",
    )(ids, weights, local_weights[0], carried_error[0])
    qt = jnp.swapaxes(initial_factor, 1, 2)
    shares = exchange_z(keep + sibling(send))
    inner, factor = pl.pallas_call(
        factor_kernel,
        out_shape=[
            jax.ShapeDtypeStruct((MROWS, BLOCK), f32),
            jax.ShapeDtypeStruct((FROWS, BLOCK), f32),
        ],
        in_specs=[SMEM, VMEM, VMEM],
        out_specs=[VMEM, VMEM],
        compiler_params=PARAMS,
        name="factor",
    )(ids, qt, shares)

    inner = lax.all_to_all(
        jnp.broadcast_to(inner, (16, MROWS, BLOCK)), "fsdp", 0, 0, tiled=True
    )
    inner = jnp.sum(inner, axis=0)
    own = exchange_z(
        jnp.broadcast_to(jnp.concatenate([factor, inner]), (CHIPS, GROWS, BLOCK))
    )
    sib = sibling(own)

    next_weights, next_error, next_momentum, following = pl.pallas_call(
        lambda *refs: final_kernel(lax.axis_size("replica"), *refs),
        out_shape=[
            jax.ShapeDtypeStruct(shape, jnp.bfloat16),
            jax.ShapeDtypeStruct(shape, f32),
            jax.ShapeDtypeStruct(shape, f32),
            jax.ShapeDtypeStruct((MATS, RANK, COLS), f32),
        ],
        in_specs=[SMEM] + [VMEM] * 6,
        out_specs=[HBM, HBM, HBM, VMEM],
        scratch_shapes=[
            pltpu.VMEM((MATS, 6 * RANK, WIDTH), jnp.bfloat16),
            pltpu.VMEM(shape, jnp.bfloat16),
            pltpu.VMEM(shape, f32),
            pltpu.VMEM(shape, f32),
            pltpu.SemaphoreType.DMA((3, 3)),
        ],
        compiler_params=PARAMS,
        name="final",
    )(ids, qt, own, sib, weights, momentum, drift)
    return (next_weights, next_error[None], next_momentum, jnp.swapaxes(following, 1, 2))


def solution(mesh):
    return jax.shard_map(
        local,
        mesh=mesh,
        in_specs=(
            P(None, None, "fsdp"),
            P("replica", None, None, "fsdp"),
            P("replica", None, None, "fsdp"),
            P(None, None, "fsdp"),
            P(),
        ),
        out_specs=(
            P(None, None, "fsdp"),
            P("replica", None, None, "fsdp"),
            P(None, None, "fsdp"),
            P(),
        ),
        check_vma=False,
    )
```

```python
import jax
import jax.numpy as jnp
from jax import lax
from jax.experimental import pallas as pl
from jax.experimental.pallas import tpu as pltpu
from jax.sharding import PartitionSpec as P

CHIPS = 16
BLOCK = 128
SIDE = BLOCK // 2
BLOCKS = 14
WIDTH = BLOCK * BLOCKS
MATS = 3
COLS = 32
RANK = 16
SHARE = MATS * COLS // 2
FROWS = SHARE // 2
MROWS = 8
GROWS = FROWS + MROWS
PAIR = RANK + COLS
HIGHEST = lax.Precision.HIGHEST
VMEM = pl.BlockSpec(memory_space=pltpu.VMEM)
SMEM = pl.BlockSpec(memory_space=pltpu.SMEM)
HBM = pl.BlockSpec(memory_space=pl.ANY)
PARAMS = pltpu.CompilerParams(vmem_limit_bytes=32 * 1024 * 1024)
PACK_PARAMS = pltpu.CompilerParams(vmem_limit_bytes=56 * 1024 * 1024)


def swap_sides(x):
    return pltpu.roll(x, SIDE, 1)


def left_side(rows):
    return lax.broadcasted_iota(jnp.int32, (rows, BLOCK), 1) < SIDE


def pack_kernel(ids, w_hbm, lw_hbm, ce_hbm, keep, send, drift, w, lw, ce, sems):
    core = ids[0]
    copies = [
        [
            pltpu.make_async_copy(src.at[mat], dst.at[mat], sems.at[kind, mat])
            for kind, (src, dst) in enumerate(((ce_hbm, ce), (w_hbm, w), (lw_hbm, lw)))
        ]
        for mat in range(MATS)
    ]
    for group in copies:
        for copy in group:
            copy.start()
    left = left_side(16)
    for out in (keep, send):
        out[BLOCKS:CHIPS] = jnp.zeros((CHIPS - BLOCKS, SHARE, BLOCK), jnp.float32)
    for mat in range(MATS):
        for copy in copies[mat]:
            copy.wait()
        for block in range(BLOCKS):
            lanes = slice(block * BLOCK, (block + 1) * BLOCK)
            value = (
                w[mat, :, lanes].astype(jnp.float32)
                - lw[mat, :, lanes].astype(jnp.float32)
                + ce[mat, :, lanes]
            )
            drift[mat, :, lanes] = value
    for block in range(BLOCKS):
        lanes = slice(block * BLOCK, (block + 1) * BLOCK)
        keep[block, 0:COLS] = drift[2 * core, :, lanes]
        send[block, 0:COLS] = drift[2 - 2 * core, :, lanes]
        top, bottom = drift[1, 0:16, lanes], drift[1, 16:32, lanes]
        first = jnp.where(left, top, swap_sides(bottom))
        second = jnp.where(left, swap_sides(top), bottom)
        keep[block, COLS:SHARE] = jnp.where(core == 0, first, second)
        send[block, COLS:SHARE] = jnp.where(core == 0, second, first)


def outer(a, b):
    return lax.dot_general(
        a, b, (((1,), (1,)), ((), ())), precision=HIGHEST, preferred_element_type=jnp.float32
    )


def factor_kernel(ids, qt, got, inner, factor):
    core = ids[0]
    total = jnp.sum(got[...], axis=0)
    left = left_side(16)
    whole = total[0:COLS]
    half = total[COLS:SHARE]
    half = jnp.concatenate(
        [jnp.where(left, half, 0.0), jnp.where(left, swap_sides(half), 0.0)], axis=0
    )
    whole_factor = jnp.dot(
        qt[2 * core], whole, precision=HIGHEST, preferred_element_type=jnp.float32
    )
    half_factor = jnp.dot(qt[1], half, precision=HIGHEST, preferred_element_type=jnp.float32)
    factor[0:RANK] = whole_factor
    factor[RANK:FROWS] = half_factor[0:8] + swap_sides(half_factor[8:16])
    whole, half = outer(whole_factor, whole), outer(half_factor, half)
    inner[...] = jnp.concatenate([whole[0:8], whole[8:16], half[0:8], half[8:16]], axis=1)


def split(x):
    high = x.astype(jnp.bfloat16)
    rest = x - high.astype(jnp.float32)
    middle = rest.astype(jnp.bfloat16)
    return high, middle, (rest - middle.astype(jnp.float32)).astype(jnp.bfloat16)


def final_kernel(
    islands, ids, qt, own, sib, w, mom, drift,
    out_w, out_e, out_m, out_f, fac, buf_w, buf_e, buf_m, sems,
):
    first = ids[0] == 0

    rows = slice(CHIPS * FROWS, CHIPS * FROWS + MROWS)
    mine, other = own[rows], sib[rows]
    middle = pltpu.roll(mine + other, SIDE, 1)
    table = []
    for mat, rows in enumerate(
        (jnp.where(first, mine, other), middle, jnp.where(first, other, mine))
    ):
        rows = jnp.concatenate([rows[:, 0:COLS], rows[:, COLS : 2 * COLS]], axis=0)
        gram = outer(qt[mat], rows)
        rest = jnp.zeros((RANK, BLOCK - PAIR), jnp.float32)
        table.append(jnp.concatenate([gram, rows, rest], axis=1))
    table = jnp.stack(table)
    row = lax.broadcasted_iota(jnp.int32, table.shape, 1)
    small = table
    for step in range(RANK):
        spread = jnp.broadcast_to(table[:, :, step : step + 1], table.shape)
        pivot = spread[:, step : step + 1, :]
        line = table[:, step : step + 1, :]
        scaled = line * (1.0 / pivot)
        here = row == step
        small = jnp.where(here, line * lax.rsqrt(pivot), small)
        table = jnp.where(here, scaled, table - spread * scaled)

    left = left_side(8)
    for block in range(BLOCKS):
        lanes = slice(block * BLOCK, (block + 1) * BLOCK)
        rows = slice(block * FROWS, block * FROWS + FROWS)
        mine, other = own[rows], sib[rows]
        low, high = jnp.where(first, mine, other), jnp.where(first, other, mine)
        low_half, high_half = low[RANK:FROWS], high[RANK:FROWS]
        half = jnp.concatenate(
            [
                jnp.where(left, low_half, swap_sides(high_half)),
                jnp.where(left, swap_sides(low_half), high_half),
            ],
            axis=0,
        )
        for mat, value in enumerate((low[0:RANK], half, high[0:RANK])):
            top, mid, last = split(value)
            for place, part in enumerate((top, mid, last, top, mid, top)):
                fac[mat, place * RANK : place * RANK + RANK, lanes] = part

    for mat in range(MATS):
        out_f[mat] = small[mat, :, RANK:PAIR] * (1.0 / islands)
        top, mid, last = split(table[mat, :, RANK:PAIR] * (1.0 / islands))
        parts = [x.astype(jnp.float32) for x in (top, top, top, mid, mid, last)]
        mixed = jnp.transpose(jnp.concatenate(parts, axis=0)).astype(jnp.bfloat16)
        for tile in range(7):
            lanes = slice(tile * 256, (tile + 1) * 256)
            approx = jnp.dot(mixed, fac[mat, :, lanes], preferred_element_type=jnp.float32)
            wide = w[mat, :, lanes].astype(jnp.float32)
            momentum = 0.9 * mom[mat, :, lanes] + approx
            buf_e[mat, :, lanes] = drift[mat, :, lanes] - approx
            buf_m[mat, :, lanes] = momentum
            buf_w[mat, :, lanes] = (wide - 0.7 * (approx + 0.9 * momentum)).astype(jnp.bfloat16)
        for kind, (buf, out) in enumerate(((buf_w, out_w), (buf_e, out_e), (buf_m, out_m))):
            pltpu.make_async_copy(buf.at[mat], out.at[mat], sems.at[kind, mat]).start()
    for mat in range(MATS):
        for kind, (buf, out) in enumerate(((buf_w, out_w), (buf_e, out_e), (buf_m, out_m))):
            pltpu.make_async_copy(buf.at[mat], out.at[mat], sems.at[kind, mat]).wait()


def sibling(x):
    return lax.ppermute(x, "replica", [(i, i ^ 1) for i in range(2 * CHIPS)])


def exchange_z(x):
    groups = [[2 * chip + core for chip in range(CHIPS)] for core in range(2)]
    return lax.all_to_all(x, "replica", 0, 0, axis_index_groups=groups, tiled=True)


def local(weights, local_weights, carried_error, momentum, initial_factor):
    f32 = jnp.float32
    ids = (lax.axis_index("replica") & 1).astype(jnp.int32).reshape(1)
    shape = (MATS, COLS, WIDTH)
    keep, send, drift = pl.pallas_call(
        pack_kernel,
        out_shape=[pltpu.VMEM((CHIPS, SHARE, BLOCK), f32)] * 2 + [pltpu.VMEM(shape, f32)],
        in_specs=[SMEM, HBM, HBM, HBM],
        out_specs=[VMEM] * 3,
        scratch_shapes=[
            pltpu.VMEM(shape, jnp.bfloat16),
            pltpu.VMEM(shape, jnp.bfloat16),
            pltpu.VMEM(shape, f32),
            pltpu.SemaphoreType.DMA((3, 3)),
        ],
        compiler_params=PACK_PARAMS,
        name="pack",
    )(ids, weights, local_weights[0], carried_error[0])
    qt = jnp.swapaxes(initial_factor, 1, 2)
    shares = exchange_z(keep + sibling(send))
    inner, factor = pl.pallas_call(
        factor_kernel,
        out_shape=[
            jax.ShapeDtypeStruct((MROWS, BLOCK), f32),
            jax.ShapeDtypeStruct((FROWS, BLOCK), f32),
        ],
        in_specs=[SMEM, VMEM, VMEM],
        out_specs=[VMEM, VMEM],
        compiler_params=PARAMS,
        name="factor",
    )(ids, qt, shares)

    rows = exchange_z(
        jnp.broadcast_to(jnp.concatenate([factor, inner]), (CHIPS, GROWS, BLOCK))
    )
    inner = jnp.sum(rows[:, FROWS:], axis=0)
    inner = lax.all_to_all(
        jnp.broadcast_to(inner, (16, MROWS, BLOCK)), "fsdp", 0, 0, tiled=True
    )
    own = jnp.concatenate(
        [rows[:, :FROWS].reshape(CHIPS * FROWS, BLOCK), jnp.sum(inner, axis=0)]
    )
    sib = sibling(own)

    next_weights, next_error, next_momentum, following = pl.pallas_call(
        lambda *refs: final_kernel(lax.axis_size("replica"), *refs),
        out_shape=[
            jax.ShapeDtypeStruct(shape, jnp.bfloat16),
            jax.ShapeDtypeStruct(shape, f32),
            jax.ShapeDtypeStruct(shape, f32),
            jax.ShapeDtypeStruct((MATS, RANK, COLS), f32),
        ],
        in_specs=[SMEM] + [VMEM] * 6,
        out_specs=[HBM, HBM, HBM, VMEM],
        scratch_shapes=[
            pltpu.VMEM((MATS, 6 * RANK, WIDTH), jnp.bfloat16),
            pltpu.VMEM(shape, jnp.bfloat16),
            pltpu.VMEM(shape, f32),
            pltpu.VMEM(shape, f32),
            pltpu.SemaphoreType.DMA((3, 3)),
        ],
        compiler_params=PARAMS,
        name="final",
    )(ids, qt, own, sib, weights, momentum, drift)
    return (next_weights, next_error[None], next_momentum, jnp.swapaxes(following, 1, 2))


def solution(mesh):
    return jax.shard_map(
        local,
        mesh=mesh,
        in_specs=(
            P(None, None, "fsdp"),
            P("replica", None, None, "fsdp"),
            P("replica", None, None, "fsdp"),
            P(None, None, "fsdp"),
            P(),
        ),
        out_specs=(
            P(None, None, "fsdp"),
            P("replica", None, None, "fsdp"),
            P(None, None, "fsdp"),
            P(),
        ),
        check_vma=False,
    )
```

```python
import jax
import jax.numpy as jnp
from jax import lax
from jax.experimental import pallas as pl
from jax.experimental.pallas import tpu as pltpu
from jax.sharding import PartitionSpec as P

CHIPS = 16
BLOCK = 128
SIDE = BLOCK // 2
BLOCKS = 14
WIDTH = BLOCK * BLOCKS
MATS = 3
COLS = 32
RANK = 16
SHARE = MATS * COLS // 2
FROWS = SHARE // 2
MROWS = 8
PAIR = RANK + COLS
HIGHEST = lax.Precision.HIGHEST
VMEM = pl.BlockSpec(memory_space=pltpu.VMEM)
SMEM = pl.BlockSpec(memory_space=pltpu.SMEM)
HBM = pl.BlockSpec(memory_space=pl.ANY)
PARAMS = pltpu.CompilerParams(vmem_limit_bytes=32 * 1024 * 1024)
PACK_PARAMS = pltpu.CompilerParams(vmem_limit_bytes=56 * 1024 * 1024)


def swap_sides(x):
    return pltpu.roll(x, SIDE, 1)


def left_side(rows):
    return lax.broadcasted_iota(jnp.int32, (rows, BLOCK), 1) < SIDE


def pack_kernel(ids, w_hbm, lw_hbm, ce_hbm, keep, send, drift, w, lw, ce, sems):
    core = ids[0]
    copies = [
        [
            pltpu.make_async_copy(src.at[mat], dst.at[mat], sems.at[kind, mat])
            for kind, (src, dst) in enumerate(((ce_hbm, ce), (w_hbm, w), (lw_hbm, lw)))
        ]
        for mat in range(MATS)
    ]
    for group in copies:
        for copy in group:
            copy.start()
    left = left_side(16)
    for out in (keep, send):
        out[BLOCKS:CHIPS] = jnp.zeros((CHIPS - BLOCKS, SHARE, BLOCK), jnp.float32)
    for mat in range(MATS):
        for copy in copies[mat]:
            copy.wait()
        for block in range(BLOCKS):
            lanes = slice(block * BLOCK, (block + 1) * BLOCK)
            value = (
                w[mat, :, lanes].astype(jnp.float32)
                - lw[mat, :, lanes].astype(jnp.float32)
                + ce[mat, :, lanes]
            )
            drift[mat, :, lanes] = value
    for block in range(BLOCKS):
        lanes = slice(block * BLOCK, (block + 1) * BLOCK)
        keep[block, 0:COLS] = drift[2 * core, :, lanes]
        send[block, 0:COLS] = drift[2 - 2 * core, :, lanes]
        top, bottom = drift[1, 0:16, lanes], drift[1, 16:32, lanes]
        first = jnp.where(left, top, swap_sides(bottom))
        second = jnp.where(left, swap_sides(top), bottom)
        keep[block, COLS:SHARE] = jnp.where(core == 0, first, second)
        send[block, COLS:SHARE] = jnp.where(core == 0, second, first)


def outer(a, b):
    return lax.dot_general(
        a, b, (((1,), (1,)), ((), ())), precision=HIGHEST, preferred_element_type=jnp.float32
    )


def factor_kernel(ids, qt, got, inner, factor):
    core = ids[0]
    total = jnp.sum(got[...], axis=0)
    left = left_side(16)
    whole = total[0:COLS]
    half = total[COLS:SHARE]
    half = jnp.concatenate(
        [jnp.where(left, half, 0.0), jnp.where(left, swap_sides(half), 0.0)], axis=0
    )
    whole_factor = jnp.dot(
        qt[2 * core], whole, precision=HIGHEST, preferred_element_type=jnp.float32
    )
    half_factor = jnp.dot(qt[1], half, precision=HIGHEST, preferred_element_type=jnp.float32)
    factor[0:RANK] = whole_factor
    factor[RANK:FROWS] = half_factor[0:8] + swap_sides(half_factor[8:16])
    whole, half = outer(whole_factor, whole), outer(half_factor, half)
    inner[...] = jnp.concatenate([whole[0:8], whole[8:16], half[0:8], half[8:16]], axis=1)


def split(x):
    high = x.astype(jnp.bfloat16)
    rest = x - high.astype(jnp.float32)
    middle = rest.astype(jnp.bfloat16)
    return high, middle, (rest - middle.astype(jnp.float32)).astype(jnp.bfloat16)


def unpack_kernel(ids, own, sib, fac):
    first = ids[0] == 0
    left = left_side(8)
    for block in range(BLOCKS):
        lanes = slice(block * BLOCK, (block + 1) * BLOCK)
        mine, other = own[block], sib[block]
        low, high = jnp.where(first, mine, other), jnp.where(first, other, mine)
        low_half, high_half = low[RANK:FROWS], high[RANK:FROWS]
        half = jnp.concatenate(
            [
                jnp.where(left, low_half, swap_sides(high_half)),
                jnp.where(left, swap_sides(low_half), high_half),
            ],
            axis=0,
        )
        for mat, value in enumerate((low[0:RANK], half, high[0:RANK])):
            top, mid, last = split(value)
            for place, part in enumerate((top, mid, last, top, mid, top)):
                fac[mat, place * RANK : place * RANK + RANK, lanes] = part


def final_kernel(
    islands, ids, qt, own, sib, fac, w, mom, drift,
    out_w, out_e, out_m, out_f, buf_w, buf_e, buf_m, sems,
):
    first = ids[0] == 0

    mine, other = own[...], sib[...]
    middle = pltpu.roll(mine + other, SIDE, 1)
    table = []
    for mat, rows in enumerate(
        (jnp.where(first, mine, other), middle, jnp.where(first, other, mine))
    ):
        rows = jnp.concatenate([rows[:, 0:COLS], rows[:, COLS : 2 * COLS]], axis=0)
        gram = outer(qt[mat], rows)
        rest = jnp.zeros((RANK, BLOCK - PAIR), jnp.float32)
        table.append(jnp.concatenate([gram, rows, rest], axis=1))
    table = jnp.stack(table)
    row = lax.broadcasted_iota(jnp.int32, table.shape, 1)
    small = table
    for step in range(RANK):
        spread = jnp.broadcast_to(table[:, :, step : step + 1], table.shape)
        pivot = spread[:, step : step + 1, :]
        line = table[:, step : step + 1, :]
        scaled = line * (1.0 / pivot)
        here = row == step
        small = jnp.where(here, line * lax.rsqrt(pivot), small)
        table = jnp.where(here, scaled, table - spread * scaled)

    for mat in range(MATS):
        out_f[mat] = small[mat, :, RANK:PAIR] * (1.0 / islands)
        top, mid, last = split(table[mat, :, RANK:PAIR] * (1.0 / islands))
        parts = [x.astype(jnp.float32) for x in (top, top, top, mid, mid, last)]
        mixed = jnp.transpose(jnp.concatenate(parts, axis=0)).astype(jnp.bfloat16)
        for tile in range(7):
            lanes = slice(tile * 256, (tile + 1) * 256)
            approx = jnp.dot(mixed, fac[mat, :, lanes], preferred_element_type=jnp.float32)
            wide = w[mat, :, lanes].astype(jnp.float32)
            momentum = 0.9 * mom[mat, :, lanes] + approx
            buf_e[mat, :, lanes] = drift[mat, :, lanes] - approx
            buf_m[mat, :, lanes] = momentum
            buf_w[mat, :, lanes] = (wide - 0.7 * (approx + 0.9 * momentum)).astype(jnp.bfloat16)
        for kind, (buf, out) in enumerate(((buf_w, out_w), (buf_e, out_e), (buf_m, out_m))):
            pltpu.make_async_copy(buf.at[mat], out.at[mat], sems.at[kind, mat]).start()
    for mat in range(MATS):
        for kind, (buf, out) in enumerate(((buf_w, out_w), (buf_e, out_e), (buf_m, out_m))):
            pltpu.make_async_copy(buf.at[mat], out.at[mat], sems.at[kind, mat]).wait()


def sibling(x):
    return lax.ppermute(x, "replica", [(i, i ^ 1) for i in range(2 * CHIPS)])


def exchange_z(x):
    groups = [[2 * chip + core for chip in range(CHIPS)] for core in range(2)]
    return lax.all_to_all(x, "replica", 0, 0, axis_index_groups=groups, tiled=True)


def local(weights, local_weights, carried_error, momentum, initial_factor):
    f32 = jnp.float32
    ids = (lax.axis_index("replica") & 1).astype(jnp.int32).reshape(1)
    shape = (MATS, COLS, WIDTH)
    keep, send, drift = pl.pallas_call(
        pack_kernel,
        out_shape=[pltpu.VMEM((CHIPS, SHARE, BLOCK), f32)] * 2 + [pltpu.VMEM(shape, f32)],
        in_specs=[SMEM, HBM, HBM, HBM],
        out_specs=[VMEM] * 3,
        scratch_shapes=[
            pltpu.VMEM(shape, jnp.bfloat16),
            pltpu.VMEM(shape, jnp.bfloat16),
            pltpu.VMEM(shape, f32),
            pltpu.SemaphoreType.DMA((3, 3)),
        ],
        compiler_params=PACK_PARAMS,
        name="pack",
    )(ids, weights, local_weights[0], carried_error[0])
    qt = jnp.swapaxes(initial_factor, 1, 2)
    shares = exchange_z(keep + sibling(send))
    inner, factor = pl.pallas_call(
        factor_kernel,
        out_shape=[
            jax.ShapeDtypeStruct((MROWS, BLOCK), f32),
            jax.ShapeDtypeStruct((FROWS, BLOCK), f32),
        ],
        in_specs=[SMEM, VMEM, VMEM],
        out_specs=[VMEM, VMEM],
        compiler_params=PARAMS,
        name="factor",
    )(ids, qt, shares)

    inner = lax.all_to_all(
        jnp.broadcast_to(inner, (16, MROWS, BLOCK)), "fsdp", 0, 0, tiled=True
    )
    fown = exchange_z(jnp.broadcast_to(factor, (CHIPS, FROWS, BLOCK)))
    inner = jnp.sum(inner, axis=0)
    inner = exchange_z(jnp.broadcast_to(inner, (CHIPS, MROWS, BLOCK)))
    fac = pl.pallas_call(
        unpack_kernel,
        out_shape=pltpu.VMEM((MATS, 6 * RANK, WIDTH), jnp.bfloat16),
        in_specs=[SMEM, VMEM, VMEM],
        out_specs=VMEM,
        compiler_params=PARAMS,
        cost_estimate=pl.CostEstimate(flops=500_000, bytes_accessed=1_500_000, transcendentals=0),
        name="unpack",
    )(ids, fown, sibling(fown))
    inner = jnp.sum(inner, axis=0)

    next_weights, next_error, next_momentum, following = pl.pallas_call(
        lambda *refs: final_kernel(lax.axis_size("replica"), *refs),
        out_shape=[
            jax.ShapeDtypeStruct(shape, jnp.bfloat16),
            jax.ShapeDtypeStruct(shape, f32),
            jax.ShapeDtypeStruct(shape, f32),
            jax.ShapeDtypeStruct((MATS, RANK, COLS), f32),
        ],
        in_specs=[SMEM] + [VMEM] * 7,
        out_specs=[HBM, HBM, HBM, VMEM],
        scratch_shapes=[
            pltpu.VMEM(shape, jnp.bfloat16),
            pltpu.VMEM(shape, f32),
            pltpu.VMEM(shape, f32),
            pltpu.SemaphoreType.DMA((3, 3)),
        ],
        compiler_params=PARAMS,
        name="final",
    )(ids, qt, inner, sibling(inner), fac, weights, momentum, drift)
    return (next_weights, next_error[None], next_momentum, jnp.swapaxes(following, 1, 2))


def solution(mesh):
    return jax.shard_map(
        local,
        mesh=mesh,
        in_specs=(
            P(None, None, "fsdp"),
            P("replica", None, None, "fsdp"),
            P("replica", None, None, "fsdp"),
            P(None, None, "fsdp"),
            P(),
        ),
        out_specs=(
            P(None, None, "fsdp"),
            P("replica", None, None, "fsdp"),
            P(None, None, "fsdp"),
            P(),
        ),
        check_vma=False,
    )
```

```python
import jax
import jax.numpy as jnp
from jax import lax
from jax.experimental import pallas as pl
from jax.experimental.pallas import tpu as pltpu
from jax.sharding import PartitionSpec as P

CHIPS = 16
BLOCK = 128
SIDE = BLOCK // 2
BLOCKS = 14
WIDTH = BLOCK * BLOCKS
MATS = 3
COLS = 32
RANK = 16
SHARE = MATS * COLS // 2
FROWS = SHARE // 2
MROWS = 8
GROWS = FROWS + MROWS
PAIR = RANK + COLS
HIGHEST = lax.Precision.HIGHEST
VMEM = pl.BlockSpec(memory_space=pltpu.VMEM)
SMEM = pl.BlockSpec(memory_space=pltpu.SMEM)
HBM = pl.BlockSpec(memory_space=pl.ANY)
PARAMS = pltpu.CompilerParams(vmem_limit_bytes=32 * 1024 * 1024)
PACK_PARAMS = pltpu.CompilerParams(vmem_limit_bytes=56 * 1024 * 1024)


def swap_sides(x):
    return pltpu.roll(x, SIDE, 1)


def left_side(rows):
    return lax.broadcasted_iota(jnp.int32, (rows, BLOCK), 1) < SIDE


def pack_kernel(ids, w_hbm, lw_hbm, ce_hbm, keep, send, drift, w, lw, ce, sems):
    core = ids[0]
    copies = [
        [
            pltpu.make_async_copy(src.at[mat], dst.at[mat], sems.at[kind, mat])
            for kind, (src, dst) in enumerate(((ce_hbm, ce), (w_hbm, w), (lw_hbm, lw)))
        ]
        for mat in range(MATS)
    ]
    for group in copies:
        for copy in group:
            copy.start()
    left = left_side(16)
    flip = core * (CHIPS - 1)
    for block in range(BLOCKS, CHIPS):
        keep[block ^ flip] = jnp.zeros((SHARE, BLOCK), jnp.float32)
        send[(block ^ (CHIPS - 1)) ^ flip] = jnp.zeros((SHARE, BLOCK), jnp.float32)
    for mat in range(MATS):
        for copy in copies[mat]:
            copy.wait()
        for block in range(BLOCKS):
            lanes = slice(block * BLOCK, (block + 1) * BLOCK)
            value = (
                w[mat, :, lanes].astype(jnp.float32)
                - lw[mat, :, lanes].astype(jnp.float32)
                + ce[mat, :, lanes]
            )
            drift[mat, :, lanes] = value
    for block in range(BLOCKS):
        lanes = slice(block * BLOCK, (block + 1) * BLOCK)
        keep[block ^ flip, 0:COLS] = drift[2 * core, :, lanes]
        send[(block ^ (CHIPS - 1)) ^ flip, 0:COLS] = drift[2 - 2 * core, :, lanes]
        top, bottom = drift[1, 0:16, lanes], drift[1, 16:32, lanes]
        first = jnp.where(left, top, swap_sides(bottom))
        second = jnp.where(left, swap_sides(top), bottom)
        keep[block ^ flip, COLS:SHARE] = jnp.where(core == 0, first, second)
        send[(block ^ (CHIPS - 1)) ^ flip, COLS:SHARE] = jnp.where(core == 0, second, first)


def outer(a, b):
    return lax.dot_general(
        a, b, (((1,), (1,)), ((), ())), precision=HIGHEST, preferred_element_type=jnp.float32
    )


def factor_kernel(ids, qt, got, inner, factor):
    core = ids[0]
    total = jnp.sum(got[...], axis=0)
    left = left_side(16)
    whole = total[0:COLS]
    half = total[COLS:SHARE]
    half = jnp.concatenate(
        [jnp.where(left, half, 0.0), jnp.where(left, swap_sides(half), 0.0)], axis=0
    )
    whole_factor = jnp.dot(
        qt[2 * core], whole, precision=HIGHEST, preferred_element_type=jnp.float32
    )
    half_factor = jnp.dot(qt[1], half, precision=HIGHEST, preferred_element_type=jnp.float32)
    factor[0:RANK] = whole_factor
    factor[RANK:FROWS] = half_factor[0:8] + swap_sides(half_factor[8:16])
    whole, half = outer(whole_factor, whole), outer(half_factor, half)
    inner[...] = jnp.concatenate([whole[0:8], whole[8:16], half[0:8], half[8:16]], axis=1)


def split(x):
    high = x.astype(jnp.bfloat16)
    rest = x - high.astype(jnp.float32)
    middle = rest.astype(jnp.bfloat16)
    return high, middle, (rest - middle.astype(jnp.float32)).astype(jnp.bfloat16)


def final_kernel(
    islands, ids, qt, own, sib, w, mom, drift,
    out_w, out_e, out_m, out_f, fac, buf_w, buf_e, buf_m, sems,
):
    first = ids[0] == 0

    mine = jnp.sum(own[:, FROWS:GROWS], axis=0)
    other = jnp.sum(sib[:, FROWS:GROWS], axis=0)
    middle = pltpu.roll(mine + other, SIDE, 1)
    table = []
    for mat, rows in enumerate(
        (jnp.where(first, mine, other), middle, jnp.where(first, other, mine))
    ):
        rows = jnp.concatenate([rows[:, 0:COLS], rows[:, COLS : 2 * COLS]], axis=0)
        gram = outer(qt[mat], rows)
        rest = jnp.zeros((RANK, BLOCK - PAIR), jnp.float32)
        table.append(jnp.concatenate([gram, rows, rest], axis=1))
    table = jnp.stack(table)
    row = lax.broadcasted_iota(jnp.int32, table.shape, 1)
    small = table
    for step in range(RANK):
        spread = jnp.broadcast_to(table[:, :, step : step + 1], table.shape)
        pivot = spread[:, step : step + 1, :]
        line = table[:, step : step + 1, :]
        scaled = line * (1.0 / pivot)
        here = row == step
        small = jnp.where(here, line * lax.rsqrt(pivot), small)
        table = jnp.where(here, scaled, table - spread * scaled)

    flip = ids[0] * (CHIPS - 1)
    left = left_side(8)
    for block in range(BLOCKS):
        lanes = slice(block * BLOCK, (block + 1) * BLOCK)
        mine = own[block ^ flip, 0:FROWS]
        other = sib[(block ^ (CHIPS - 1)) ^ flip, 0:FROWS]
        low, high = jnp.where(first, mine, other), jnp.where(first, other, mine)
        low_half, high_half = low[RANK:FROWS], high[RANK:FROWS]
        half = jnp.concatenate(
            [
                jnp.where(left, low_half, swap_sides(high_half)),
                jnp.where(left, swap_sides(low_half), high_half),
            ],
            axis=0,
        )
        for mat, value in enumerate((low[0:RANK], half, high[0:RANK])):
            top, mid, last = split(value)
            for place, part in enumerate((top, mid, last, top, mid, top)):
                fac[mat, place * RANK : place * RANK + RANK, lanes] = part

    for mat in range(MATS):
        out_f[mat] = small[mat, :, RANK:PAIR] * (1.0 / islands)
        top, mid, last = split(table[mat, :, RANK:PAIR] * (1.0 / islands))
        parts = [x.astype(jnp.float32) for x in (top, top, top, mid, mid, last)]
        mixed = jnp.transpose(jnp.concatenate(parts, axis=0)).astype(jnp.bfloat16)
        for tile in range(7):
            lanes = slice(tile * 256, (tile + 1) * 256)
            approx = jnp.dot(mixed, fac[mat, :, lanes], preferred_element_type=jnp.float32)
            wide = w[mat, :, lanes].astype(jnp.float32)
            momentum = 0.9 * mom[mat, :, lanes] + approx
            buf_e[mat, :, lanes] = drift[mat, :, lanes] - approx
            buf_m[mat, :, lanes] = momentum
            buf_w[mat, :, lanes] = (wide - 0.7 * (approx + 0.9 * momentum)).astype(jnp.bfloat16)
        for kind, (buf, out) in enumerate(((buf_w, out_w), (buf_e, out_e), (buf_m, out_m))):
            pltpu.make_async_copy(buf.at[mat], out.at[mat], sems.at[kind, mat]).start()
    for mat in range(MATS):
        for kind, (buf, out) in enumerate(((buf_w, out_w), (buf_e, out_e), (buf_m, out_m))):
            pltpu.make_async_copy(buf.at[mat], out.at[mat], sems.at[kind, mat]).wait()


def sibling(x):
    return lax.ppermute(x, "replica", [(i, i ^ 1) for i in range(2 * CHIPS)])


def exchange_z(x):
    groups = [
        [2 * chip for chip in range(CHIPS)],
        [2 * chip + 1 for chip in reversed(range(CHIPS))],
    ]
    return lax.all_to_all(x, "replica", 0, 0, axis_index_groups=groups, tiled=True)


def local(weights, local_weights, carried_error, momentum, initial_factor):
    f32 = jnp.float32
    ids = (lax.axis_index("replica") & 1).astype(jnp.int32).reshape(1)
    shape = (MATS, COLS, WIDTH)
    keep, send, drift = pl.pallas_call(
        pack_kernel,
        out_shape=[pltpu.VMEM((CHIPS, SHARE, BLOCK), f32)] * 2 + [pltpu.VMEM(shape, f32)],
        in_specs=[SMEM, HBM, HBM, HBM],
        out_specs=[VMEM] * 3,
        scratch_shapes=[
            pltpu.VMEM(shape, jnp.bfloat16),
            pltpu.VMEM(shape, jnp.bfloat16),
            pltpu.VMEM(shape, f32),
            pltpu.SemaphoreType.DMA((3, 3)),
        ],
        compiler_params=PACK_PARAMS,
        name="pack",
    )(ids, weights, local_weights[0], carried_error[0])
    qt = jnp.swapaxes(initial_factor, 1, 2)
    shares = exchange_z(keep + sibling(send))
    inner, factor = pl.pallas_call(
        factor_kernel,
        out_shape=[
            jax.ShapeDtypeStruct((MROWS, BLOCK), f32),
            jax.ShapeDtypeStruct((FROWS, BLOCK), f32),
        ],
        in_specs=[SMEM, VMEM, VMEM],
        out_specs=[VMEM, VMEM],
        compiler_params=PARAMS,
        name="factor",
    )(ids, qt, shares)

    inner = lax.all_to_all(
        jnp.broadcast_to(inner, (16, MROWS, BLOCK)), "fsdp", 0, 0, tiled=True
    )
    inner = jnp.sum(inner, axis=0)
    own = exchange_z(
        jnp.broadcast_to(jnp.concatenate([factor, inner]), (CHIPS, GROWS, BLOCK))
    )
    sib = sibling(own)

    next_weights, next_error, next_momentum, following = pl.pallas_call(
        lambda *refs: final_kernel(lax.axis_size("replica"), *refs),
        out_shape=[
            jax.ShapeDtypeStruct(shape, jnp.bfloat16),
            jax.ShapeDtypeStruct(shape, f32),
            jax.ShapeDtypeStruct(shape, f32),
            jax.ShapeDtypeStruct((MATS, RANK, COLS), f32),
        ],
        in_specs=[SMEM] + [VMEM] * 6,
        out_specs=[HBM, HBM, HBM, VMEM],
        scratch_shapes=[
            pltpu.VMEM((MATS, 6 * RANK, WIDTH), jnp.bfloat16),
            pltpu.VMEM(shape, jnp.bfloat16),
            pltpu.VMEM(shape, f32),
            pltpu.VMEM(shape, f32),
            pltpu.SemaphoreType.DMA((3, 3)),
        ],
        compiler_params=PARAMS,
        name="final",
    )(ids, qt, own, sib, weights, momentum, drift)
    return (next_weights, next_error[None], next_momentum, jnp.swapaxes(following, 1, 2))


def solution(mesh):
    return jax.shard_map(
        local,
        mesh=mesh,
        in_specs=(
            P(None, None, "fsdp"),
            P("replica", None, None, "fsdp"),
            P("replica", None, None, "fsdp"),
            P(None, None, "fsdp"),
            P(),
        ),
        out_specs=(
            P(None, None, "fsdp"),
            P("replica", None, None, "fsdp"),
            P(None, None, "fsdp"),
            P(),
        ),
        check_vma=False,
    )
```

```python
import jax
import jax.numpy as jnp
from jax import lax
from jax.experimental import pallas as pl
from jax.experimental.pallas import tpu as pltpu
from jax.sharding import PartitionSpec as P

CHIPS = 16
BLOCK = 128
SIDE = BLOCK // 2
BLOCKS = 14
WIDTH = BLOCK * BLOCKS
MATS = 3
COLS = 32
RANK = 16
SHARE = MATS * COLS // 2
FROWS = SHARE // 2
MROWS = 8
GROWS = FROWS + MROWS
PAIR = RANK + COLS
HIGHEST = lax.Precision.HIGHEST
VMEM = pl.BlockSpec(memory_space=pltpu.VMEM)
SMEM = pl.BlockSpec(memory_space=pltpu.SMEM)
HBM = pl.BlockSpec(memory_space=pl.ANY)
PARAMS = pltpu.CompilerParams(vmem_limit_bytes=32 * 1024 * 1024)
PACK_PARAMS = pltpu.CompilerParams(vmem_limit_bytes=56 * 1024 * 1024)


REVERSED = [int(format(i, "04b")[::-1], 2) for i in range(CHIPS)]


def slot_of(chip, core):
    return REVERSED[chip] ^ (3 * core)


def chip_at(slot, core):
    return REVERSED[slot ^ (3 * core)]


def swap_sides(x):
    return pltpu.roll(x, SIDE, 1)


def left_side(rows):
    return lax.broadcasted_iota(jnp.int32, (rows, BLOCK), 1) < SIDE


def pack_kernel(ids, w_hbm, lw_hbm, ce_hbm, keep, send, drift, w, lw, ce, sems):
    core = ids[0]
    copies = [
        [
            pltpu.make_async_copy(src.at[mat], dst.at[mat], sems.at[kind, mat])
            for kind, (src, dst) in enumerate(((ce_hbm, ce), (w_hbm, w), (lw_hbm, lw)))
        ]
        for mat in range(MATS)
    ]
    for group in copies:
        for copy in group:
            copy.start()
    left = left_side(16)
    for block in range(BLOCKS, CHIPS):
        keep[slot_of(block, core)] = jnp.zeros((SHARE, BLOCK), jnp.float32)
        send[slot_of(block, 1 - core)] = jnp.zeros((SHARE, BLOCK), jnp.float32)
    for mat in range(MATS):
        for copy in copies[mat]:
            copy.wait()
        for block in range(BLOCKS):
            lanes = slice(block * BLOCK, (block + 1) * BLOCK)
            value = (
                w[mat, :, lanes].astype(jnp.float32)
                - lw[mat, :, lanes].astype(jnp.float32)
                + ce[mat, :, lanes]
            )
            drift[mat, :, lanes] = value
    for block in range(BLOCKS):
        lanes = slice(block * BLOCK, (block + 1) * BLOCK)
        keep[slot_of(block, core), 0:COLS] = drift[2 * core, :, lanes]
        send[slot_of(block, 1 - core), 0:COLS] = drift[2 - 2 * core, :, lanes]
        top, bottom = drift[1, 0:16, lanes], drift[1, 16:32, lanes]
        first = jnp.where(left, top, swap_sides(bottom))
        second = jnp.where(left, swap_sides(top), bottom)
        keep[slot_of(block, core), COLS:SHARE] = jnp.where(core == 0, first, second)
        send[slot_of(block, 1 - core), COLS:SHARE] = jnp.where(core == 0, second, first)


def outer(a, b):
    return lax.dot_general(
        a, b, (((1,), (1,)), ((), ())), precision=HIGHEST, preferred_element_type=jnp.float32
    )


def factor_kernel(ids, qt, got, inner, factor):
    core = ids[0]
    total = jnp.sum(got[...], axis=0)
    left = left_side(16)
    whole = total[0:COLS]
    half = total[COLS:SHARE]
    half = jnp.concatenate(
        [jnp.where(left, half, 0.0), jnp.where(left, swap_sides(half), 0.0)], axis=0
    )
    whole_factor = jnp.dot(
        qt[2 * core], whole, precision=HIGHEST, preferred_element_type=jnp.float32
    )
    half_factor = jnp.dot(qt[1], half, precision=HIGHEST, preferred_element_type=jnp.float32)
    factor[0:RANK] = whole_factor
    factor[RANK:FROWS] = half_factor[0:8] + swap_sides(half_factor[8:16])
    whole, half = outer(whole_factor, whole), outer(half_factor, half)
    inner[...] = jnp.concatenate([whole[0:8], whole[8:16], half[0:8], half[8:16]], axis=1)


def split(x):
    high = x.astype(jnp.bfloat16)
    rest = x - high.astype(jnp.float32)
    middle = rest.astype(jnp.bfloat16)
    return high, middle, (rest - middle.astype(jnp.float32)).astype(jnp.bfloat16)


def final_kernel(
    islands, ids, qt, own, sib, w, mom, drift,
    out_w, out_e, out_m, out_f, fac, buf_w, buf_e, buf_m, sems,
):
    first = ids[0] == 0

    mine = jnp.sum(own[:, FROWS:GROWS], axis=0)
    other = jnp.sum(sib[:, FROWS:GROWS], axis=0)
    middle = pltpu.roll(mine + other, SIDE, 1)
    table = []
    for mat, rows in enumerate(
        (jnp.where(first, mine, other), middle, jnp.where(first, other, mine))
    ):
        rows = jnp.concatenate([rows[:, 0:COLS], rows[:, COLS : 2 * COLS]], axis=0)
        gram = outer(qt[mat], rows)
        rest = jnp.zeros((RANK, BLOCK - PAIR), jnp.float32)
        table.append(jnp.concatenate([gram, rows, rest], axis=1))
    table = jnp.stack(table)
    row = lax.broadcasted_iota(jnp.int32, table.shape, 1)
    small = table
    for step in range(RANK):
        spread = jnp.broadcast_to(table[:, :, step : step + 1], table.shape)
        pivot = spread[:, step : step + 1, :]
        line = table[:, step : step + 1, :]
        scaled = line * (1.0 / pivot)
        here = row == step
        small = jnp.where(here, line * lax.rsqrt(pivot), small)
        table = jnp.where(here, scaled, table - spread * scaled)

    left = left_side(8)
    for block in range(BLOCKS):
        lanes = slice(block * BLOCK, (block + 1) * BLOCK)
        mine = own[slot_of(block, ids[0]), 0:FROWS]
        other = sib[slot_of(block, 1 - ids[0]), 0:FROWS]
        low, high = jnp.where(first, mine, other), jnp.where(first, other, mine)
        low_half, high_half = low[RANK:FROWS], high[RANK:FROWS]
        half = jnp.concatenate(
            [
                jnp.where(left, low_half, swap_sides(high_half)),
                jnp.where(left, swap_sides(low_half), high_half),
            ],
            axis=0,
        )
        for mat, value in enumerate((low[0:RANK], half, high[0:RANK])):
            top, mid, last = split(value)
            for place, part in enumerate((top, mid, last, top, mid, top)):
                fac[mat, place * RANK : place * RANK + RANK, lanes] = part

    for mat in range(MATS):
        out_f[mat] = small[mat, :, RANK:PAIR] * (1.0 / islands)
        top, mid, last = split(table[mat, :, RANK:PAIR] * (1.0 / islands))
        parts = [x.astype(jnp.float32) for x in (top, top, top, mid, mid, last)]
        mixed = jnp.transpose(jnp.concatenate(parts, axis=0)).astype(jnp.bfloat16)
        for tile in range(7):
            lanes = slice(tile * 256, (tile + 1) * 256)
            approx = jnp.dot(mixed, fac[mat, :, lanes], preferred_element_type=jnp.float32)
            wide = w[mat, :, lanes].astype(jnp.float32)
            momentum = 0.9 * mom[mat, :, lanes] + approx
            buf_e[mat, :, lanes] = drift[mat, :, lanes] - approx
            buf_m[mat, :, lanes] = momentum
            buf_w[mat, :, lanes] = (wide - 0.7 * (approx + 0.9 * momentum)).astype(jnp.bfloat16)
        for kind, (buf, out) in enumerate(((buf_w, out_w), (buf_e, out_e), (buf_m, out_m))):
            pltpu.make_async_copy(buf.at[mat], out.at[mat], sems.at[kind, mat]).start()
    for mat in range(MATS):
        for kind, (buf, out) in enumerate(((buf_w, out_w), (buf_e, out_e), (buf_m, out_m))):
            pltpu.make_async_copy(buf.at[mat], out.at[mat], sems.at[kind, mat]).wait()


def sibling(x):
    return lax.ppermute(x, "replica", [(i, i ^ 1) for i in range(2 * CHIPS)])


def exchange_z(x):
    groups = [[2 * chip_at(slot, core) + core for slot in range(CHIPS)] for core in range(2)]
    return lax.all_to_all(x, "replica", 0, 0, axis_index_groups=groups, tiled=True)


def local(weights, local_weights, carried_error, momentum, initial_factor):
    f32 = jnp.float32
    ids = (lax.axis_index("replica") & 1).astype(jnp.int32).reshape(1)
    shape = (MATS, COLS, WIDTH)
    keep, send, drift = pl.pallas_call(
        pack_kernel,
        out_shape=[pltpu.VMEM((CHIPS, SHARE, BLOCK), f32)] * 2 + [pltpu.VMEM(shape, f32)],
        in_specs=[SMEM, HBM, HBM, HBM],
        out_specs=[VMEM] * 3,
        scratch_shapes=[
            pltpu.VMEM(shape, jnp.bfloat16),
            pltpu.VMEM(shape, jnp.bfloat16),
            pltpu.VMEM(shape, f32),
            pltpu.SemaphoreType.DMA((3, 3)),
        ],
        compiler_params=PACK_PARAMS,
        name="pack",
    )(ids, weights, local_weights[0], carried_error[0])
    qt = jnp.swapaxes(initial_factor, 1, 2)
    shares = exchange_z(keep + sibling(send))
    inner, factor = pl.pallas_call(
        factor_kernel,
        out_shape=[
            jax.ShapeDtypeStruct((MROWS, BLOCK), f32),
            jax.ShapeDtypeStruct((FROWS, BLOCK), f32),
        ],
        in_specs=[SMEM, VMEM, VMEM],
        out_specs=[VMEM, VMEM],
        compiler_params=PARAMS,
        name="factor",
    )(ids, qt, shares)

    inner = lax.all_to_all(
        jnp.broadcast_to(inner, (16, MROWS, BLOCK)), "fsdp", 0, 0, tiled=True
    )
    inner = jnp.sum(inner, axis=0)
    own = exchange_z(
        jnp.broadcast_to(jnp.concatenate([factor, inner]), (CHIPS, GROWS, BLOCK))
    )
    sib = sibling(own)

    next_weights, next_error, next_momentum, following = pl.pallas_call(
        lambda *refs: final_kernel(lax.axis_size("replica"), *refs),
        out_shape=[
            jax.ShapeDtypeStruct(shape, jnp.bfloat16),
            jax.ShapeDtypeStruct(shape, f32),
            jax.ShapeDtypeStruct(shape, f32),
            jax.ShapeDtypeStruct((MATS, RANK, COLS), f32),
        ],
        in_specs=[SMEM] + [VMEM] * 6,
        out_specs=[HBM, HBM, HBM, VMEM],
        scratch_shapes=[
            pltpu.VMEM((MATS, 6 * RANK, WIDTH), jnp.bfloat16),
            pltpu.VMEM(shape, jnp.bfloat16),
            pltpu.VMEM(shape, f32),
            pltpu.VMEM(shape, f32),
            pltpu.SemaphoreType.DMA((3, 3)),
        ],
        compiler_params=PARAMS,
        name="final",
    )(ids, qt, own, sib, weights, momentum, drift)
    return (next_weights, next_error[None], next_momentum, jnp.swapaxes(following, 1, 2))


def solution(mesh):
    return jax.shard_map(
        local,
        mesh=mesh,
        in_specs=(
            P(None, None, "fsdp"),
            P("replica", None, None, "fsdp"),
            P("replica", None, None, "fsdp"),
            P(None, None, "fsdp"),
            P(),
        ),
        out_specs=(
            P(None, None, "fsdp"),
            P("replica", None, None, "fsdp"),
            P(None, None, "fsdp"),
            P(),
        ),
        check_vma=False,
    )
```

```python
import jax
import jax.numpy as jnp
from jax import lax
from jax.experimental import pallas as pl
from jax.experimental.pallas import tpu as pltpu
from jax.sharding import PartitionSpec as P

CHIPS = 16
BLOCK = 128
SIDE = BLOCK // 2
BLOCKS = 14
WIDTH = BLOCK * BLOCKS
MATS = 3
COLS = 32
RANK = 16
SHARE = MATS * COLS // 2
FROWS = SHARE // 2
MROWS = 8
GROWS = FROWS + MROWS
PAIR = RANK + COLS
HIGHEST = lax.Precision.HIGHEST
VMEM = pl.BlockSpec(memory_space=pltpu.VMEM)
SMEM = pl.BlockSpec(memory_space=pltpu.SMEM)
HBM = pl.BlockSpec(memory_space=pl.ANY)
PARAMS = pltpu.CompilerParams(vmem_limit_bytes=32 * 1024 * 1024)
PACK_PARAMS = pltpu.CompilerParams(vmem_limit_bytes=56 * 1024 * 1024)


REVERSED = [int(format(i, "04b")[::-1], 2) for i in range(CHIPS)]


def slot_of(chip, core):
    return REVERSED[chip] ^ (3 * core)


def chip_at(slot, core):
    return REVERSED[slot ^ (3 * core)]


def swap_sides(x):
    return pltpu.roll(x, SIDE, 1)


def left_side(rows):
    return lax.broadcasted_iota(jnp.int32, (rows, BLOCK), 1) < SIDE


def pack_kernel(ids, w_hbm, lw_hbm, ce_hbm, keep, send, drift, w, lw, ce, sems):
    core = ids[0]
    copies = [
        [
            pltpu.make_async_copy(src.at[mat], dst.at[mat], sems.at[kind, mat])
            for kind, (src, dst) in enumerate(((ce_hbm, ce), (w_hbm, w), (lw_hbm, lw)))
        ]
        for mat in range(MATS)
    ]
    for group in copies:
        for copy in group:
            copy.start()
    left = left_side(16)
    for block in range(BLOCKS, CHIPS):
        keep[slot_of(block, core)] = jnp.zeros((SHARE, BLOCK), jnp.float32)
        send[slot_of(block, 1 - core)] = jnp.zeros((SHARE, BLOCK), jnp.float32)
    for mat in range(MATS):
        for copy in copies[mat]:
            copy.wait()
        for block in range(BLOCKS):
            lanes = slice(block * BLOCK, (block + 1) * BLOCK)
            value = (
                w[mat, :, lanes].astype(jnp.float32)
                - lw[mat, :, lanes].astype(jnp.float32)
                + ce[mat, :, lanes]
            )
            drift[mat, :, lanes] = value
    for block in range(BLOCKS):
        lanes = slice(block * BLOCK, (block + 1) * BLOCK)
        keep[slot_of(block, core), 0:COLS] = drift[2 * core, :, lanes]
        send[slot_of(block, 1 - core), 0:COLS] = drift[2 - 2 * core, :, lanes]
        top, bottom = drift[1, 0:16, lanes], drift[1, 16:32, lanes]
        first = jnp.where(left, top, swap_sides(bottom))
        second = jnp.where(left, swap_sides(top), bottom)
        keep[slot_of(block, core), COLS:SHARE] = jnp.where(core == 0, first, second)
        send[slot_of(block, 1 - core), COLS:SHARE] = jnp.where(core == 0, second, first)


def outer(a, b):
    return lax.dot_general(
        a, b, (((1,), (1,)), ((), ())), precision=HIGHEST, preferred_element_type=jnp.float32
    )


def factor_kernel(ids, qt, got, inner, factor):
    core = ids[0]
    total = jnp.sum(got[...], axis=0)
    left = left_side(16)
    whole = total[0:COLS]
    half = total[COLS:SHARE]
    half = jnp.concatenate(
        [jnp.where(left, half, 0.0), jnp.where(left, swap_sides(half), 0.0)], axis=0
    )
    whole_factor = jnp.dot(
        qt[2 * core], whole, precision=HIGHEST, preferred_element_type=jnp.float32
    )
    half_factor = jnp.dot(qt[1], half, precision=HIGHEST, preferred_element_type=jnp.float32)
    factor[0:RANK] = whole_factor
    factor[RANK:FROWS] = half_factor[0:8] + swap_sides(half_factor[8:16])
    whole, half = outer(whole_factor, whole), outer(half_factor, half)
    inner[...] = jnp.concatenate([whole[0:8], whole[8:16], half[0:8], half[8:16]], axis=1)


def split(x):
    high = x.astype(jnp.bfloat16)
    rest = x - high.astype(jnp.float32)
    middle = rest.astype(jnp.bfloat16)
    return high, middle, (rest - middle.astype(jnp.float32)).astype(jnp.bfloat16)


def final_kernel(
    islands, ids, qt, own, sib, w, mom, drift,
    out_w, out_e, out_m, out_f, fac, buf_w, buf_e, buf_m, sems,
):
    first = ids[0] == 0

    rows = slice(CHIPS * FROWS, CHIPS * FROWS + MROWS)
    mine, other = own[rows], sib[rows]
    middle = pltpu.roll(mine + other, SIDE, 1)
    table = []
    for mat, rows in enumerate(
        (jnp.where(first, mine, other), middle, jnp.where(first, other, mine))
    ):
        rows = jnp.concatenate([rows[:, 0:COLS], rows[:, COLS : 2 * COLS]], axis=0)
        gram = outer(qt[mat], rows)
        rest = jnp.zeros((RANK, BLOCK - PAIR), jnp.float32)
        table.append(jnp.concatenate([gram, rows, rest], axis=1))
    table = jnp.stack(table)
    row = lax.broadcasted_iota(jnp.int32, table.shape, 1)
    small = table
    for step in range(RANK):
        spread = jnp.broadcast_to(table[:, :, step : step + 1], table.shape)
        pivot = spread[:, step : step + 1, :]
        line = table[:, step : step + 1, :]
        scaled = line * (1.0 / pivot)
        here = row == step
        small = jnp.where(here, line * lax.rsqrt(pivot), small)
        table = jnp.where(here, scaled, table - spread * scaled)

    left = left_side(8)
    for block in range(BLOCKS):
        lanes = slice(block * BLOCK, (block + 1) * BLOCK)
        mine = own[pl.ds(pl.multiple_of(slot_of(block, ids[0]) * FROWS, 8), FROWS)]
        other = sib[pl.ds(pl.multiple_of(slot_of(block, 1 - ids[0]) * FROWS, 8), FROWS)]
        low, high = jnp.where(first, mine, other), jnp.where(first, other, mine)
        low_half, high_half = low[RANK:FROWS], high[RANK:FROWS]
        half = jnp.concatenate(
            [
                jnp.where(left, low_half, swap_sides(high_half)),
                jnp.where(left, swap_sides(low_half), high_half),
            ],
            axis=0,
        )
        for mat, value in enumerate((low[0:RANK], half, high[0:RANK])):
            top, mid, last = split(value)
            for place, part in enumerate((top, mid, last, top, mid, top)):
                fac[mat, place * RANK : place * RANK + RANK, lanes] = part

    for mat in range(MATS):
        out_f[mat] = small[mat, :, RANK:PAIR] * (1.0 / islands)
        top, mid, last = split(table[mat, :, RANK:PAIR] * (1.0 / islands))
        parts = [x.astype(jnp.float32) for x in (top, top, top, mid, mid, last)]
        mixed = jnp.transpose(jnp.concatenate(parts, axis=0)).astype(jnp.bfloat16)
        for tile in range(7):
            lanes = slice(tile * 256, (tile + 1) * 256)
            approx = jnp.dot(mixed, fac[mat, :, lanes], preferred_element_type=jnp.float32)
            wide = w[mat, :, lanes].astype(jnp.float32)
            momentum = 0.9 * mom[mat, :, lanes] + approx
            buf_e[mat, :, lanes] = drift[mat, :, lanes] - approx
            buf_m[mat, :, lanes] = momentum
            buf_w[mat, :, lanes] = (wide - 0.7 * (approx + 0.9 * momentum)).astype(jnp.bfloat16)
        for kind, (buf, out) in enumerate(((buf_w, out_w), (buf_e, out_e), (buf_m, out_m))):
            pltpu.make_async_copy(buf.at[mat], out.at[mat], sems.at[kind, mat]).start()
    for mat in range(MATS):
        for kind, (buf, out) in enumerate(((buf_w, out_w), (buf_e, out_e), (buf_m, out_m))):
            pltpu.make_async_copy(buf.at[mat], out.at[mat], sems.at[kind, mat]).wait()


def sibling(x):
    return lax.ppermute(x, "replica", [(i, i ^ 1) for i in range(2 * CHIPS)])


def exchange_z(x):
    groups = [[2 * chip_at(slot, core) + core for slot in range(CHIPS)] for core in range(2)]
    return lax.all_to_all(x, "replica", 0, 0, axis_index_groups=groups, tiled=True)


def exchange_mixed(x, line_core):
    lines = [
        [(2 * chip_at(slot, line_core) + line_core) * 16 + place for slot in range(CHIPS)]
        for place in range(16)
    ]
    planes = [
        [(2 * chip + 1 - line_core) * 16 + place for place in range(16)] for chip in range(CHIPS)
    ]
    return lax.all_to_all(
        x, ("replica", "fsdp"), 0, 0, axis_index_groups=lines + planes, tiled=True
    )


def local(weights, local_weights, carried_error, momentum, initial_factor):
    f32 = jnp.float32
    ids = (lax.axis_index("replica") & 1).astype(jnp.int32).reshape(1)
    shape = (MATS, COLS, WIDTH)
    keep, send, drift = pl.pallas_call(
        pack_kernel,
        out_shape=[pltpu.VMEM((CHIPS, SHARE, BLOCK), f32)] * 2 + [pltpu.VMEM(shape, f32)],
        in_specs=[SMEM, HBM, HBM, HBM],
        out_specs=[VMEM] * 3,
        scratch_shapes=[
            pltpu.VMEM(shape, jnp.bfloat16),
            pltpu.VMEM(shape, jnp.bfloat16),
            pltpu.VMEM(shape, f32),
            pltpu.SemaphoreType.DMA((3, 3)),
        ],
        compiler_params=PACK_PARAMS,
        name="pack",
    )(ids, weights, local_weights[0], carried_error[0])
    qt = jnp.swapaxes(initial_factor, 1, 2)
    shares = exchange_z(keep + sibling(send))
    inner, factor = pl.pallas_call(
        factor_kernel,
        out_shape=[
            jax.ShapeDtypeStruct((MROWS, BLOCK), f32),
            jax.ShapeDtypeStruct((FROWS, BLOCK), f32),
        ],
        in_specs=[SMEM, VMEM, VMEM],
        out_specs=[VMEM, VMEM],
        compiler_params=PARAMS,
        name="factor",
    )(ids, qt, shares)

    factors = []
    for line_core in (1, 0):
        rows = exchange_mixed(
            jnp.broadcast_to(jnp.concatenate([factor, inner]), (CHIPS, GROWS, BLOCK)), line_core
        )
        factors.append(rows[:, :FROWS])
        inner = jnp.sum(rows[:, FROWS:], axis=0)
    factors = jnp.where(ids[0] == 0, factors[1], factors[0])
    own = jnp.concatenate([factors.reshape(CHIPS * FROWS, BLOCK), inner])
    sib = sibling(own)

    next_weights, next_error, next_momentum, following = pl.pallas_call(
        lambda *refs: final_kernel(lax.axis_size("replica"), *refs),
        out_shape=[
            jax.ShapeDtypeStruct(shape, jnp.bfloat16),
            jax.ShapeDtypeStruct(shape, f32),
            jax.ShapeDtypeStruct(shape, f32),
            jax.ShapeDtypeStruct((MATS, RANK, COLS), f32),
        ],
        in_specs=[SMEM] + [VMEM] * 6,
        out_specs=[HBM, HBM, HBM, VMEM],
        scratch_shapes=[
            pltpu.VMEM((MATS, 6 * RANK, WIDTH), jnp.bfloat16),
            pltpu.VMEM(shape, jnp.bfloat16),
            pltpu.VMEM(shape, f32),
            pltpu.VMEM(shape, f32),
            pltpu.SemaphoreType.DMA((3, 3)),
        ],
        compiler_params=PARAMS,
        name="final",
    )(ids, qt, own, sib, weights, momentum, drift)
    return (next_weights, next_error[None], next_momentum, jnp.swapaxes(following, 1, 2))


def solution(mesh):
    return jax.shard_map(
        local,
        mesh=mesh,
        in_specs=(
            P(None, None, "fsdp"),
            P("replica", None, None, "fsdp"),
            P("replica", None, None, "fsdp"),
            P(None, None, "fsdp"),
            P(),
        ),
        out_specs=(
            P(None, None, "fsdp"),
            P("replica", None, None, "fsdp"),
            P(None, None, "fsdp"),
            P(),
        ),
        check_vma=False,
    )
```

```python
import jax
import jax.numpy as jnp
from jax import lax
from jax.experimental import pallas as pl
from jax.experimental.pallas import tpu as pltpu
from jax.sharding import PartitionSpec as P

CHIPS = 16
BLOCK = 128
SIDE = BLOCK // 2
BLOCKS = 14
WIDTH = BLOCK * BLOCKS
MATS = 3
COLS = 32
RANK = 16
SHARE = MATS * COLS // 2
FROWS = SHARE // 2
MROWS = 8
GROWS = FROWS + MROWS
PAIR = RANK + COLS
HIGHEST = lax.Precision.HIGHEST
VMEM = pl.BlockSpec(memory_space=pltpu.VMEM)
SMEM = pl.BlockSpec(memory_space=pltpu.SMEM)
HBM = pl.BlockSpec(memory_space=pl.ANY)
PARAMS = pltpu.CompilerParams(vmem_limit_bytes=32 * 1024 * 1024)
PACK_PARAMS = pltpu.CompilerParams(vmem_limit_bytes=56 * 1024 * 1024)


REVERSED = [int(format(i, "04b")[::-1], 2) for i in range(CHIPS)]


def slot_of(chip, core):
    return REVERSED[chip] ^ (3 * core)


def chip_at(slot, core):
    return REVERSED[slot ^ (3 * core)]


def swap_sides(x):
    return pltpu.roll(x, SIDE, 1)


def left_side(rows):
    return lax.broadcasted_iota(jnp.int32, (rows, BLOCK), 1) < SIDE


def pack_kernel(ids, w_hbm, lw_hbm, ce_hbm, keep, send, drift, w, lw, ce, sems):
    core = ids[0]
    copies = [
        [
            pltpu.make_async_copy(src.at[mat], dst.at[mat], sems.at[kind, mat])
            for kind, (src, dst) in enumerate(((ce_hbm, ce), (w_hbm, w), (lw_hbm, lw)))
        ]
        for mat in range(MATS)
    ]
    for group in copies:
        for copy in group:
            copy.start()
    left = left_side(16)
    for block in range(BLOCKS, CHIPS):
        keep[slot_of(block, core)] = jnp.zeros((SHARE, BLOCK), jnp.float32)
        send[slot_of(block, 1 - core)] = jnp.zeros((SHARE, BLOCK), jnp.float32)
    for mat in range(MATS):
        for copy in copies[mat]:
            copy.wait()
        for block in range(BLOCKS):
            lanes = slice(block * BLOCK, (block + 1) * BLOCK)
            value = (
                w[mat, :, lanes].astype(jnp.float32)
                - lw[mat, :, lanes].astype(jnp.float32)
                + ce[mat, :, lanes]
            )
            drift[mat, :, lanes] = value
    for block in range(BLOCKS):
        lanes = slice(block * BLOCK, (block + 1) * BLOCK)
        keep[slot_of(block, core), 0:COLS] = drift[2 * core, :, lanes]
        send[slot_of(block, 1 - core), 0:COLS] = drift[2 - 2 * core, :, lanes]
        top, bottom = drift[1, 0:16, lanes], drift[1, 16:32, lanes]
        first = jnp.where(left, top, swap_sides(bottom))
        second = jnp.where(left, swap_sides(top), bottom)
        keep[slot_of(block, core), COLS:SHARE] = jnp.where(core == 0, first, second)
        send[slot_of(block, 1 - core), COLS:SHARE] = jnp.where(core == 0, second, first)


def outer(a, b):
    return lax.dot_general(
        a, b, (((1,), (1,)), ((), ())), precision=HIGHEST, preferred_element_type=jnp.float32
    )


def factor_kernel(ids, qt, got, inner, factor):
    core = ids[0]
    total = jnp.sum(got[...], axis=0)
    left = left_side(16)
    whole = total[0:COLS]
    half = total[COLS:SHARE]
    half = jnp.concatenate(
        [jnp.where(left, half, 0.0), jnp.where(left, swap_sides(half), 0.0)], axis=0
    )
    whole_factor = jnp.dot(
        qt[2 * core], whole, precision=HIGHEST, preferred_element_type=jnp.float32
    )
    half_factor = jnp.dot(qt[1], half, precision=HIGHEST, preferred_element_type=jnp.float32)
    factor[0:RANK] = whole_factor
    factor[RANK:FROWS] = half_factor[0:8] + swap_sides(half_factor[8:16])
    whole, half = outer(whole_factor, whole), outer(half_factor, half)
    inner[...] = jnp.concatenate([whole[0:8], whole[8:16], half[0:8], half[8:16]], axis=1)


def choose_kernel(ids, one, two, out):
    out[CHIPS * FROWS :] = jnp.sum(two[:, FROWS:GROWS], axis=0)
    for core, arrived in enumerate((two, one)):

        @pl.when(ids[0] == core)
        def _():
            for slot in range(CHIPS):
                out[slot * FROWS : slot * FROWS + FROWS] = arrived[slot, 0:FROWS]


def split(x):
    high = x.astype(jnp.bfloat16)
    rest = x - high.astype(jnp.float32)
    middle = rest.astype(jnp.bfloat16)
    return high, middle, (rest - middle.astype(jnp.float32)).astype(jnp.bfloat16)


def final_kernel(
    islands, ids, qt, own, sib, w, mom, drift,
    out_w, out_e, out_m, out_f, fac, buf_w, buf_e, buf_m, sems,
):
    first = ids[0] == 0

    rows = slice(CHIPS * FROWS, CHIPS * FROWS + MROWS)
    mine, other = own[rows], sib[rows]
    middle = pltpu.roll(mine + other, SIDE, 1)
    table = []
    for mat, rows in enumerate(
        (jnp.where(first, mine, other), middle, jnp.where(first, other, mine))
    ):
        rows = jnp.concatenate([rows[:, 0:COLS], rows[:, COLS : 2 * COLS]], axis=0)
        gram = outer(qt[mat], rows)
        rest = jnp.zeros((RANK, BLOCK - PAIR), jnp.float32)
        table.append(jnp.concatenate([gram, rows, rest], axis=1))
    table = jnp.stack(table)
    row = lax.broadcasted_iota(jnp.int32, table.shape, 1)
    small = table
    for step in range(RANK):
        spread = jnp.broadcast_to(table[:, :, step : step + 1], table.shape)
        pivot = spread[:, step : step + 1, :]
        line = table[:, step : step + 1, :]
        scaled = line * (1.0 / pivot)
        here = row == step
        small = jnp.where(here, line * lax.rsqrt(pivot), small)
        table = jnp.where(here, scaled, table - spread * scaled)

    left = left_side(8)
    for block in range(BLOCKS):
        lanes = slice(block * BLOCK, (block + 1) * BLOCK)
        mine = own[pl.ds(pl.multiple_of(slot_of(block, ids[0]) * FROWS, 8), FROWS)]
        other = sib[pl.ds(pl.multiple_of(slot_of(block, 1 - ids[0]) * FROWS, 8), FROWS)]
        low, high = jnp.where(first, mine, other), jnp.where(first, other, mine)
        low_half, high_half = low[RANK:FROWS], high[RANK:FROWS]
        half = jnp.concatenate(
            [
                jnp.where(left, low_half, swap_sides(high_half)),
                jnp.where(left, swap_sides(low_half), high_half),
            ],
            axis=0,
        )
        for mat, value in enumerate((low[0:RANK], half, high[0:RANK])):
            top, mid, last = split(value)
            for place, part in enumerate((top, mid, last, top, mid, top)):
                fac[mat, place * RANK : place * RANK + RANK, lanes] = part

    for mat in range(MATS):
        out_f[mat] = small[mat, :, RANK:PAIR] * (1.0 / islands)
        top, mid, last = split(table[mat, :, RANK:PAIR] * (1.0 / islands))
        parts = [x.astype(jnp.float32) for x in (top, top, top, mid, mid, last)]
        mixed = jnp.transpose(jnp.concatenate(parts, axis=0)).astype(jnp.bfloat16)
        for tile in range(7):
            lanes = slice(tile * 256, (tile + 1) * 256)
            approx = jnp.dot(mixed, fac[mat, :, lanes], preferred_element_type=jnp.float32)
            wide = w[mat, :, lanes].astype(jnp.float32)
            momentum = 0.9 * mom[mat, :, lanes] + approx
            buf_e[mat, :, lanes] = drift[mat, :, lanes] - approx
            buf_m[mat, :, lanes] = momentum
            buf_w[mat, :, lanes] = (wide - 0.7 * (approx + 0.9 * momentum)).astype(jnp.bfloat16)
        for kind, (buf, out) in enumerate(((buf_w, out_w), (buf_e, out_e), (buf_m, out_m))):
            pltpu.make_async_copy(buf.at[mat], out.at[mat], sems.at[kind, mat]).start()
    for mat in range(MATS):
        for kind, (buf, out) in enumerate(((buf_w, out_w), (buf_e, out_e), (buf_m, out_m))):
            pltpu.make_async_copy(buf.at[mat], out.at[mat], sems.at[kind, mat]).wait()


def sibling(x):
    return lax.ppermute(x, "replica", [(i, i ^ 1) for i in range(2 * CHIPS)])


def exchange_z(x):
    groups = [[2 * chip_at(slot, core) + core for slot in range(CHIPS)] for core in range(2)]
    return lax.all_to_all(x, "replica", 0, 0, axis_index_groups=groups, tiled=True)


def exchange_mixed(x, line_core):
    lines = [
        [(2 * chip_at(slot, line_core) + line_core) * 16 + place for slot in range(CHIPS)]
        for place in range(16)
    ]
    planes = [
        [(2 * chip + 1 - line_core) * 16 + place for place in range(16)] for chip in range(CHIPS)
    ]
    return lax.all_to_all(
        x, ("replica", "fsdp"), 0, 0, axis_index_groups=lines + planes, tiled=True
    )


def local(weights, local_weights, carried_error, momentum, initial_factor):
    f32 = jnp.float32
    ids = (lax.axis_index("replica") & 1).astype(jnp.int32).reshape(1)
    shape = (MATS, COLS, WIDTH)
    keep, send, drift = pl.pallas_call(
        pack_kernel,
        out_shape=[pltpu.VMEM((CHIPS, SHARE, BLOCK), f32)] * 2 + [pltpu.VMEM(shape, f32)],
        in_specs=[SMEM, HBM, HBM, HBM],
        out_specs=[VMEM] * 3,
        scratch_shapes=[
            pltpu.VMEM(shape, jnp.bfloat16),
            pltpu.VMEM(shape, jnp.bfloat16),
            pltpu.VMEM(shape, f32),
            pltpu.SemaphoreType.DMA((3, 3)),
        ],
        compiler_params=PACK_PARAMS,
        name="pack",
    )(ids, weights, local_weights[0], carried_error[0])
    qt = jnp.swapaxes(initial_factor, 1, 2)
    shares = exchange_z(keep + sibling(send))
    inner, factor = pl.pallas_call(
        factor_kernel,
        out_shape=[
            jax.ShapeDtypeStruct((MROWS, BLOCK), f32),
            jax.ShapeDtypeStruct((FROWS, BLOCK), f32),
        ],
        in_specs=[SMEM, VMEM, VMEM],
        out_specs=[VMEM, VMEM],
        compiler_params=PARAMS,
        name="factor",
    )(ids, qt, shares)

    arrivals = []
    for line_core in (1, 0):
        arrivals.append(
            exchange_mixed(
                jnp.broadcast_to(jnp.concatenate([factor, inner]), (CHIPS, GROWS, BLOCK)),
                line_core,
            )
        )
        inner = jnp.sum(arrivals[-1][:, FROWS:], axis=0)
    own = pl.pallas_call(
        choose_kernel,
        out_shape=pltpu.VMEM((CHIPS * FROWS + MROWS, BLOCK), f32),
        in_specs=[SMEM, VMEM, VMEM],
        out_specs=VMEM,
        compiler_params=PARAMS,
        name="choose",
    )(ids, *arrivals)
    sib = sibling(own)

    next_weights, next_error, next_momentum, following = pl.pallas_call(
        lambda *refs: final_kernel(lax.axis_size("replica"), *refs),
        out_shape=[
            jax.ShapeDtypeStruct(shape, jnp.bfloat16),
            jax.ShapeDtypeStruct(shape, f32),
            jax.ShapeDtypeStruct(shape, f32),
            jax.ShapeDtypeStruct((MATS, RANK, COLS), f32),
        ],
        in_specs=[SMEM] + [VMEM] * 6,
        out_specs=[HBM, HBM, HBM, VMEM],
        scratch_shapes=[
            pltpu.VMEM((MATS, 6 * RANK, WIDTH), jnp.bfloat16),
            pltpu.VMEM(shape, jnp.bfloat16),
            pltpu.VMEM(shape, f32),
            pltpu.VMEM(shape, f32),
            pltpu.SemaphoreType.DMA((3, 3)),
        ],
        compiler_params=PARAMS,
        name="final",
    )(ids, qt, own, sib, weights, momentum, drift)
    return (next_weights, next_error[None], next_momentum, jnp.swapaxes(following, 1, 2))


def solution(mesh):
    return jax.shard_map(
        local,
        mesh=mesh,
        in_specs=(
            P(None, None, "fsdp"),
            P("replica", None, None, "fsdp"),
            P("replica", None, None, "fsdp"),
            P(None, None, "fsdp"),
            P(),
        ),
        out_specs=(
            P(None, None, "fsdp"),
            P("replica", None, None, "fsdp"),
            P(None, None, "fsdp"),
            P(),
        ),
        check_vma=False,
    )
```

```python
import jax
import jax.numpy as jnp
from jax import lax
from jax.experimental import pallas as pl
from jax.experimental.pallas import tpu as pltpu
from jax.sharding import PartitionSpec as P

CHIPS = 16
BLOCK = 128
SIDE = BLOCK // 2
BLOCKS = 14
WIDTH = BLOCK * BLOCKS
MATS = 3
COLS = 32
RANK = 16
SHARE = MATS * COLS // 2
FROWS = SHARE // 2
MROWS = 8
GROWS = FROWS + MROWS
PAIR = RANK + COLS
HIGHEST = lax.Precision.HIGHEST
VMEM = pl.BlockSpec(memory_space=pltpu.VMEM)
SMEM = pl.BlockSpec(memory_space=pltpu.SMEM)
HBM = pl.BlockSpec(memory_space=pl.ANY)
PARAMS = pltpu.CompilerParams(vmem_limit_bytes=32 * 1024 * 1024)
PACK_PARAMS = pltpu.CompilerParams(vmem_limit_bytes=56 * 1024 * 1024)


def slot_of(chip, core):
    return chip ^ ((CHIPS - 1) * core)


def chip_at(slot, core):
    return slot ^ ((CHIPS - 1) * core)


def swap_sides(x):
    return pltpu.roll(x, SIDE, 1)


def left_side(rows):
    return lax.broadcasted_iota(jnp.int32, (rows, BLOCK), 1) < SIDE


def pack_kernel(ids, w_hbm, lw_hbm, ce_hbm, keep, send, drift, w, lw, ce, sems):
    core = ids[0]
    copies = [
        [
            pltpu.make_async_copy(src.at[mat], dst.at[mat], sems.at[kind, mat])
            for kind, (src, dst) in enumerate(((ce_hbm, ce), (w_hbm, w), (lw_hbm, lw)))
        ]
        for mat in range(MATS)
    ]
    for group in copies:
        for copy in group:
            copy.start()
    left = left_side(16)
    for block in range(BLOCKS, CHIPS):
        keep[slot_of(block, core)] = jnp.zeros((SHARE, BLOCK), jnp.float32)
        send[slot_of(block, 1 - core)] = jnp.zeros((SHARE, BLOCK), jnp.float32)
    for mat in range(MATS):
        for copy in copies[mat]:
            copy.wait()
        for block in range(BLOCKS):
            lanes = slice(block * BLOCK, (block + 1) * BLOCK)
            value = (
                w[mat, :, lanes].astype(jnp.float32)
                - lw[mat, :, lanes].astype(jnp.float32)
                + ce[mat, :, lanes]
            )
            drift[mat, :, lanes] = value
    for block in range(BLOCKS):
        lanes = slice(block * BLOCK, (block + 1) * BLOCK)
        keep[slot_of(block, core), 0:COLS] = drift[2 * core, :, lanes]
        send[slot_of(block, 1 - core), 0:COLS] = drift[2 - 2 * core, :, lanes]
        top, bottom = drift[1, 0:16, lanes], drift[1, 16:32, lanes]
        first = jnp.where(left, top, swap_sides(bottom))
        second = jnp.where(left, swap_sides(top), bottom)
        keep[slot_of(block, core), COLS:SHARE] = jnp.where(core == 0, first, second)
        send[slot_of(block, 1 - core), COLS:SHARE] = jnp.where(core == 0, second, first)


def outer(a, b):
    return lax.dot_general(
        a, b, (((1,), (1,)), ((), ())), precision=HIGHEST, preferred_element_type=jnp.float32
    )


def factor_kernel(ids, qt, got, inner, factor):
    core = ids[0]
    total = jnp.sum(got[...], axis=0)
    left = left_side(16)
    whole = total[0:COLS]
    half = total[COLS:SHARE]
    half = jnp.concatenate(
        [jnp.where(left, half, 0.0), jnp.where(left, swap_sides(half), 0.0)], axis=0
    )
    whole_factor = jnp.dot(
        qt[2 * core], whole, precision=HIGHEST, preferred_element_type=jnp.float32
    )
    half_factor = jnp.dot(qt[1], half, precision=HIGHEST, preferred_element_type=jnp.float32)
    factor[0:RANK] = whole_factor
    factor[RANK:FROWS] = half_factor[0:8] + swap_sides(half_factor[8:16])
    whole, half = outer(whole_factor, whole), outer(half_factor, half)
    inner[...] = jnp.concatenate([whole[0:8], whole[8:16], half[0:8], half[8:16]], axis=1)


def choose_kernel(ids, one, two, out):
    out[CHIPS * FROWS :] = jnp.sum(two[:, FROWS:GROWS], axis=0)
    for core, arrived in enumerate((two, one)):

        @pl.when(ids[0] == core)
        def _():
            for slot in range(CHIPS):
                out[slot * FROWS : slot * FROWS + FROWS] = arrived[slot, 0:FROWS]


def split(x):
    high = x.astype(jnp.bfloat16)
    rest = x - high.astype(jnp.float32)
    middle = rest.astype(jnp.bfloat16)
    return high, middle, (rest - middle.astype(jnp.float32)).astype(jnp.bfloat16)


def final_kernel(
    islands, ids, qt, own, sib, w, mom, drift,
    out_w, out_e, out_m, out_f, fac, buf_w, buf_e, buf_m, sems,
):
    first = ids[0] == 0

    rows = slice(CHIPS * FROWS, CHIPS * FROWS + MROWS)
    mine, other = own[rows], sib[rows]
    middle = pltpu.roll(mine + other, SIDE, 1)
    table = []
    for mat, rows in enumerate(
        (jnp.where(first, mine, other), middle, jnp.where(first, other, mine))
    ):
        rows = jnp.concatenate([rows[:, 0:COLS], rows[:, COLS : 2 * COLS]], axis=0)
        gram = outer(qt[mat], rows)
        rest = jnp.zeros((RANK, BLOCK - PAIR), jnp.float32)
        table.append(jnp.concatenate([gram, rows, rest], axis=1))
    table = jnp.stack(table)
    row = lax.broadcasted_iota(jnp.int32, table.shape, 1)
    small = table
    for step in range(RANK):
        spread = jnp.broadcast_to(table[:, :, step : step + 1], table.shape)
        pivot = spread[:, step : step + 1, :]
        line = table[:, step : step + 1, :]
        scaled = line * (1.0 / pivot)
        here = row == step
        small = jnp.where(here, line * lax.rsqrt(pivot), small)
        table = jnp.where(here, scaled, table - spread * scaled)

    left = left_side(8)
    for block in range(BLOCKS):
        lanes = slice(block * BLOCK, (block + 1) * BLOCK)
        mine = own[pl.ds(pl.multiple_of(slot_of(block, ids[0]) * FROWS, 8), FROWS)]
        other = sib[pl.ds(pl.multiple_of(slot_of(block, 1 - ids[0]) * FROWS, 8), FROWS)]
        low, high = jnp.where(first, mine, other), jnp.where(first, other, mine)
        low_half, high_half = low[RANK:FROWS], high[RANK:FROWS]
        half = jnp.concatenate(
            [
                jnp.where(left, low_half, swap_sides(high_half)),
                jnp.where(left, swap_sides(low_half), high_half),
            ],
            axis=0,
        )
        for mat, value in enumerate((low[0:RANK], half, high[0:RANK])):
            top, mid, last = split(value)
            for place, part in enumerate((top, mid, last, top, mid, top)):
                fac[mat, place * RANK : place * RANK + RANK, lanes] = part

    for mat in range(MATS):
        out_f[mat] = small[mat, :, RANK:PAIR] * (1.0 / islands)
        top, mid, last = split(table[mat, :, RANK:PAIR] * (1.0 / islands))
        parts = [x.astype(jnp.float32) for x in (top, top, top, mid, mid, last)]
        mixed = jnp.transpose(jnp.concatenate(parts, axis=0)).astype(jnp.bfloat16)
        for tile in range(7):
            lanes = slice(tile * 256, (tile + 1) * 256)
            approx = jnp.dot(mixed, fac[mat, :, lanes], preferred_element_type=jnp.float32)
            wide = w[mat, :, lanes].astype(jnp.float32)
            momentum = 0.9 * mom[mat, :, lanes] + approx
            buf_e[mat, :, lanes] = drift[mat, :, lanes] - approx
            buf_m[mat, :, lanes] = momentum
            buf_w[mat, :, lanes] = (wide - 0.7 * (approx + 0.9 * momentum)).astype(jnp.bfloat16)
        for kind, (buf, out) in enumerate(((buf_w, out_w), (buf_e, out_e), (buf_m, out_m))):
            pltpu.make_async_copy(buf.at[mat], out.at[mat], sems.at[kind, mat]).start()
    for mat in range(MATS):
        for kind, (buf, out) in enumerate(((buf_w, out_w), (buf_e, out_e), (buf_m, out_m))):
            pltpu.make_async_copy(buf.at[mat], out.at[mat], sems.at[kind, mat]).wait()


def sibling(x):
    return lax.ppermute(x, "replica", [(i, i ^ 1) for i in range(2 * CHIPS)])


def exchange_z(x):
    groups = [[2 * chip_at(slot, core) + core for slot in range(CHIPS)] for core in range(2)]
    return lax.all_to_all(x, "replica", 0, 0, axis_index_groups=groups, tiled=True)


def exchange_mixed(x, line_core):
    lines = [
        [(2 * chip_at(slot, line_core) + line_core) * 16 + place for slot in range(CHIPS)]
        for place in range(16)
    ]
    planes = [
        [(2 * chip + 1 - line_core) * 16 + place for place in range(16)] for chip in range(CHIPS)
    ]
    return lax.all_to_all(
        x, ("replica", "fsdp"), 0, 0, axis_index_groups=lines + planes, tiled=True
    )


def local(weights, local_weights, carried_error, momentum, initial_factor):
    f32 = jnp.float32
    ids = (lax.axis_index("replica") & 1).astype(jnp.int32).reshape(1)
    shape = (MATS, COLS, WIDTH)
    keep, send, drift = pl.pallas_call(
        pack_kernel,
        out_shape=[pltpu.VMEM((CHIPS, SHARE, BLOCK), f32)] * 2 + [pltpu.VMEM(shape, f32)],
        in_specs=[SMEM, HBM, HBM, HBM],
        out_specs=[VMEM] * 3,
        scratch_shapes=[
            pltpu.VMEM(shape, jnp.bfloat16),
            pltpu.VMEM(shape, jnp.bfloat16),
            pltpu.VMEM(shape, f32),
            pltpu.SemaphoreType.DMA((3, 3)),
        ],
        compiler_params=PACK_PARAMS,
        name="pack",
    )(ids, weights, local_weights[0], carried_error[0])
    qt = jnp.swapaxes(initial_factor, 1, 2)
    shares = exchange_z(keep + sibling(send))
    inner, factor = pl.pallas_call(
        factor_kernel,
        out_shape=[
            jax.ShapeDtypeStruct((MROWS, BLOCK), f32),
            jax.ShapeDtypeStruct((FROWS, BLOCK), f32),
        ],
        in_specs=[SMEM, VMEM, VMEM],
        out_specs=[VMEM, VMEM],
        compiler_params=PARAMS,
        name="factor",
    )(ids, qt, shares)

    arrivals = []
    for line_core in (1, 0):
        arrivals.append(
            exchange_mixed(
                jnp.broadcast_to(jnp.concatenate([factor, inner]), (CHIPS, GROWS, BLOCK)),
                line_core,
            )
        )
        inner = jnp.sum(arrivals[-1][:, FROWS:], axis=0)
    own = pl.pallas_call(
        choose_kernel,
        out_shape=pltpu.VMEM((CHIPS * FROWS + MROWS, BLOCK), f32),
        in_specs=[SMEM, VMEM, VMEM],
        out_specs=VMEM,
        compiler_params=PARAMS,
        name="choose",
    )(ids, *arrivals)
    sib = sibling(own)

    next_weights, next_error, next_momentum, following = pl.pallas_call(
        lambda *refs: final_kernel(lax.axis_size("replica"), *refs),
        out_shape=[
            jax.ShapeDtypeStruct(shape, jnp.bfloat16),
            jax.ShapeDtypeStruct(shape, f32),
            jax.ShapeDtypeStruct(shape, f32),
            jax.ShapeDtypeStruct((MATS, RANK, COLS), f32),
        ],
        in_specs=[SMEM] + [VMEM] * 6,
        out_specs=[HBM, HBM, HBM, VMEM],
        scratch_shapes=[
            pltpu.VMEM((MATS, 6 * RANK, WIDTH), jnp.bfloat16),
            pltpu.VMEM(shape, jnp.bfloat16),
            pltpu.VMEM(shape, f32),
            pltpu.VMEM(shape, f32),
            pltpu.SemaphoreType.DMA((3, 3)),
        ],
        compiler_params=PARAMS,
        name="final",
    )(ids, qt, own, sib, weights, momentum, drift)
    return (next_weights, next_error[None], next_momentum, jnp.swapaxes(following, 1, 2))


def solution(mesh):
    return jax.shard_map(
        local,
        mesh=mesh,
        in_specs=(
            P(None, None, "fsdp"),
            P("replica", None, None, "fsdp"),
            P("replica", None, None, "fsdp"),
            P(None, None, "fsdp"),
            P(),
        ),
        out_specs=(
            P(None, None, "fsdp"),
            P("replica", None, None, "fsdp"),
            P(None, None, "fsdp"),
            P(),
        ),
        check_vma=False,
    )
```

```python
import jax
import jax.numpy as jnp
from jax import lax
from jax.experimental import pallas as pl
from jax.experimental.pallas import tpu as pltpu
from jax.sharding import PartitionSpec as P

CHIPS = 16
BLOCK = 128
SIDE = BLOCK // 2
BLOCKS = 14
WIDTH = BLOCK * BLOCKS
MATS = 3
COLS = 32
RANK = 16
SHARE = MATS * COLS // 2
FROWS = SHARE // 2
MROWS = 8
GROWS = FROWS + MROWS
PAIR = RANK + COLS
HIGHEST = lax.Precision.HIGHEST
VMEM = pl.BlockSpec(memory_space=pltpu.VMEM)
SMEM = pl.BlockSpec(memory_space=pltpu.SMEM)
HBM = pl.BlockSpec(memory_space=pl.ANY)
PARAMS = pltpu.CompilerParams(vmem_limit_bytes=32 * 1024 * 1024)
PACK_PARAMS = pltpu.CompilerParams(vmem_limit_bytes=56 * 1024 * 1024)


def slot_of(chip, core):
    return chip ^ ((CHIPS - 1) * core)


def chip_at(slot, core):
    return slot ^ ((CHIPS - 1) * core)


def swap_sides(x):
    return pltpu.roll(x, SIDE, 1)


def left_side(rows):
    return lax.broadcasted_iota(jnp.int32, (rows, BLOCK), 1) < SIDE


def pack_kernel(ids, w_hbm, lw_hbm, ce_hbm, keep, send, drift, w, lw, ce, sems):
    core = ids[0]
    copies = [
        [
            pltpu.make_async_copy(src.at[mat], dst.at[mat], sems.at[kind, mat])
            for kind, (src, dst) in enumerate(((ce_hbm, ce), (w_hbm, w), (lw_hbm, lw)))
        ]
        for mat in range(MATS)
    ]
    for group in copies:
        for copy in group:
            copy.start()
    left = left_side(16)
    for block in range(BLOCKS, CHIPS):
        keep[slot_of(block, core)] = jnp.zeros((SHARE, BLOCK), jnp.float32)
        send[slot_of(block, 1 - core)] = jnp.zeros((SHARE, BLOCK), jnp.float32)
    for mat in range(MATS):
        for copy in copies[mat]:
            copy.wait()
        for block in range(BLOCKS):
            lanes = slice(block * BLOCK, (block + 1) * BLOCK)
            value = (
                w[mat, :, lanes].astype(jnp.float32)
                - lw[mat, :, lanes].astype(jnp.float32)
                + ce[mat, :, lanes]
            )
            drift[mat, :, lanes] = value
    for block in range(BLOCKS):
        lanes = slice(block * BLOCK, (block + 1) * BLOCK)
        keep[slot_of(block, core), 0:COLS] = drift[2 * core, :, lanes]
        send[slot_of(block, 1 - core), 0:COLS] = drift[2 - 2 * core, :, lanes]
        top, bottom = drift[1, 0:16, lanes], drift[1, 16:32, lanes]
        first = jnp.where(left, top, swap_sides(bottom))
        second = jnp.where(left, swap_sides(top), bottom)
        keep[slot_of(block, core), COLS:SHARE] = jnp.where(core == 0, first, second)
        send[slot_of(block, 1 - core), COLS:SHARE] = jnp.where(core == 0, second, first)


def outer(a, b):
    return lax.dot_general(
        a, b, (((1,), (1,)), ((), ())), precision=HIGHEST, preferred_element_type=jnp.float32
    )


def factor_kernel(ids, qt, got, inner, factor):
    core = ids[0]
    total = jnp.sum(got[...], axis=0)
    left = left_side(16)
    whole = total[0:COLS]
    half = total[COLS:SHARE]
    half = jnp.concatenate(
        [jnp.where(left, half, 0.0), jnp.where(left, swap_sides(half), 0.0)], axis=0
    )
    whole_factor = jnp.dot(
        qt[2 * core], whole, precision=HIGHEST, preferred_element_type=jnp.float32
    )
    half_factor = jnp.dot(qt[1], half, precision=HIGHEST, preferred_element_type=jnp.float32)
    factor[0:RANK] = whole_factor
    factor[RANK:FROWS] = half_factor[0:8] + swap_sides(half_factor[8:16])
    whole, half = outer(whole_factor, whole), outer(half_factor, half)
    inner[...] = jnp.concatenate([whole[0:8], whole[8:16], half[0:8], half[8:16]], axis=1)


def choose_kernel(ids, one, two, out):
    out[CHIPS * FROWS :] = jnp.sum(two[:, FROWS:GROWS], axis=0)
    for core, arrived in enumerate((one, two)):

        @pl.when(ids[0] == core)
        def _():
            for slot in range(CHIPS):
                out[slot * FROWS : slot * FROWS + FROWS] = arrived[slot, 0:FROWS]


def split(x):
    high = x.astype(jnp.bfloat16)
    rest = x - high.astype(jnp.float32)
    middle = rest.astype(jnp.bfloat16)
    return high, middle, (rest - middle.astype(jnp.float32)).astype(jnp.bfloat16)


def final_kernel(
    islands, ids, qt, own, sib, w, mom, drift,
    out_w, out_e, out_m, out_f, fac, buf_w, buf_e, buf_m, sems,
):
    first = ids[0] == 0

    rows = slice(CHIPS * FROWS, CHIPS * FROWS + MROWS)
    mine, other = own[rows], sib[rows]
    middle = pltpu.roll(mine + other, SIDE, 1)
    table = []
    for mat, rows in enumerate(
        (jnp.where(first, mine, other), middle, jnp.where(first, other, mine))
    ):
        rows = jnp.concatenate([rows[:, 0:COLS], rows[:, COLS : 2 * COLS]], axis=0)
        gram = outer(qt[mat], rows)
        rest = jnp.zeros((RANK, BLOCK - PAIR), jnp.float32)
        table.append(jnp.concatenate([gram, rows, rest], axis=1))
    table = jnp.stack(table)
    row = lax.broadcasted_iota(jnp.int32, table.shape, 1)
    small = table
    for step in range(RANK):
        spread = jnp.broadcast_to(table[:, :, step : step + 1], table.shape)
        pivot = spread[:, step : step + 1, :]
        line = table[:, step : step + 1, :]
        scaled = line * (1.0 / pivot)
        here = row == step
        small = jnp.where(here, line * lax.rsqrt(pivot), small)
        table = jnp.where(here, scaled, table - spread * scaled)

    left = left_side(8)
    for block in range(BLOCKS):
        lanes = slice(block * BLOCK, (block + 1) * BLOCK)
        mine = own[pl.ds(pl.multiple_of(slot_of(block, ids[0]) * FROWS, 8), FROWS)]
        other = sib[pl.ds(pl.multiple_of(slot_of(block, 1 - ids[0]) * FROWS, 8), FROWS)]
        low, high = jnp.where(first, mine, other), jnp.where(first, other, mine)
        low_half, high_half = low[RANK:FROWS], high[RANK:FROWS]
        half = jnp.concatenate(
            [
                jnp.where(left, low_half, swap_sides(high_half)),
                jnp.where(left, swap_sides(low_half), high_half),
            ],
            axis=0,
        )
        for mat, value in enumerate((low[0:RANK], half, high[0:RANK])):
            top, mid, last = split(value)
            for place, part in enumerate((top, mid, last, top, mid, top)):
                fac[mat, place * RANK : place * RANK + RANK, lanes] = part

    for mat in range(MATS):
        out_f[mat] = small[mat, :, RANK:PAIR] * (1.0 / islands)
        top, mid, last = split(table[mat, :, RANK:PAIR] * (1.0 / islands))
        parts = [x.astype(jnp.float32) for x in (top, top, top, mid, mid, last)]
        mixed = jnp.transpose(jnp.concatenate(parts, axis=0)).astype(jnp.bfloat16)
        for tile in range(7):
            lanes = slice(tile * 256, (tile + 1) * 256)
            approx = jnp.dot(mixed, fac[mat, :, lanes], preferred_element_type=jnp.float32)
            wide = w[mat, :, lanes].astype(jnp.float32)
            momentum = 0.9 * mom[mat, :, lanes] + approx
            buf_e[mat, :, lanes] = drift[mat, :, lanes] - approx
            buf_m[mat, :, lanes] = momentum
            buf_w[mat, :, lanes] = (wide - 0.7 * (approx + 0.9 * momentum)).astype(jnp.bfloat16)
        for kind, (buf, out) in enumerate(((buf_w, out_w), (buf_e, out_e), (buf_m, out_m))):
            pltpu.make_async_copy(buf.at[mat], out.at[mat], sems.at[kind, mat]).start()
    for mat in range(MATS):
        for kind, (buf, out) in enumerate(((buf_w, out_w), (buf_e, out_e), (buf_m, out_m))):
            pltpu.make_async_copy(buf.at[mat], out.at[mat], sems.at[kind, mat]).wait()


def sibling(x):
    return lax.ppermute(x, "replica", [(i, i ^ 1) for i in range(2 * CHIPS)])


def exchange_z(x):
    groups = [[2 * chip_at(slot, core) + core for slot in range(CHIPS)] for core in range(2)]
    return lax.all_to_all(x, "replica", 0, 0, axis_index_groups=groups, tiled=True)


def exchange_mixed(x, line_core):
    lines = [
        [(2 * chip_at(slot, line_core) + line_core) * 16 + place for slot in range(CHIPS)]
        for place in range(16)
    ]
    planes = [
        [(2 * chip + 1 - line_core) * 16 + place for place in range(16)] for chip in range(CHIPS)
    ]
    return lax.all_to_all(
        x, ("replica", "fsdp"), 0, 0, axis_index_groups=lines + planes, tiled=True
    )


def local(weights, local_weights, carried_error, momentum, initial_factor):
    f32 = jnp.float32
    ids = (lax.axis_index("replica") & 1).astype(jnp.int32).reshape(1)
    shape = (MATS, COLS, WIDTH)
    keep, send, drift = pl.pallas_call(
        pack_kernel,
        out_shape=[pltpu.VMEM((CHIPS, SHARE, BLOCK), f32)] * 2 + [pltpu.VMEM(shape, f32)],
        in_specs=[SMEM, HBM, HBM, HBM],
        out_specs=[VMEM] * 3,
        scratch_shapes=[
            pltpu.VMEM(shape, jnp.bfloat16),
            pltpu.VMEM(shape, jnp.bfloat16),
            pltpu.VMEM(shape, f32),
            pltpu.SemaphoreType.DMA((3, 3)),
        ],
        compiler_params=PACK_PARAMS,
        name="pack",
    )(ids, weights, local_weights[0], carried_error[0])
    qt = jnp.swapaxes(initial_factor, 1, 2)
    shares = exchange_z(keep + sibling(send))
    inner, factor = pl.pallas_call(
        factor_kernel,
        out_shape=[
            jax.ShapeDtypeStruct((MROWS, BLOCK), f32),
            jax.ShapeDtypeStruct((FROWS, BLOCK), f32),
        ],
        in_specs=[SMEM, VMEM, VMEM],
        out_specs=[VMEM, VMEM],
        compiler_params=PARAMS,
        name="factor",
    )(ids, qt, shares)

    arrivals = []
    for line_core in (0, 1):
        arrivals.append(
            exchange_mixed(
                jnp.broadcast_to(jnp.concatenate([factor, inner]), (CHIPS, GROWS, BLOCK)),
                line_core,
            )
        )
        inner = jnp.sum(arrivals[-1][:, FROWS:], axis=0)
    own = pl.pallas_call(
        choose_kernel,
        out_shape=pltpu.VMEM((CHIPS * FROWS + MROWS, BLOCK), f32),
        in_specs=[SMEM, VMEM, VMEM],
        out_specs=VMEM,
        compiler_params=PARAMS,
        name="choose",
    )(ids, *arrivals)
    sib = sibling(own)

    next_weights, next_error, next_momentum, following = pl.pallas_call(
        lambda *refs: final_kernel(lax.axis_size("replica"), *refs),
        out_shape=[
            jax.ShapeDtypeStruct(shape, jnp.bfloat16),
            jax.ShapeDtypeStruct(shape, f32),
            jax.ShapeDtypeStruct(shape, f32),
            jax.ShapeDtypeStruct((MATS, RANK, COLS), f32),
        ],
        in_specs=[SMEM] + [VMEM] * 6,
        out_specs=[HBM, HBM, HBM, VMEM],
        scratch_shapes=[
            pltpu.VMEM((MATS, 6 * RANK, WIDTH), jnp.bfloat16),
            pltpu.VMEM(shape, jnp.bfloat16),
            pltpu.VMEM(shape, f32),
            pltpu.VMEM(shape, f32),
            pltpu.SemaphoreType.DMA((3, 3)),
        ],
        compiler_params=PARAMS,
        name="final",
    )(ids, qt, own, sib, weights, momentum, drift)
    return (next_weights, next_error[None], next_momentum, jnp.swapaxes(following, 1, 2))


def solution(mesh):
    return jax.shard_map(
        local,
        mesh=mesh,
        in_specs=(
            P(None, None, "fsdp"),
            P("replica", None, None, "fsdp"),
            P("replica", None, None, "fsdp"),
            P(None, None, "fsdp"),
            P(),
        ),
        out_specs=(
            P(None, None, "fsdp"),
            P("replica", None, None, "fsdp"),
            P(None, None, "fsdp"),
            P(),
        ),
        check_vma=False,
    )
```

```python
import jax
import jax.numpy as jnp
from jax import lax
from jax.experimental import pallas as pl
from jax.experimental.pallas import tpu as pltpu
from jax.sharding import PartitionSpec as P

CHIPS = 16
BLOCK = 128
SIDE = BLOCK // 2
BLOCKS = 14
WIDTH = BLOCK * BLOCKS
MATS = 3
COLS = 32
RANK = 16
SHARE = MATS * COLS // 2
FROWS = SHARE // 2
MROWS = 8
GROWS = FROWS + MROWS
PAIR = RANK + COLS
HIGHEST = lax.Precision.HIGHEST
VMEM = pl.BlockSpec(memory_space=pltpu.VMEM)
SMEM = pl.BlockSpec(memory_space=pltpu.SMEM)
HBM = pl.BlockSpec(memory_space=pl.ANY)
PARAMS = pltpu.CompilerParams(vmem_limit_bytes=32 * 1024 * 1024)
PACK_PARAMS = pltpu.CompilerParams(vmem_limit_bytes=56 * 1024 * 1024)


def slot_of(chip, core):
    return chip ^ ((CHIPS - 1) * core)


def chip_at(slot, core):
    return slot ^ ((CHIPS - 1) * core)


def swap_sides(x):
    return pltpu.roll(x, SIDE, 1)


def left_side(rows):
    return lax.broadcasted_iota(jnp.int32, (rows, BLOCK), 1) < SIDE


def pack_kernel(ids, w_hbm, lw_hbm, ce_hbm, keep, send, drift, w, lw, ce, sems):
    core = ids[0]
    copies = [
        [
            pltpu.make_async_copy(src.at[mat], dst.at[mat], sems.at[kind, mat])
            for kind, (src, dst) in enumerate(((ce_hbm, ce), (w_hbm, w), (lw_hbm, lw)))
        ]
        for mat in range(MATS)
    ]
    for group in copies:
        for copy in group:
            copy.start()
    left = left_side(16)
    for block in range(BLOCKS, CHIPS):
        keep[slot_of(block, core)] = jnp.zeros((SHARE, BLOCK), jnp.float32)
        send[slot_of(block, 1 - core)] = jnp.zeros((SHARE, BLOCK), jnp.float32)
    for mat in range(MATS):
        for copy in copies[mat]:
            copy.wait()
        for block in range(BLOCKS):
            lanes = slice(block * BLOCK, (block + 1) * BLOCK)
            value = (
                w[mat, :, lanes].astype(jnp.float32)
                - lw[mat, :, lanes].astype(jnp.float32)
                + ce[mat, :, lanes]
            )
            drift[mat, :, lanes] = value
    for block in range(BLOCKS):
        lanes = slice(block * BLOCK, (block + 1) * BLOCK)
        keep[slot_of(block, core), 0:COLS] = drift[2 * core, :, lanes]
        send[slot_of(block, 1 - core), 0:COLS] = drift[2 - 2 * core, :, lanes]
        top, bottom = drift[1, 0:16, lanes], drift[1, 16:32, lanes]
        first = jnp.where(left, top, swap_sides(bottom))
        second = jnp.where(left, swap_sides(top), bottom)
        keep[slot_of(block, core), COLS:SHARE] = jnp.where(core == 0, first, second)
        send[slot_of(block, 1 - core), COLS:SHARE] = jnp.where(core == 0, second, first)


def outer(a, b):
    return lax.dot_general(
        a, b, (((1,), (1,)), ((), ())), precision=HIGHEST, preferred_element_type=jnp.float32
    )


def factor_kernel(ids, qt, got, inner, factor):
    core = ids[0]
    total = jnp.sum(got[...], axis=0)
    left = left_side(16)
    whole = total[0:COLS]
    half = total[COLS:SHARE]
    half = jnp.concatenate(
        [jnp.where(left, half, 0.0), jnp.where(left, swap_sides(half), 0.0)], axis=0
    )
    whole_factor = jnp.dot(
        qt[2 * core], whole, precision=HIGHEST, preferred_element_type=jnp.float32
    )
    half_factor = jnp.dot(qt[1], half, precision=HIGHEST, preferred_element_type=jnp.float32)
    factor[0:RANK] = whole_factor
    factor[RANK:FROWS] = half_factor[0:8] + swap_sides(half_factor[8:16])
    whole, half = outer(whole_factor, whole), outer(half_factor, half)
    inner[...] = jnp.concatenate([whole[0:8], whole[8:16], half[0:8], half[8:16]], axis=1)


def choose_kernel(ids, one, two, out):
    out[CHIPS * FROWS :] = jnp.sum(two[:, FROWS:GROWS], axis=0)
    for core, arrived in enumerate((one, two)):

        @pl.when(ids[0] == core)
        def _():
            for slot in range(CHIPS):
                out[slot * FROWS : slot * FROWS + FROWS] = arrived[slot, 0:FROWS]


def split(x):
    high = x.astype(jnp.bfloat16)
    rest = x - high.astype(jnp.float32)
    middle = rest.astype(jnp.bfloat16)
    return high, middle, (rest - middle.astype(jnp.float32)).astype(jnp.bfloat16)


def final_kernel(
    islands, ids, qt, own, sib, w, mom, drift,
    out_w, out_e, out_m, out_f, fac, buf_w, buf_e, buf_m, sems,
):
    first = ids[0] == 0

    rows = slice(CHIPS * FROWS, CHIPS * FROWS + MROWS)
    mine, other = own[rows], sib[rows]
    middle = pltpu.roll(mine + other, SIDE, 1)
    table = []
    for mat, rows in enumerate(
        (jnp.where(first, mine, other), middle, jnp.where(first, other, mine))
    ):
        rows = jnp.concatenate([rows[:, 0:COLS], rows[:, COLS : 2 * COLS]], axis=0)
        gram = outer(qt[mat], rows)
        rest = jnp.zeros((RANK, BLOCK - PAIR), jnp.float32)
        table.append(jnp.concatenate([gram, rows, rest], axis=1))
    table = jnp.stack(table)
    row = lax.broadcasted_iota(jnp.int32, table.shape, 1)
    small = table
    for step in range(0, RANK, 2):
        one = jnp.broadcast_to(table[:, :, step : step + 1], table.shape)
        two = jnp.broadcast_to(table[:, :, step + 1 : step + 2], table.shape)
        line = table[:, step : step + 1, :]
        pivot, cross = one[:, step : step + 1, :], two[:, step : step + 1, :]
        inverse = 1.0 / pivot
        ratio = one[:, step + 1 : step + 2, :] * inverse
        next_line = table[:, step + 1 : step + 2, :] - ratio * line
        next_pivot = two[:, step + 1 : step + 2, :] - ratio * cross
        next_scaled = next_line * (1.0 / next_pivot)
        scaled = (line - cross * next_scaled) * inverse
        here, below = row == step, row == step + 1
        small = jnp.where(here, line * lax.rsqrt(pivot), small)
        small = jnp.where(below, next_line * lax.rsqrt(next_pivot), small)
        rest = table - one * scaled - two * next_scaled
        table = jnp.where(here, scaled, jnp.where(below, next_scaled, rest))

    left = left_side(8)
    for block in range(BLOCKS):
        lanes = slice(block * BLOCK, (block + 1) * BLOCK)
        rows = slice(block * FROWS, block * FROWS + FROWS)
        mine, other = own[rows], sib[rows]
        low, high = jnp.where(first, mine, other), jnp.where(first, other, mine)
        low_half, high_half = low[RANK:FROWS], high[RANK:FROWS]
        half = jnp.concatenate(
            [
                jnp.where(left, low_half, swap_sides(high_half)),
                jnp.where(left, swap_sides(low_half), high_half),
            ],
            axis=0,
        )
        for mat, value in enumerate((low[0:RANK], half, high[0:RANK])):
            top, mid, last = split(value)
            for place, part in enumerate((top, mid, last, top, mid, top)):
                fac[mat, place * RANK : place * RANK + RANK, lanes] = part

    for mat in range(MATS):
        out_f[mat] = small[mat, :, RANK:PAIR] * (1.0 / islands)
        top, mid, last = split(table[mat, :, RANK:PAIR] * (1.0 / islands))
        parts = [x.astype(jnp.float32) for x in (top, top, top, mid, mid, last)]
        mixed = jnp.transpose(jnp.concatenate(parts, axis=0)).astype(jnp.bfloat16)
        for tile in range(7):
            lanes = slice(tile * 256, (tile + 1) * 256)
            approx = jnp.dot(mixed, fac[mat, :, lanes], preferred_element_type=jnp.float32)
            wide = w[mat, :, lanes].astype(jnp.float32)
            momentum = 0.9 * mom[mat, :, lanes] + approx
            buf_e[mat, :, lanes] = drift[mat, :, lanes] - approx
            buf_m[mat, :, lanes] = momentum
            buf_w[mat, :, lanes] = (wide - 0.7 * (approx + 0.9 * momentum)).astype(jnp.bfloat16)
        for kind, (buf, out) in enumerate(((buf_w, out_w), (buf_e, out_e), (buf_m, out_m))):
            pltpu.make_async_copy(buf.at[mat], out.at[mat], sems.at[kind, mat]).start()
    for mat in range(MATS):
        for kind, (buf, out) in enumerate(((buf_w, out_w), (buf_e, out_e), (buf_m, out_m))):
            pltpu.make_async_copy(buf.at[mat], out.at[mat], sems.at[kind, mat]).wait()


def sibling(x):
    return lax.ppermute(x, "replica", [(i, i ^ 1) for i in range(2 * CHIPS)])


def exchange_z(x):
    groups = [[2 * chip_at(slot, core) + core for slot in range(CHIPS)] for core in range(2)]
    return lax.all_to_all(x, "replica", 0, 0, axis_index_groups=groups, tiled=True)


def exchange_mixed(x, line_core):
    lines = [
        [(2 * chip + line_core) * 16 + place for chip in range(CHIPS)]
        for place in range(16)
    ]
    planes = [
        [(2 * chip + 1 - line_core) * 16 + place for place in range(16)] for chip in range(CHIPS)
    ]
    return lax.all_to_all(
        x, ("replica", "fsdp"), 0, 0, axis_index_groups=lines + planes, tiled=True
    )


def local(weights, local_weights, carried_error, momentum, initial_factor):
    f32 = jnp.float32
    ids = (lax.axis_index("replica") & 1).astype(jnp.int32).reshape(1)
    shape = (MATS, COLS, WIDTH)
    keep, send, drift = pl.pallas_call(
        pack_kernel,
        out_shape=[pltpu.VMEM((CHIPS, SHARE, BLOCK), f32)] * 2 + [pltpu.VMEM(shape, f32)],
        in_specs=[SMEM, HBM, HBM, HBM],
        out_specs=[VMEM] * 3,
        scratch_shapes=[
            pltpu.VMEM(shape, jnp.bfloat16),
            pltpu.VMEM(shape, jnp.bfloat16),
            pltpu.VMEM(shape, f32),
            pltpu.SemaphoreType.DMA((3, 3)),
        ],
        compiler_params=PACK_PARAMS,
        name="pack",
    )(ids, weights, local_weights[0], carried_error[0])
    qt = jnp.swapaxes(initial_factor, 1, 2)
    shares = exchange_z(keep + sibling(send))
    inner, factor = pl.pallas_call(
        factor_kernel,
        out_shape=[
            jax.ShapeDtypeStruct((MROWS, BLOCK), f32),
            jax.ShapeDtypeStruct((FROWS, BLOCK), f32),
        ],
        in_specs=[SMEM, VMEM, VMEM],
        out_specs=[VMEM, VMEM],
        compiler_params=PARAMS,
        name="factor",
    )(ids, qt, shares)

    arrivals = []
    for line_core in (0, 1):
        arrivals.append(
            exchange_mixed(
                jnp.broadcast_to(jnp.concatenate([factor, inner]), (CHIPS, GROWS, BLOCK)),
                line_core,
            )
        )
        inner = jnp.sum(arrivals[-1][:, FROWS:], axis=0)
    own = pl.pallas_call(
        choose_kernel,
        out_shape=pltpu.VMEM((CHIPS * FROWS + MROWS, BLOCK), f32),
        in_specs=[SMEM, VMEM, VMEM],
        out_specs=VMEM,
        compiler_params=PARAMS,
        name="choose",
    )(ids, *arrivals)
    sib = sibling(own)

    next_weights, next_error, next_momentum, following = pl.pallas_call(
        lambda *refs: final_kernel(lax.axis_size("replica"), *refs),
        out_shape=[
            jax.ShapeDtypeStruct(shape, jnp.bfloat16),
            jax.ShapeDtypeStruct(shape, f32),
            jax.ShapeDtypeStruct(shape, f32),
            jax.ShapeDtypeStruct((MATS, RANK, COLS), f32),
        ],
        in_specs=[SMEM] + [VMEM] * 6,
        out_specs=[HBM, HBM, HBM, VMEM],
        scratch_shapes=[
            pltpu.VMEM((MATS, 6 * RANK, WIDTH), jnp.bfloat16),
            pltpu.VMEM(shape, jnp.bfloat16),
            pltpu.VMEM(shape, f32),
            pltpu.VMEM(shape, f32),
            pltpu.SemaphoreType.DMA((3, 3)),
        ],
        compiler_params=PARAMS,
        name="final",
    )(ids, qt, own, sib, weights, momentum, drift)
    return (next_weights, next_error[None], next_momentum, jnp.swapaxes(following, 1, 2))


def solution(mesh):
    return jax.shard_map(
        local,
        mesh=mesh,
        in_specs=(
            P(None, None, "fsdp"),
            P("replica", None, None, "fsdp"),
            P("replica", None, None, "fsdp"),
            P(None, None, "fsdp"),
            P(),
        ),
        out_specs=(
            P(None, None, "fsdp"),
            P("replica", None, None, "fsdp"),
            P(None, None, "fsdp"),
            P(),
        ),
        check_vma=False,
    )
```

```python
import jax
import jax.numpy as jnp
from jax import lax
from jax.experimental import pallas as pl
from jax.experimental.pallas import tpu as pltpu
from jax.sharding import PartitionSpec as P

CHIPS = 16
BLOCK = 128
SIDE = BLOCK // 2
BLOCKS = 14
WIDTH = BLOCK * BLOCKS
MATS = 3
COLS = 32
RANK = 16
SHARE = MATS * COLS // 2
FROWS = SHARE // 2
MROWS = 8
GROWS = FROWS + MROWS
PAIR = RANK + COLS
HIGHEST = lax.Precision.HIGHEST
VMEM = pl.BlockSpec(memory_space=pltpu.VMEM)
SMEM = pl.BlockSpec(memory_space=pltpu.SMEM)
HBM = pl.BlockSpec(memory_space=pl.ANY)
PARAMS = pltpu.CompilerParams(vmem_limit_bytes=32 * 1024 * 1024)
PACK_PARAMS = pltpu.CompilerParams(vmem_limit_bytes=56 * 1024 * 1024)


def slot_of(chip, core):
    return ((13 * (chip - 3)) & 15) ^ (8 * core)


def chip_at(slot, core):
    return (3 + 8 * core + 5 * slot) % CHIPS


def gather_slot(chip):
    return (9 * chip) % CHIPS


def swap_sides(x):
    return pltpu.roll(x, SIDE, 1)


def left_side(rows):
    return lax.broadcasted_iota(jnp.int32, (rows, BLOCK), 1) < SIDE


def pack_kernel(ids, w_hbm, lw_hbm, ce_hbm, keep, send, drift, w, lw, ce, sems):
    core = ids[0]
    copies = [
        [
            pltpu.make_async_copy(src.at[mat], dst.at[mat], sems.at[kind, mat])
            for kind, (src, dst) in enumerate(((ce_hbm, ce), (w_hbm, w), (lw_hbm, lw)))
        ]
        for mat in range(MATS)
    ]
    for group in copies:
        for copy in group:
            copy.start()
    left = left_side(16)
    for block in range(BLOCKS, CHIPS):
        keep[slot_of(block, core)] = jnp.zeros((SHARE, BLOCK), jnp.float32)
        send[slot_of(block, 1 - core)] = jnp.zeros((SHARE, BLOCK), jnp.float32)
    for mat in range(MATS):
        for copy in copies[mat]:
            copy.wait()
        for block in range(BLOCKS):
            lanes = slice(block * BLOCK, (block + 1) * BLOCK)
            value = (
                w[mat, :, lanes].astype(jnp.float32)
                - lw[mat, :, lanes].astype(jnp.float32)
                + ce[mat, :, lanes]
            )
            drift[mat, :, lanes] = value
    for block in range(BLOCKS):
        lanes = slice(block * BLOCK, (block + 1) * BLOCK)
        keep[slot_of(block, core), 0:COLS] = drift[2 * core, :, lanes]
        send[slot_of(block, 1 - core), 0:COLS] = drift[2 - 2 * core, :, lanes]
        top, bottom = drift[1, 0:16, lanes], drift[1, 16:32, lanes]
        first = jnp.where(left, top, swap_sides(bottom))
        second = jnp.where(left, swap_sides(top), bottom)
        keep[slot_of(block, core), COLS:SHARE] = jnp.where(core == 0, first, second)
        send[slot_of(block, 1 - core), COLS:SHARE] = jnp.where(core == 0, second, first)


def outer(a, b):
    return lax.dot_general(
        a, b, (((1,), (1,)), ((), ())), precision=HIGHEST, preferred_element_type=jnp.float32
    )


def factor_kernel(ids, qt, got, inner, factor):
    core = ids[0]
    total = jnp.sum(got[...], axis=0)
    left = left_side(16)
    whole = total[0:COLS]
    half = total[COLS:SHARE]
    half = jnp.concatenate(
        [jnp.where(left, half, 0.0), jnp.where(left, swap_sides(half), 0.0)], axis=0
    )
    whole_factor = jnp.dot(
        qt[2 * core], whole, precision=HIGHEST, preferred_element_type=jnp.float32
    )
    half_factor = jnp.dot(qt[1], half, precision=HIGHEST, preferred_element_type=jnp.float32)
    factor[0:RANK] = whole_factor
    factor[RANK:FROWS] = half_factor[0:8] + swap_sides(half_factor[8:16])
    whole, half = outer(whole_factor, whole), outer(half_factor, half)
    inner[...] = jnp.concatenate([whole[0:8], whole[8:16], half[0:8], half[8:16]], axis=1)


def choose_kernel(ids, one, two, out):
    out[CHIPS * FROWS :] = jnp.sum(two[:, FROWS:GROWS], axis=0)
    for core, arrived in enumerate((one, two)):

        @pl.when(ids[0] == core)
        def _():
            for slot in range(CHIPS):
                out[slot * FROWS : slot * FROWS + FROWS] = arrived[slot, 0:FROWS]


def split(x):
    high = x.astype(jnp.bfloat16)
    rest = x - high.astype(jnp.float32)
    middle = rest.astype(jnp.bfloat16)
    return high, middle, (rest - middle.astype(jnp.float32)).astype(jnp.bfloat16)


def final_kernel(
    islands, ids, qt, own, sib, w, mom, drift,
    out_w, out_e, out_m, out_f, fac, buf_w, buf_e, buf_m, sems,
):
    first = ids[0] == 0

    rows = slice(CHIPS * FROWS, CHIPS * FROWS + MROWS)
    mine, other = own[rows], sib[rows]
    middle = pltpu.roll(mine + other, SIDE, 1)
    table = []
    for mat, rows in enumerate(
        (jnp.where(first, mine, other), middle, jnp.where(first, other, mine))
    ):
        rows = jnp.concatenate([rows[:, 0:COLS], rows[:, COLS : 2 * COLS]], axis=0)
        gram = outer(qt[mat], rows)
        rest = jnp.zeros((RANK, BLOCK - PAIR), jnp.float32)
        table.append(jnp.concatenate([gram, rows, rest], axis=1))
    table = jnp.stack(table)
    row = lax.broadcasted_iota(jnp.int32, table.shape, 1)
    small = table
    for step in range(0, RANK, 2):
        one = jnp.broadcast_to(table[:, :, step : step + 1], table.shape)
        two = jnp.broadcast_to(table[:, :, step + 1 : step + 2], table.shape)
        line = table[:, step : step + 1, :]
        pivot, cross = one[:, step : step + 1, :], two[:, step : step + 1, :]
        inverse = 1.0 / pivot
        ratio = one[:, step + 1 : step + 2, :] * inverse
        next_line = table[:, step + 1 : step + 2, :] - ratio * line
        next_pivot = two[:, step + 1 : step + 2, :] - ratio * cross
        next_scaled = next_line * (1.0 / next_pivot)
        scaled = (line - cross * next_scaled) * inverse
        here, below = row == step, row == step + 1
        small = jnp.where(here, line * lax.rsqrt(pivot), small)
        small = jnp.where(below, next_line * lax.rsqrt(next_pivot), small)
        rest = table - one * scaled - two * next_scaled
        table = jnp.where(here, scaled, jnp.where(below, next_scaled, rest))

    left = left_side(8)
    for block in range(BLOCKS):
        lanes = slice(block * BLOCK, (block + 1) * BLOCK)
        start = gather_slot(block) * FROWS
        mine, other = own[start : start + FROWS], sib[start : start + FROWS]
        low, high = jnp.where(first, mine, other), jnp.where(first, other, mine)
        low_half, high_half = low[RANK:FROWS], high[RANK:FROWS]
        half = jnp.concatenate(
            [
                jnp.where(left, low_half, swap_sides(high_half)),
                jnp.where(left, swap_sides(low_half), high_half),
            ],
            axis=0,
        )
        for mat, value in enumerate((low[0:RANK], half, high[0:RANK])):
            top, mid, last = split(value)
            for place, part in enumerate((top, mid, last, top, mid, top)):
                fac[mat, place * RANK : place * RANK + RANK, lanes] = part

    for mat in range(MATS):
        out_f[mat] = small[mat, :, RANK:PAIR] * (1.0 / islands)
        top, mid, last = split(table[mat, :, RANK:PAIR] * (1.0 / islands))
        parts = [x.astype(jnp.float32) for x in (top, top, top, mid, mid, last)]
        mixed = jnp.transpose(jnp.concatenate(parts, axis=0)).astype(jnp.bfloat16)
        for tile in range(7):
            lanes = slice(tile * 256, (tile + 1) * 256)
            approx = jnp.dot(mixed, fac[mat, :, lanes], preferred_element_type=jnp.float32)
            wide = w[mat, :, lanes].astype(jnp.float32)
            momentum = 0.9 * mom[mat, :, lanes] + approx
            buf_e[mat, :, lanes] = drift[mat, :, lanes] - approx
            buf_m[mat, :, lanes] = momentum
            buf_w[mat, :, lanes] = (wide - 0.7 * (approx + 0.9 * momentum)).astype(jnp.bfloat16)
        for kind, (buf, out) in enumerate(((buf_w, out_w), (buf_e, out_e), (buf_m, out_m))):
            pltpu.make_async_copy(buf.at[mat], out.at[mat], sems.at[kind, mat]).start()
    for mat in range(MATS):
        for kind, (buf, out) in enumerate(((buf_w, out_w), (buf_e, out_e), (buf_m, out_m))):
            pltpu.make_async_copy(buf.at[mat], out.at[mat], sems.at[kind, mat]).wait()


def sibling(x):
    return lax.ppermute(x, "replica", [(i, i ^ 1) for i in range(2 * CHIPS)])


def exchange_z(x):
    groups = [[2 * chip_at(slot, core) + core for slot in range(CHIPS)] for core in range(2)]
    return lax.all_to_all(x, "replica", 0, 0, axis_index_groups=groups, tiled=True)


def exchange_mixed(x, line_core):
    lines = [
        [(2 * gather_slot(slot) + line_core) * 16 + place for slot in range(CHIPS)]
        for place in range(16)
    ]
    planes = [
        [(2 * chip + 1 - line_core) * 16 + place for place in range(16)] for chip in range(CHIPS)
    ]
    return lax.all_to_all(
        x, ("replica", "fsdp"), 0, 0, axis_index_groups=lines + planes, tiled=True
    )


def local(weights, local_weights, carried_error, momentum, initial_factor):
    f32 = jnp.float32
    ids = (lax.axis_index("replica") & 1).astype(jnp.int32).reshape(1)
    shape = (MATS, COLS, WIDTH)
    keep, send, drift = pl.pallas_call(
        pack_kernel,
        out_shape=[pltpu.VMEM((CHIPS, SHARE, BLOCK), f32)] * 2 + [pltpu.VMEM(shape, f32)],
        in_specs=[SMEM, HBM, HBM, HBM],
        out_specs=[VMEM] * 3,
        scratch_shapes=[
            pltpu.VMEM(shape, jnp.bfloat16),
            pltpu.VMEM(shape, jnp.bfloat16),
            pltpu.VMEM(shape, f32),
            pltpu.SemaphoreType.DMA((3, 3)),
        ],
        compiler_params=PACK_PARAMS,
        name="pack",
    )(ids, weights, local_weights[0], carried_error[0])
    qt = jnp.swapaxes(initial_factor, 1, 2)
    shares = exchange_z(keep + sibling(send))
    inner, factor = pl.pallas_call(
        factor_kernel,
        out_shape=[
            jax.ShapeDtypeStruct((MROWS, BLOCK), f32),
            jax.ShapeDtypeStruct((FROWS, BLOCK), f32),
        ],
        in_specs=[SMEM, VMEM, VMEM],
        out_specs=[VMEM, VMEM],
        compiler_params=PARAMS,
        name="factor",
    )(ids, qt, shares)

    arrivals = []
    for line_core in (0, 1):
        arrivals.append(
            exchange_mixed(
                jnp.broadcast_to(jnp.concatenate([factor, inner]), (CHIPS, GROWS, BLOCK)),
                line_core,
            )
        )
        inner = jnp.sum(arrivals[-1][:, FROWS:], axis=0)
    own = pl.pallas_call(
        choose_kernel,
        out_shape=pltpu.VMEM((CHIPS * FROWS + MROWS, BLOCK), f32),
        in_specs=[SMEM, VMEM, VMEM],
        out_specs=VMEM,
        compiler_params=PARAMS,
        name="choose",
    )(ids, *arrivals)
    sib = sibling(own)

    next_weights, next_error, next_momentum, following = pl.pallas_call(
        lambda *refs: final_kernel(lax.axis_size("replica"), *refs),
        out_shape=[
            jax.ShapeDtypeStruct(shape, jnp.bfloat16),
            jax.ShapeDtypeStruct(shape, f32),
            jax.ShapeDtypeStruct(shape, f32),
            jax.ShapeDtypeStruct((MATS, RANK, COLS), f32),
        ],
        in_specs=[SMEM] + [VMEM] * 6,
        out_specs=[HBM, HBM, HBM, VMEM],
        scratch_shapes=[
            pltpu.VMEM((MATS, 6 * RANK, WIDTH), jnp.bfloat16),
            pltpu.VMEM(shape, jnp.bfloat16),
            pltpu.VMEM(shape, f32),
            pltpu.VMEM(shape, f32),
            pltpu.SemaphoreType.DMA((3, 3)),
        ],
        compiler_params=PARAMS,
        name="final",
    )(ids, qt, own, sib, weights, momentum, drift)
    return (next_weights, next_error[None], next_momentum, jnp.swapaxes(following, 1, 2))


def solution(mesh):
    return jax.shard_map(
        local,
        mesh=mesh,
        in_specs=(
            P(None, None, "fsdp"),
            P("replica", None, None, "fsdp"),
            P("replica", None, None, "fsdp"),
            P(None, None, "fsdp"),
            P(),
        ),
        out_specs=(
            P(None, None, "fsdp"),
            P("replica", None, None, "fsdp"),
            P(None, None, "fsdp"),
            P(),
        ),
        check_vma=False,
    )
```

```python
import jax
import jax.numpy as jnp
from jax import lax
from jax.experimental import pallas as pl
from jax.experimental.pallas import tpu as pltpu
from jax.sharding import PartitionSpec as P

CHIPS = 16
BLOCK = 128
SIDE = BLOCK // 2
BLOCKS = 14
WIDTH = BLOCK * BLOCKS
MATS = 3
COLS = 32
RANK = 16
SHARE = MATS * COLS // 2
FROWS = SHARE // 2
MROWS = 8
GROWS = FROWS + MROWS
PAIR = RANK + COLS
HIGHEST = lax.Precision.HIGHEST
VMEM = pl.BlockSpec(memory_space=pltpu.VMEM)
SMEM = pl.BlockSpec(memory_space=pltpu.SMEM)
HBM = pl.BlockSpec(memory_space=pl.ANY)
PARAMS = pltpu.CompilerParams(vmem_limit_bytes=32 * 1024 * 1024)
PACK_PARAMS = pltpu.CompilerParams(vmem_limit_bytes=56 * 1024 * 1024)


def slot_of(chip, core):
    return ((13 * (chip - 3)) & 15) ^ (8 * core)


def chip_at(slot, core):
    return (3 + 8 * core + 5 * slot) % CHIPS


def gather_slot(chip):
    return (9 * chip) % CHIPS


def swap_sides(x):
    return pltpu.roll(x, SIDE, 1)


def left_side(rows):
    return lax.broadcasted_iota(jnp.int32, (rows, BLOCK), 1) < SIDE


def pack_kernel(ids, w_hbm, lw_hbm, ce_hbm, keep, send, drift, w, lw, ce, sems):
    core = ids[0]
    copies = [
        [
            pltpu.make_async_copy(src.at[mat], dst.at[mat], sems.at[kind, mat])
            for kind, (src, dst) in enumerate(((ce_hbm, ce), (w_hbm, w), (lw_hbm, lw)))
        ]
        for mat in range(MATS)
    ]
    for group in copies:
        for copy in group:
            copy.start()
    left = left_side(16)
    for block in range(BLOCKS, CHIPS):
        keep[slot_of(block, core)] = jnp.zeros((SHARE, BLOCK), jnp.float32)
        send[slot_of(block, 1 - core)] = jnp.zeros((SHARE, BLOCK), jnp.float32)
    for mat in range(MATS):
        for copy in copies[mat]:
            copy.wait()
        for block in range(BLOCKS):
            lanes = slice(block * BLOCK, (block + 1) * BLOCK)
            value = (
                w[mat, :, lanes].astype(jnp.float32)
                - lw[mat, :, lanes].astype(jnp.float32)
                + ce[mat, :, lanes]
            )
            drift[mat, :, lanes] = value
    for block in range(BLOCKS):
        lanes = slice(block * BLOCK, (block + 1) * BLOCK)
        keep[slot_of(block, core), 0:COLS] = drift[2 * core, :, lanes]
        send[slot_of(block, 1 - core), 0:COLS] = drift[2 - 2 * core, :, lanes]
        top, bottom = drift[1, 0:16, lanes], drift[1, 16:32, lanes]
        first = jnp.where(left, top, swap_sides(bottom))
        second = jnp.where(left, swap_sides(top), bottom)
        keep[slot_of(block, core), COLS:SHARE] = jnp.where(core == 0, first, second)
        send[slot_of(block, 1 - core), COLS:SHARE] = jnp.where(core == 0, second, first)


def outer(a, b):
    return lax.dot_general(
        a, b, (((1,), (1,)), ((), ())), precision=HIGHEST, preferred_element_type=jnp.float32
    )


def factor_kernel(ids, qt, got, inner, factor):
    core = ids[0]
    total = jnp.sum(got[...], axis=0)
    left = left_side(16)
    whole = total[0:COLS]
    half = total[COLS:SHARE]
    half = jnp.concatenate(
        [jnp.where(left, half, 0.0), jnp.where(left, swap_sides(half), 0.0)], axis=0
    )
    whole_factor = jnp.dot(
        qt[2 * core], whole, precision=HIGHEST, preferred_element_type=jnp.float32
    )
    half_factor = jnp.dot(qt[1], half, precision=HIGHEST, preferred_element_type=jnp.float32)
    factor[0:RANK] = whole_factor
    factor[RANK:FROWS] = half_factor[0:8] + swap_sides(half_factor[8:16])
    whole, half = outer(whole_factor, whole), outer(half_factor, half)
    inner[...] = jnp.concatenate([whole[0:8], whole[8:16], half[0:8], half[8:16]], axis=1)


def choose_kernel(ids, one, two, out):
    out[CHIPS * FROWS :] = jnp.sum(two[:, FROWS:GROWS], axis=0)
    for core, arrived in enumerate((two, one)):

        @pl.when(ids[0] == core)
        def _():
            for slot in range(CHIPS):
                out[slot * FROWS : slot * FROWS + FROWS] = arrived[slot, 0:FROWS]


def split(x):
    high = x.astype(jnp.bfloat16)
    rest = x - high.astype(jnp.float32)
    middle = rest.astype(jnp.bfloat16)
    return high, middle, (rest - middle.astype(jnp.float32)).astype(jnp.bfloat16)


def final_kernel(
    islands, ids, qt, own, sib, w, mom, drift,
    out_w, out_e, out_m, out_f, fac, buf_w, buf_e, buf_m, sems,
):
    first = ids[0] == 0

    rows = slice(CHIPS * FROWS, CHIPS * FROWS + MROWS)
    mine, other = own[rows], sib[rows]
    middle = pltpu.roll(mine + other, SIDE, 1)
    table = []
    for mat, rows in enumerate(
        (jnp.where(first, mine, other), middle, jnp.where(first, other, mine))
    ):
        rows = jnp.concatenate([rows[:, 0:COLS], rows[:, COLS : 2 * COLS]], axis=0)
        gram = outer(qt[mat], rows)
        rest = jnp.zeros((RANK, BLOCK - PAIR), jnp.float32)
        table.append(jnp.concatenate([gram, rows, rest], axis=1))
    table = jnp.stack(table)
    row = lax.broadcasted_iota(jnp.int32, table.shape, 1)
    small = table
    for step in range(0, RANK, 2):
        one = jnp.broadcast_to(table[:, :, step : step + 1], table.shape)
        two = jnp.broadcast_to(table[:, :, step + 1 : step + 2], table.shape)
        line = table[:, step : step + 1, :]
        pivot, cross = one[:, step : step + 1, :], two[:, step : step + 1, :]
        inverse = 1.0 / pivot
        ratio = one[:, step + 1 : step + 2, :] * inverse
        next_line = table[:, step + 1 : step + 2, :] - ratio * line
        next_pivot = two[:, step + 1 : step + 2, :] - ratio * cross
        next_scaled = next_line * (1.0 / next_pivot)
        scaled = (line - cross * next_scaled) * inverse
        here, below = row == step, row == step + 1
        small = jnp.where(here, line * lax.rsqrt(pivot), small)
        small = jnp.where(below, next_line * lax.rsqrt(next_pivot), small)
        rest = table - one * scaled - two * next_scaled
        table = jnp.where(here, scaled, jnp.where(below, next_scaled, rest))

    left = left_side(8)
    for block in range(BLOCKS):
        lanes = slice(block * BLOCK, (block + 1) * BLOCK)
        start = gather_slot(block) * FROWS
        mine, other = own[start : start + FROWS], sib[start : start + FROWS]
        low, high = jnp.where(first, mine, other), jnp.where(first, other, mine)
        low_half, high_half = low[RANK:FROWS], high[RANK:FROWS]
        half = jnp.concatenate(
            [
                jnp.where(left, low_half, swap_sides(high_half)),
                jnp.where(left, swap_sides(low_half), high_half),
            ],
            axis=0,
        )
        for mat, value in enumerate((low[0:RANK], half, high[0:RANK])):
            top, mid, last = split(value)
            for place, part in enumerate((top, mid, last, top, mid, top)):
                fac[mat, place * RANK : place * RANK + RANK, lanes] = part

    for mat in range(MATS):
        out_f[mat] = small[mat, :, RANK:PAIR] * (1.0 / islands)
        top, mid, last = split(table[mat, :, RANK:PAIR] * (1.0 / islands))
        parts = [x.astype(jnp.float32) for x in (top, top, top, mid, mid, last)]
        mixed = jnp.transpose(jnp.concatenate(parts, axis=0)).astype(jnp.bfloat16)
        for tile in range(7):
            lanes = slice(tile * 256, (tile + 1) * 256)
            approx = jnp.dot(mixed, fac[mat, :, lanes], preferred_element_type=jnp.float32)
            wide = w[mat, :, lanes].astype(jnp.float32)
            momentum = 0.9 * mom[mat, :, lanes] + approx
            buf_e[mat, :, lanes] = drift[mat, :, lanes] - approx
            buf_m[mat, :, lanes] = momentum
            buf_w[mat, :, lanes] = (wide - 0.7 * (approx + 0.9 * momentum)).astype(jnp.bfloat16)
        for kind, (buf, out) in enumerate(((buf_w, out_w), (buf_e, out_e), (buf_m, out_m))):
            pltpu.make_async_copy(buf.at[mat], out.at[mat], sems.at[kind, mat]).start()
    for mat in range(MATS):
        for kind, (buf, out) in enumerate(((buf_w, out_w), (buf_e, out_e), (buf_m, out_m))):
            pltpu.make_async_copy(buf.at[mat], out.at[mat], sems.at[kind, mat]).wait()


def sibling(x):
    return lax.ppermute(x, "replica", [(i, i ^ 1) for i in range(2 * CHIPS)])


def exchange_z(x):
    groups = [[2 * chip_at(slot, core) + core for slot in range(CHIPS)] for core in range(2)]
    return lax.all_to_all(x, "replica", 0, 0, axis_index_groups=groups, tiled=True)


def exchange_mixed(x, line_core):
    lines = [
        [(2 * gather_slot(slot) + line_core) * 16 + place for slot in range(CHIPS)]
        for place in range(16)
    ]
    planes = [
        [(2 * chip + 1 - line_core) * 16 + place for place in range(16)] for chip in range(CHIPS)
    ]
    return lax.all_to_all(
        x, ("replica", "fsdp"), 0, 0, axis_index_groups=lines + planes, tiled=True
    )


def local(weights, local_weights, carried_error, momentum, initial_factor):
    f32 = jnp.float32
    ids = (lax.axis_index("replica") & 1).astype(jnp.int32).reshape(1)
    shape = (MATS, COLS, WIDTH)
    keep, send, drift = pl.pallas_call(
        pack_kernel,
        out_shape=[pltpu.VMEM((CHIPS, SHARE, BLOCK), f32)] * 2 + [pltpu.VMEM(shape, f32)],
        in_specs=[SMEM, HBM, HBM, HBM],
        out_specs=[VMEM] * 3,
        scratch_shapes=[
            pltpu.VMEM(shape, jnp.bfloat16),
            pltpu.VMEM(shape, jnp.bfloat16),
            pltpu.VMEM(shape, f32),
            pltpu.SemaphoreType.DMA((3, 3)),
        ],
        compiler_params=PACK_PARAMS,
        name="pack",
    )(ids, weights, local_weights[0], carried_error[0])
    qt = jnp.swapaxes(initial_factor, 1, 2)
    shares = exchange_z(keep + sibling(send))
    inner, factor = pl.pallas_call(
        factor_kernel,
        out_shape=[
            jax.ShapeDtypeStruct((MROWS, BLOCK), f32),
            jax.ShapeDtypeStruct((FROWS, BLOCK), f32),
        ],
        in_specs=[SMEM, VMEM, VMEM],
        out_specs=[VMEM, VMEM],
        compiler_params=PARAMS,
        name="factor",
    )(ids, qt, shares)

    arrivals = []
    for line_core in (1, 0):
        arrivals.append(
            exchange_mixed(
                jnp.broadcast_to(jnp.concatenate([factor, inner]), (CHIPS, GROWS, BLOCK)),
                line_core,
            )
        )
        inner = jnp.sum(arrivals[-1][:, FROWS:], axis=0)
    own = pl.pallas_call(
        choose_kernel,
        out_shape=pltpu.VMEM((CHIPS * FROWS + MROWS, BLOCK), f32),
        in_specs=[SMEM, VMEM, VMEM],
        out_specs=VMEM,
        compiler_params=PARAMS,
        name="choose",
    )(ids, *arrivals)
    sib = sibling(own)

    next_weights, next_error, next_momentum, following = pl.pallas_call(
        lambda *refs: final_kernel(lax.axis_size("replica"), *refs),
        out_shape=[
            jax.ShapeDtypeStruct(shape, jnp.bfloat16),
            jax.ShapeDtypeStruct(shape, f32),
            jax.ShapeDtypeStruct(shape, f32),
            jax.ShapeDtypeStruct((MATS, RANK, COLS), f32),
        ],
        in_specs=[SMEM] + [VMEM] * 6,
        out_specs=[HBM, HBM, HBM, VMEM],
        scratch_shapes=[
            pltpu.VMEM((MATS, 6 * RANK, WIDTH), jnp.bfloat16),
            pltpu.VMEM(shape, jnp.bfloat16),
            pltpu.VMEM(shape, f32),
            pltpu.VMEM(shape, f32),
            pltpu.SemaphoreType.DMA((3, 3)),
        ],
        compiler_params=PARAMS,
        name="final",
    )(ids, qt, own, sib, weights, momentum, drift)
    return (next_weights, next_error[None], next_momentum, jnp.swapaxes(following, 1, 2))


def solution(mesh):
    return jax.shard_map(
        local,
        mesh=mesh,
        in_specs=(
            P(None, None, "fsdp"),
            P("replica", None, None, "fsdp"),
            P("replica", None, None, "fsdp"),
            P(None, None, "fsdp"),
            P(),
        ),
        out_specs=(
            P(None, None, "fsdp"),
            P("replica", None, None, "fsdp"),
            P(None, None, "fsdp"),
            P(),
        ),
        check_vma=False,
    )
```

```python
import jax
import jax.numpy as jnp
from jax import lax
from jax.experimental import pallas as pl
from jax.experimental.pallas import tpu as pltpu
from jax.sharding import PartitionSpec as P

CHIPS = 16
BLOCK = 128
SIDE = BLOCK // 2
BLOCKS = 14
WIDTH = BLOCK * BLOCKS
MATS = 3
COLS = 32
RANK = 16
SHARE = MATS * COLS // 2
FROWS = SHARE // 2
MROWS = 8
GROWS = FROWS + MROWS
PAIR = RANK + COLS
HIGHEST = lax.Precision.HIGHEST
VMEM = pl.BlockSpec(memory_space=pltpu.VMEM)
SMEM = pl.BlockSpec(memory_space=pltpu.SMEM)
HBM = pl.BlockSpec(memory_space=pl.ANY)
PARAMS = pltpu.CompilerParams(vmem_limit_bytes=32 * 1024 * 1024)
PACK_PARAMS = pltpu.CompilerParams(vmem_limit_bytes=56 * 1024 * 1024)


def slot_of(chip, core):
    return ((13 * (chip - 3)) & 15) ^ (8 * core)


def chip_at(slot, core):
    return (3 + 8 * core + 5 * slot) % CHIPS


def gather_slot(chip):
    return (9 * chip) % CHIPS


def swap_sides(x):
    return pltpu.roll(x, SIDE, 1)


def left_side(rows):
    return lax.broadcasted_iota(jnp.int32, (rows, BLOCK), 1) < SIDE


def corrected(w, lw, ce, mat, lanes):
    return (
        w[mat, :, lanes].astype(jnp.float32)
        - lw[mat, :, lanes].astype(jnp.float32)
        + ce[mat, :, lanes]
    )


def half_block(value, core):
    left = left_side(16)
    top, bottom = value[0:16], value[16:32]
    first = jnp.where(left, top, swap_sides(bottom))
    second = jnp.where(left, swap_sides(top), bottom)
    return jnp.where(core == 0, first, second)


def send_kernel(ids, w_hbm, lw_hbm, ce_hbm, send, ids_out, w, lw, ce, sems):
    other = 1 - ids[0]
    ids_out[0] = ids[0]
    copies = [
        [
            pltpu.make_async_copy(src.at[mat], dst.at[place], sems.at[kind, place])
            for kind, (src, dst) in enumerate(((ce_hbm, ce), (w_hbm, w), (lw_hbm, lw)))
        ]
        for place, mat in enumerate((1, 2 * other))
    ]
    for group in copies:
        for copy in group:
            copy.start()
    for block in range(BLOCKS, CHIPS):
        send[slot_of(block, other)] = jnp.zeros((SHARE, BLOCK), jnp.float32)
    for place, rows in enumerate((slice(COLS, SHARE), slice(0, COLS))):
        for copy in copies[place]:
            copy.wait()
        for block in range(BLOCKS):
            lanes = slice(block * BLOCK, (block + 1) * BLOCK)
            value = corrected(w, lw, ce, place, lanes)
            send[slot_of(block, other), rows] = half_block(value, other) if place == 0 else value


def keep_kernel(ids, w_hbm, lw_hbm, ce_hbm, keep, drift, w, lw, ce, sems):
    core = ids[0]
    copies = [
        [
            pltpu.make_async_copy(src.at[mat], dst.at[mat], sems.at[kind, mat])
            for kind, (src, dst) in enumerate(((ce_hbm, ce), (w_hbm, w), (lw_hbm, lw)))
        ]
        for mat in range(MATS)
    ]
    for group in copies:
        for copy in group:
            copy.start()
    for block in range(BLOCKS, CHIPS):
        keep[slot_of(block, core)] = jnp.zeros((SHARE, BLOCK), jnp.float32)
    for mat in range(MATS):
        for copy in copies[mat]:
            copy.wait()
        for block in range(BLOCKS):
            lanes = slice(block * BLOCK, (block + 1) * BLOCK)
            drift[mat, :, lanes] = corrected(w, lw, ce, mat, lanes)
    for block in range(BLOCKS):
        lanes = slice(block * BLOCK, (block + 1) * BLOCK)
        keep[slot_of(block, core), 0:COLS] = drift[2 * core, :, lanes]
        keep[slot_of(block, core), COLS:SHARE] = half_block(drift[1, :, lanes], core)


def outer(a, b):
    return lax.dot_general(
        a, b, (((1,), (1,)), ((), ())), precision=HIGHEST, preferred_element_type=jnp.float32
    )


def factor_kernel(ids, qt, got, inner, factor):
    core = ids[0]
    total = jnp.sum(got[...], axis=0)
    left = left_side(16)
    whole = total[0:COLS]
    half = total[COLS:SHARE]
    half = jnp.concatenate(
        [jnp.where(left, half, 0.0), jnp.where(left, swap_sides(half), 0.0)], axis=0
    )
    whole_factor = jnp.dot(
        qt[2 * core], whole, precision=HIGHEST, preferred_element_type=jnp.float32
    )
    half_factor = jnp.dot(qt[1], half, precision=HIGHEST, preferred_element_type=jnp.float32)
    factor[0:RANK] = whole_factor
    factor[RANK:FROWS] = half_factor[0:8] + swap_sides(half_factor[8:16])
    whole, half = outer(whole_factor, whole), outer(half_factor, half)
    inner[...] = jnp.concatenate([whole[0:8], whole[8:16], half[0:8], half[8:16]], axis=1)


def stacked(a, b):
    a_top, a_mid, a_last = split(a)
    b_top, b_mid, b_last = split(b)
    a = jnp.concatenate([a_top, a_top, a_top, a_mid, a_mid, a_last], axis=1)
    b = jnp.concatenate([b_top, b_mid, b_last, b_top, b_mid, b_top], axis=1)
    return lax.dot_general(a, b, (((1,), (1,)), ((), ())), preferred_element_type=jnp.float32)


def choose_kernel(ids, one, two, out):
    out[CHIPS * FROWS :] = jnp.sum(two[:, FROWS:GROWS], axis=0)
    for core, arrived in enumerate((one, two)):

        @pl.when(ids[0] == core)
        def _():
            for slot in range(CHIPS):
                out[slot * FROWS : slot * FROWS + FROWS] = arrived[slot, 0:FROWS]


def split(x):
    high = x.astype(jnp.bfloat16)
    rest = x - high.astype(jnp.float32)
    middle = rest.astype(jnp.bfloat16)
    return high, middle, (rest - middle.astype(jnp.float32)).astype(jnp.bfloat16)


def final_kernel(
    islands, ids, qt, own, sib, w, mom, drift,
    out_w, out_e, out_m, out_f, fac, buf_w, buf_e, buf_m, sems,
):
    first = ids[0] == 0

    rows = slice(CHIPS * FROWS, CHIPS * FROWS + MROWS)
    mine, other = own[rows], sib[rows]
    middle = pltpu.roll(mine + other, SIDE, 1)
    table = []
    for mat, rows in enumerate(
        (jnp.where(first, mine, other), middle, jnp.where(first, other, mine))
    ):
        rows = jnp.concatenate([rows[:, 0:COLS], rows[:, COLS : 2 * COLS]], axis=0)
        gram = stacked(qt[mat], rows)
        rest = jnp.zeros((RANK, BLOCK - PAIR), jnp.float32)
        table.append(jnp.concatenate([gram, rows, rest], axis=1))
    table = jnp.stack(table)
    row = lax.broadcasted_iota(jnp.int32, table.shape, 1)
    small = table
    for step in range(0, RANK, 2):
        one = jnp.broadcast_to(table[:, :, step : step + 1], table.shape)
        two = jnp.broadcast_to(table[:, :, step + 1 : step + 2], table.shape)
        line = table[:, step : step + 1, :]
        pivot, cross = one[:, step : step + 1, :], two[:, step : step + 1, :]
        inverse = 1.0 / pivot
        ratio = one[:, step + 1 : step + 2, :] * inverse
        next_line = table[:, step + 1 : step + 2, :] - ratio * line
        next_pivot = two[:, step + 1 : step + 2, :] - ratio * cross
        next_scaled = next_line * (1.0 / next_pivot)
        scaled = (line - cross * next_scaled) * inverse
        here, below = row == step, row == step + 1
        small = jnp.where(here, line * lax.rsqrt(pivot), small)
        small = jnp.where(below, next_line * lax.rsqrt(next_pivot), small)
        rest = table - one * scaled - two * next_scaled
        table = jnp.where(here, scaled, jnp.where(below, next_scaled, rest))

    left = left_side(8)
    for block in range(BLOCKS):
        lanes = slice(block * BLOCK, (block + 1) * BLOCK)
        start = gather_slot(block) * FROWS
        mine, other = own[start : start + FROWS], sib[start : start + FROWS]
        low, high = jnp.where(first, mine, other), jnp.where(first, other, mine)
        low_half, high_half = low[RANK:FROWS], high[RANK:FROWS]
        half = jnp.concatenate(
            [
                jnp.where(left, low_half, swap_sides(high_half)),
                jnp.where(left, swap_sides(low_half), high_half),
            ],
            axis=0,
        )
        for mat, value in enumerate((low[0:RANK], half, high[0:RANK])):
            top, mid, last = split(value)
            for place, part in enumerate((top, mid, last, top, mid, top)):
                fac[mat, place * RANK : place * RANK + RANK, lanes] = part

    for mat in range(MATS):
        out_f[mat] = small[mat, :, RANK:PAIR] * (1.0 / islands)
        top, mid, last = split(table[mat, :, RANK:PAIR] * (1.0 / islands))
        parts = [x.astype(jnp.float32) for x in (top, top, top, mid, mid, last)]
        mixed = jnp.transpose(jnp.concatenate(parts, axis=0)).astype(jnp.bfloat16)
        for tile in range(7):
            lanes = slice(tile * 256, (tile + 1) * 256)
            approx = jnp.dot(mixed, fac[mat, :, lanes], preferred_element_type=jnp.float32)
            wide = w[mat, :, lanes].astype(jnp.float32)
            momentum = 0.9 * mom[mat, :, lanes] + approx
            buf_e[mat, :, lanes] = drift[mat, :, lanes] - approx
            buf_m[mat, :, lanes] = momentum
            buf_w[mat, :, lanes] = (wide - 0.7 * (approx + 0.9 * momentum)).astype(jnp.bfloat16)
        for kind, (buf, out) in enumerate(((buf_w, out_w), (buf_e, out_e), (buf_m, out_m))):
            pltpu.make_async_copy(buf.at[mat], out.at[mat], sems.at[kind, mat]).start()
    for mat in range(MATS):
        for kind, (buf, out) in enumerate(((buf_w, out_w), (buf_e, out_e), (buf_m, out_m))):
            pltpu.make_async_copy(buf.at[mat], out.at[mat], sems.at[kind, mat]).wait()


def sibling(x):
    return lax.ppermute(x, "replica", [(i, i ^ 1) for i in range(2 * CHIPS)])


def exchange_z(x):
    groups = [[2 * chip_at(slot, core) + core for slot in range(CHIPS)] for core in range(2)]
    return lax.all_to_all(x, "replica", 0, 0, axis_index_groups=groups, tiled=True)


def exchange_mixed(x, line_core):
    lines = [
        [(2 * gather_slot(slot) + line_core) * 16 + place for slot in range(CHIPS)]
        for place in range(16)
    ]
    planes = [
        [(2 * chip + 1 - line_core) * 16 + place for place in range(16)] for chip in range(CHIPS)
    ]
    return lax.all_to_all(
        x, ("replica", "fsdp"), 0, 0, axis_index_groups=lines + planes, tiled=True
    )


def local(weights, local_weights, carried_error, momentum, initial_factor):
    f32 = jnp.float32
    ids = (lax.axis_index("replica") & 1).astype(jnp.int32).reshape(1)
    shape = (MATS, COLS, WIDTH)
    arrays = (weights, local_weights[0], carried_error[0])
    send, ids_after = pl.pallas_call(
        send_kernel,
        out_shape=[pltpu.VMEM((CHIPS, SHARE, BLOCK), f32), pltpu.SMEM((1,), jnp.int32)],
        in_specs=[SMEM, HBM, HBM, HBM],
        out_specs=[VMEM, SMEM],
        scratch_shapes=[
            pltpu.VMEM((2, COLS, WIDTH), jnp.bfloat16),
            pltpu.VMEM((2, COLS, WIDTH), jnp.bfloat16),
            pltpu.VMEM((2, COLS, WIDTH), f32),
            pltpu.SemaphoreType.DMA((3, 2)),
        ],
        compiler_params=PACK_PARAMS,
        name="pack_send",
    )(ids, *arrays)
    got = sibling(send)
    keep, drift = pl.pallas_call(
        keep_kernel,
        out_shape=[pltpu.VMEM((CHIPS, SHARE, BLOCK), f32), pltpu.VMEM(shape, f32)],
        in_specs=[SMEM, HBM, HBM, HBM],
        out_specs=[VMEM] * 2,
        scratch_shapes=[
            pltpu.VMEM(shape, jnp.bfloat16),
            pltpu.VMEM(shape, jnp.bfloat16),
            pltpu.VMEM(shape, f32),
            pltpu.SemaphoreType.DMA((3, 3)),
        ],
        compiler_params=PACK_PARAMS,
        cost_estimate=pl.CostEstimate(
            flops=1_000_000, bytes_accessed=4_000_000, transcendentals=0
        ),
        name="pack_keep",
    )(ids_after, *arrays)
    qt = jnp.swapaxes(initial_factor, 1, 2)
    shares = exchange_z(keep + got)
    inner, factor = pl.pallas_call(
        factor_kernel,
        out_shape=[
            jax.ShapeDtypeStruct((MROWS, BLOCK), f32),
            jax.ShapeDtypeStruct((FROWS, BLOCK), f32),
        ],
        in_specs=[SMEM, VMEM, VMEM],
        out_specs=[VMEM, VMEM],
        compiler_params=PARAMS,
        name="factor",
    )(ids, qt, shares)

    arrivals = []
    for line_core in (0, 1):
        arrivals.append(
            exchange_mixed(
                jnp.broadcast_to(jnp.concatenate([factor, inner]), (CHIPS, GROWS, BLOCK)),
                line_core,
            )
        )
        inner = jnp.sum(arrivals[-1][:, FROWS:], axis=0)
    own = pl.pallas_call(
        choose_kernel,
        out_shape=pltpu.VMEM((CHIPS * FROWS + MROWS, BLOCK), f32),
        in_specs=[SMEM, VMEM, VMEM],
        out_specs=VMEM,
        compiler_params=PARAMS,
        name="choose",
    )(ids, *arrivals)
    sib = sibling(own)

    next_weights, next_error, next_momentum, following = pl.pallas_call(
        lambda *refs: final_kernel(lax.axis_size("replica"), *refs),
        out_shape=[
            jax.ShapeDtypeStruct(shape, jnp.bfloat16),
            jax.ShapeDtypeStruct(shape, f32),
            jax.ShapeDtypeStruct(shape, f32),
            jax.ShapeDtypeStruct((MATS, RANK, COLS), f32),
        ],
        in_specs=[SMEM] + [VMEM] * 6,
        out_specs=[HBM, HBM, HBM, VMEM],
        scratch_shapes=[
            pltpu.VMEM((MATS, 6 * RANK, WIDTH), jnp.bfloat16),
            pltpu.VMEM(shape, jnp.bfloat16),
            pltpu.VMEM(shape, f32),
            pltpu.VMEM(shape, f32),
            pltpu.SemaphoreType.DMA((3, 3)),
        ],
        compiler_params=PARAMS,
        name="final",
    )(ids, qt, own, sib, weights, momentum, drift)
    return (next_weights, next_error[None], next_momentum, jnp.swapaxes(following, 1, 2))


def solution(mesh):
    return jax.shard_map(
        local,
        mesh=mesh,
        in_specs=(
            P(None, None, "fsdp"),
            P("replica", None, None, "fsdp"),
            P("replica", None, None, "fsdp"),
            P(None, None, "fsdp"),
            P(),
        ),
        out_specs=(
            P(None, None, "fsdp"),
            P("replica", None, None, "fsdp"),
            P(None, None, "fsdp"),
            P(),
        ),
        check_vma=False,
    )
```

```python
import jax
import jax.numpy as jnp
from jax import lax
from jax.experimental import pallas as pl
from jax.experimental.pallas import tpu as pltpu
from jax.sharding import PartitionSpec as P

CHIPS = 16
BLOCK = 128
SIDE = BLOCK // 2
BLOCKS = 14
WIDTH = BLOCK * BLOCKS
MATS = 3
COLS = 32
RANK = 16
SHARE = MATS * COLS // 2
FROWS = SHARE // 2
MROWS = 8
GROWS = FROWS + MROWS
PAIR = RANK + COLS
HIGHEST = lax.Precision.HIGHEST
VMEM = pl.BlockSpec(memory_space=pltpu.VMEM)
SMEM = pl.BlockSpec(memory_space=pltpu.SMEM)
HBM = pl.BlockSpec(memory_space=pl.ANY)
PARAMS = pltpu.CompilerParams(vmem_limit_bytes=32 * 1024 * 1024)
PACK_PARAMS = pltpu.CompilerParams(vmem_limit_bytes=56 * 1024 * 1024)


def slot_of(chip, core):
    return ((13 * (chip - 3)) & 15) ^ (8 * core)


def chip_at(slot, core):
    return (3 + 8 * core + 5 * slot) % CHIPS


def gather_slot(chip):
    return (9 * chip) % CHIPS


def swap_sides(x):
    return pltpu.roll(x, SIDE, 1)


def left_side(rows):
    return lax.broadcasted_iota(jnp.int32, (rows, BLOCK), 1) < SIDE


def corrected(w, lw, ce, mat, lanes):
    return (
        w[mat, :, lanes].astype(jnp.float32)
        - lw[mat, :, lanes].astype(jnp.float32)
        + ce[mat, :, lanes]
    )


def half_block(value, core):
    left = left_side(16)
    top, bottom = value[0:16], value[16:32]
    first = jnp.where(left, top, swap_sides(bottom))
    second = jnp.where(left, swap_sides(top), bottom)
    return jnp.where(core == 0, first, second)


def send_kernel(ids, w_hbm, lw_hbm, ce_hbm, send, ids_out, w, lw, ce, sems):
    other = 1 - ids[0]
    ids_out[0] = ids[0]
    copies = [
        [
            pltpu.make_async_copy(src.at[mat], dst.at[place], sems.at[kind, place])
            for kind, (src, dst) in enumerate(((ce_hbm, ce), (w_hbm, w), (lw_hbm, lw)))
        ]
        for place, mat in enumerate((1, 2 * other))
    ]
    for group in copies:
        for copy in group:
            copy.start()
    for block in range(BLOCKS, CHIPS):
        send[slot_of(block, other)] = jnp.zeros((SHARE, BLOCK), jnp.float32)
    for place, rows in enumerate((slice(COLS, SHARE), slice(0, COLS))):
        for copy in copies[place]:
            copy.wait()
        for block in range(BLOCKS):
            lanes = slice(block * BLOCK, (block + 1) * BLOCK)
            value = corrected(w, lw, ce, place, lanes)
            send[slot_of(block, other), rows] = half_block(value, other) if place == 0 else value


def keep_kernel(ids, w_hbm, lw_hbm, ce_hbm, keep, drift, w, lw, ce, sems):
    core = ids[0]
    copies = [
        [
            pltpu.make_async_copy(src.at[mat], dst.at[mat], sems.at[kind, mat])
            for kind, (src, dst) in enumerate(((ce_hbm, ce), (w_hbm, w), (lw_hbm, lw)))
        ]
        for mat in range(MATS)
    ]
    for group in copies:
        for copy in group:
            copy.start()
    for block in range(BLOCKS, CHIPS):
        keep[slot_of(block, core)] = jnp.zeros((SHARE, BLOCK), jnp.float32)
    for mat in range(MATS):
        for copy in copies[mat]:
            copy.wait()
        for block in range(BLOCKS):
            lanes = slice(block * BLOCK, (block + 1) * BLOCK)
            drift[mat, :, lanes] = corrected(w, lw, ce, mat, lanes)
    for block in range(BLOCKS):
        lanes = slice(block * BLOCK, (block + 1) * BLOCK)
        keep[slot_of(block, core), 0:COLS] = drift[2 * core, :, lanes]
        keep[slot_of(block, core), COLS:SHARE] = half_block(drift[1, :, lanes], core)


def outer(a, b):
    return lax.dot_general(
        a, b, (((1,), (1,)), ((), ())), precision=HIGHEST, preferred_element_type=jnp.float32
    )


def factor_kernel(ids, qt, got, inner, factor):
    core = ids[0]
    total = jnp.sum(got[...], axis=0)
    left = left_side(16)
    whole = total[0:COLS]
    half = total[COLS:SHARE]
    half = jnp.concatenate(
        [jnp.where(left, half, 0.0), jnp.where(left, swap_sides(half), 0.0)], axis=0
    )
    whole_factor = jnp.dot(
        qt[2 * core], whole, precision=HIGHEST, preferred_element_type=jnp.float32
    )
    half_factor = jnp.dot(qt[1], half, precision=HIGHEST, preferred_element_type=jnp.float32)
    factor[0:RANK] = whole_factor
    factor[RANK:FROWS] = half_factor[0:8] + swap_sides(half_factor[8:16])
    whole, half = outer(whole_factor, whole), outer(half_factor, half)
    inner[...] = jnp.concatenate([whole[0:8], whole[8:16], half[0:8], half[8:16]], axis=1)


def choose_kernel(ids, one, two, out):
    out[CHIPS * FROWS :] = jnp.sum(two[:, FROWS:GROWS], axis=0)
    for core, arrived in enumerate((one, two)):

        @pl.when(ids[0] == core)
        def _():
            for slot in range(CHIPS):
                out[slot * FROWS : slot * FROWS + FROWS] = arrived[slot, 0:FROWS]


def split(x):
    high = x.astype(jnp.bfloat16)
    rest = x - high.astype(jnp.float32)
    middle = rest.astype(jnp.bfloat16)
    return high, middle, (rest - middle.astype(jnp.float32)).astype(jnp.bfloat16)


def final_kernel(
    islands, ids, qt, own, sib, w, mom, drift,
    out_w, out_e, out_m, out_f, fac, buf_w, buf_e, buf_m, sems,
):
    first = ids[0] == 0

    rows = slice(CHIPS * FROWS, CHIPS * FROWS + MROWS)
    mine, other = own[rows], sib[rows]
    middle = pltpu.roll(mine + other, SIDE, 1)
    table = []
    for mat, rows in enumerate(
        (jnp.where(first, mine, other), middle, jnp.where(first, other, mine))
    ):
        rows = jnp.concatenate([rows[:, 0:COLS], rows[:, COLS : 2 * COLS]], axis=0)
        gram = outer(qt[mat], rows)
        rest = jnp.zeros((RANK, BLOCK - PAIR), jnp.float32)
        table.append(jnp.concatenate([gram, rows, rest], axis=1))
    table = jnp.stack(table)
    row = lax.broadcasted_iota(jnp.int32, table.shape, 1)
    small = table
    for step in range(0, RANK, 2):
        one = jnp.broadcast_to(table[:, :, step : step + 1], table.shape)
        two = jnp.broadcast_to(table[:, :, step + 1 : step + 2], table.shape)
        line = table[:, step : step + 1, :]
        pivot, cross = one[:, step : step + 1, :], two[:, step : step + 1, :]
        inverse = 1.0 / pivot
        ratio = one[:, step + 1 : step + 2, :] * inverse
        next_line = table[:, step + 1 : step + 2, :] - ratio * line
        next_pivot = two[:, step + 1 : step + 2, :] - ratio * cross
        next_scaled = next_line * (1.0 / next_pivot)
        scaled = (line - cross * next_scaled) * inverse
        here, below = row == step, row == step + 1
        small = jnp.where(here, line * lax.rsqrt(pivot), small)
        small = jnp.where(below, next_line * lax.rsqrt(next_pivot), small)
        rest = table - one * scaled - two * next_scaled
        table = jnp.where(here, scaled, jnp.where(below, next_scaled, rest))

    left = left_side(8)
    for block in range(BLOCKS):
        lanes = slice(block * BLOCK, (block + 1) * BLOCK)
        start = gather_slot(block) * FROWS
        mine, other = own[start : start + FROWS], sib[start : start + FROWS]
        low, high = jnp.where(first, mine, other), jnp.where(first, other, mine)
        low_half, high_half = low[RANK:FROWS], high[RANK:FROWS]
        half = jnp.concatenate(
            [
                jnp.where(left, low_half, swap_sides(high_half)),
                jnp.where(left, swap_sides(low_half), high_half),
            ],
            axis=0,
        )
        for mat, value in enumerate((low[0:RANK], half, high[0:RANK])):
            top, mid, last = split(value)
            for place, part in enumerate((top, mid, last, top, mid, top)):
                fac[mat, place * RANK : place * RANK + RANK, lanes] = part

    for mat in range(MATS):
        out_f[mat] = small[mat, :, RANK:PAIR] * (1.0 / islands)
        top, mid, last = split(table[mat, :, RANK:PAIR] * (1.0 / islands))
        parts = [x.astype(jnp.float32) for x in (top, top, top, mid, mid, last)]
        mixed = jnp.transpose(jnp.concatenate(parts, axis=0)).astype(jnp.bfloat16)
        for tile in range(7):
            lanes = slice(tile * 256, (tile + 1) * 256)
            approx = jnp.dot(mixed, fac[mat, :, lanes], preferred_element_type=jnp.float32)
            wide = w[mat, :, lanes].astype(jnp.float32)
            momentum = 0.9 * mom[mat, :, lanes] + approx
            buf_e[mat, :, lanes] = drift[mat, :, lanes] - approx
            buf_m[mat, :, lanes] = momentum
            buf_w[mat, :, lanes] = (wide - 0.7 * (approx + 0.9 * momentum)).astype(jnp.bfloat16)
        for kind, (buf, out) in enumerate(((buf_w, out_w), (buf_e, out_e), (buf_m, out_m))):
            pltpu.make_async_copy(buf.at[mat], out.at[mat], sems.at[kind, mat]).start()
    for mat in range(MATS):
        for kind, (buf, out) in enumerate(((buf_w, out_w), (buf_e, out_e), (buf_m, out_m))):
            pltpu.make_async_copy(buf.at[mat], out.at[mat], sems.at[kind, mat]).wait()


def sibling(x):
    return lax.ppermute(x, "replica", [(i, i ^ 1) for i in range(2 * CHIPS)])


def exchange_z(x):
    groups = [[2 * chip_at(slot, core) + core for slot in range(CHIPS)] for core in range(2)]
    return lax.all_to_all(x, "replica", 0, 0, axis_index_groups=groups, tiled=True)


def exchange_mixed(x, line_core):
    lines = [
        [(2 * gather_slot(slot) + line_core) * 16 + place for slot in range(CHIPS)]
        for place in range(16)
    ]
    planes = [
        [(2 * chip + 1 - line_core) * 16 + (5 * slot) % 16 for slot in range(16)]
        for chip in range(CHIPS)
    ]
    return lax.all_to_all(
        x, ("replica", "fsdp"), 0, 0, axis_index_groups=lines + planes, tiled=True
    )


def local(weights, local_weights, carried_error, momentum, initial_factor):
    f32 = jnp.float32
    ids = (lax.axis_index("replica") & 1).astype(jnp.int32).reshape(1)
    shape = (MATS, COLS, WIDTH)
    arrays = (weights, local_weights[0], carried_error[0])
    send, ids_after = pl.pallas_call(
        send_kernel,
        out_shape=[pltpu.VMEM((CHIPS, SHARE, BLOCK), f32), pltpu.SMEM((1,), jnp.int32)],
        in_specs=[SMEM, HBM, HBM, HBM],
        out_specs=[VMEM, SMEM],
        scratch_shapes=[
            pltpu.VMEM((2, COLS, WIDTH), jnp.bfloat16),
            pltpu.VMEM((2, COLS, WIDTH), jnp.bfloat16),
            pltpu.VMEM((2, COLS, WIDTH), f32),
            pltpu.SemaphoreType.DMA((3, 2)),
        ],
        compiler_params=PACK_PARAMS,
        name="pack_send",
    )(ids, *arrays)
    got = sibling(send)
    keep, drift = pl.pallas_call(
        keep_kernel,
        out_shape=[pltpu.VMEM((CHIPS, SHARE, BLOCK), f32), pltpu.VMEM(shape, f32)],
        in_specs=[SMEM, HBM, HBM, HBM],
        out_specs=[VMEM] * 2,
        scratch_shapes=[
            pltpu.VMEM(shape, jnp.bfloat16),
            pltpu.VMEM(shape, jnp.bfloat16),
            pltpu.VMEM(shape, f32),
            pltpu.SemaphoreType.DMA((3, 3)),
        ],
        compiler_params=PACK_PARAMS,
        cost_estimate=pl.CostEstimate(
            flops=1_000_000, bytes_accessed=4_000_000, transcendentals=0
        ),
        name="pack_keep",
    )(ids_after, *arrays)
    qt = jnp.swapaxes(initial_factor, 1, 2)
    shares = exchange_z(keep + got)
    inner, factor = pl.pallas_call(
        factor_kernel,
        out_shape=[
            jax.ShapeDtypeStruct((MROWS, BLOCK), f32),
            jax.ShapeDtypeStruct((FROWS, BLOCK), f32),
        ],
        in_specs=[SMEM, VMEM, VMEM],
        out_specs=[VMEM, VMEM],
        compiler_params=PARAMS,
        name="factor",
    )(ids, qt, shares)

    arrivals = []
    for line_core in (0, 1):
        arrivals.append(
            exchange_mixed(
                jnp.broadcast_to(jnp.concatenate([factor, inner]), (CHIPS, GROWS, BLOCK)),
                line_core,
            )
        )
        inner = jnp.sum(arrivals[-1][:, FROWS:], axis=0)
    own = pl.pallas_call(
        choose_kernel,
        out_shape=pltpu.VMEM((CHIPS * FROWS + MROWS, BLOCK), f32),
        in_specs=[SMEM, VMEM, VMEM],
        out_specs=VMEM,
        compiler_params=PARAMS,
        name="choose",
    )(ids, *arrivals)
    sib = sibling(own)

    next_weights, next_error, next_momentum, following = pl.pallas_call(
        lambda *refs: final_kernel(lax.axis_size("replica"), *refs),
        out_shape=[
            jax.ShapeDtypeStruct(shape, jnp.bfloat16),
            jax.ShapeDtypeStruct(shape, f32),
            jax.ShapeDtypeStruct(shape, f32),
            jax.ShapeDtypeStruct((MATS, RANK, COLS), f32),
        ],
        in_specs=[SMEM] + [VMEM] * 6,
        out_specs=[HBM, HBM, HBM, VMEM],
        scratch_shapes=[
            pltpu.VMEM((MATS, 6 * RANK, WIDTH), jnp.bfloat16),
            pltpu.VMEM(shape, jnp.bfloat16),
            pltpu.VMEM(shape, f32),
            pltpu.VMEM(shape, f32),
            pltpu.SemaphoreType.DMA((3, 3)),
        ],
        compiler_params=PARAMS,
        name="final",
    )(ids, qt, own, sib, weights, momentum, drift)
    return (next_weights, next_error[None], next_momentum, jnp.swapaxes(following, 1, 2))


def solution(mesh):
    return jax.shard_map(
        local,
        mesh=mesh,
        in_specs=(
            P(None, None, "fsdp"),
            P("replica", None, None, "fsdp"),
            P("replica", None, None, "fsdp"),
            P(None, None, "fsdp"),
            P(),
        ),
        out_specs=(
            P(None, None, "fsdp"),
            P("replica", None, None, "fsdp"),
            P(None, None, "fsdp"),
            P(),
        ),
        check_vma=False,
    )
```

```python
import jax
import jax.numpy as jnp
from jax import lax
from jax.experimental import pallas as pl
from jax.experimental.pallas import tpu as pltpu
from jax.sharding import PartitionSpec as P

CHIPS = 16
BLOCK = 128
SIDE = BLOCK // 2
BLOCKS = 14
WIDTH = BLOCK * BLOCKS
MATS = 3
COLS = 32
RANK = 16
SHARE = MATS * COLS // 2
FROWS = SHARE // 2
MROWS = 8
GROWS = FROWS + MROWS
PAIR = RANK + COLS
PARTS = ((0, 1, 2, 3), (4, 5, 6))
HIGHEST = lax.Precision.HIGHEST
VMEM = pl.BlockSpec(memory_space=pltpu.VMEM)
SMEM = pl.BlockSpec(memory_space=pltpu.SMEM)
HBM = pl.BlockSpec(memory_space=pl.ANY)
PARAMS = pltpu.CompilerParams(vmem_limit_bytes=32 * 1024 * 1024)
PACK_PARAMS = pltpu.CompilerParams(vmem_limit_bytes=56 * 1024 * 1024)


def slot_of(chip, core):
    return ((13 * (chip - 3)) & 15) ^ (8 * core)


def chip_at(slot, core):
    return (3 + 8 * core + 5 * slot) % CHIPS


def gather_slot(chip):
    return (7 * (chip - 3)) % CHIPS


def gather_chip(slot):
    return (3 + 7 * slot) % CHIPS


def swap_sides(x):
    return pltpu.roll(x, SIDE, 1)


def left_side(rows):
    return lax.broadcasted_iota(jnp.int32, (rows, BLOCK), 1) < SIDE


def corrected(w, lw, ce, mat, lanes):
    return (
        w[mat, :, lanes].astype(jnp.float32)
        - lw[mat, :, lanes].astype(jnp.float32)
        + ce[mat, :, lanes]
    )


def half_block(value, core):
    left = left_side(16)
    top, bottom = value[0:16], value[16:32]
    first = jnp.where(left, top, swap_sides(bottom))
    second = jnp.where(left, swap_sides(top), bottom)
    return jnp.where(core == 0, first, second)


def send_kernel(ids, w_hbm, lw_hbm, ce_hbm, send, ids_out, w, lw, ce, sems):
    other = 1 - ids[0]
    ids_out[0] = ids[0]
    copies = [
        [
            pltpu.make_async_copy(src.at[mat], dst.at[place], sems.at[kind, place])
            for kind, (src, dst) in enumerate(((ce_hbm, ce), (w_hbm, w), (lw_hbm, lw)))
        ]
        for place, mat in enumerate((1, 2 * other))
    ]
    for group in copies:
        for copy in group:
            copy.start()
    for block in range(BLOCKS, CHIPS):
        send[slot_of(block, other)] = jnp.zeros((SHARE, BLOCK), jnp.float32)
    for place, rows in enumerate((slice(COLS, SHARE), slice(0, COLS))):
        for copy in copies[place]:
            copy.wait()
        for block in range(BLOCKS):
            lanes = slice(block * BLOCK, (block + 1) * BLOCK)
            value = corrected(w, lw, ce, place, lanes)
            send[slot_of(block, other), rows] = half_block(value, other) if place == 0 else value


def keep_kernel(ids, w_hbm, lw_hbm, ce_hbm, keep, drift, w, lw, ce, sems):
    core = ids[0]
    copies = [
        [
            pltpu.make_async_copy(src.at[mat], dst.at[mat], sems.at[kind, mat])
            for kind, (src, dst) in enumerate(((ce_hbm, ce), (w_hbm, w), (lw_hbm, lw)))
        ]
        for mat in range(MATS)
    ]
    for group in copies:
        for copy in group:
            copy.start()
    for block in range(BLOCKS, CHIPS):
        keep[slot_of(block, core)] = jnp.zeros((SHARE, BLOCK), jnp.float32)
    for mat in range(MATS):
        for copy in copies[mat]:
            copy.wait()
        for block in range(BLOCKS):
            lanes = slice(block * BLOCK, (block + 1) * BLOCK)
            drift[mat, :, lanes] = corrected(w, lw, ce, mat, lanes)
    for block in range(BLOCKS):
        lanes = slice(block * BLOCK, (block + 1) * BLOCK)
        keep[slot_of(block, core), 0:COLS] = drift[2 * core, :, lanes]
        keep[slot_of(block, core), COLS:SHARE] = half_block(drift[1, :, lanes], core)


def outer(a, b):
    return lax.dot_general(
        a, b, (((1,), (1,)), ((), ())), precision=HIGHEST, preferred_element_type=jnp.float32
    )


def factor_kernel(ids, qt, got, inner, factor):
    core = ids[0]
    total = jnp.sum(got[...], axis=0)
    left = left_side(16)
    whole = total[0:COLS]
    half = total[COLS:SHARE]
    half = jnp.concatenate(
        [jnp.where(left, half, 0.0), jnp.where(left, swap_sides(half), 0.0)], axis=0
    )
    whole_factor = jnp.dot(
        qt[2 * core], whole, precision=HIGHEST, preferred_element_type=jnp.float32
    )
    half_factor = jnp.dot(qt[1], half, precision=HIGHEST, preferred_element_type=jnp.float32)
    factor[0:RANK] = whole_factor
    factor[RANK:FROWS] = half_factor[0:8] + swap_sides(half_factor[8:16])
    whole, half = outer(whole_factor, whole), outer(half_factor, half)
    inner[...] = jnp.concatenate([whole[0:8], whole[8:16], half[0:8], half[8:16]], axis=1)


def choose_kernel(ids, one, two, out):
    out[CHIPS * FROWS :] = jnp.sum(two[:, FROWS:GROWS], axis=0)
    for core, arrived in enumerate((one, two)):

        @pl.when(ids[0] == core)
        def _():
            for slot in range(CHIPS):
                out[slot * FROWS : slot * FROWS + FROWS] = arrived[slot, 0:FROWS]


def split(x):
    high = x.astype(jnp.bfloat16)
    rest = x - high.astype(jnp.float32)
    middle = rest.astype(jnp.bfloat16)
    return high, middle, (rest - middle.astype(jnp.float32)).astype(jnp.bfloat16)


def final_kernel(
    islands, ids, qt, own, sib, w, mom, drift,
    out_w, out_e, out_m, out_f, fac, buf_w, buf_e, buf_m, sems,
):
    first = ids[0] == 0

    def copies(mat, part):
        lanes = pl.ds(PARTS[part][0] * 256, len(PARTS[part]) * 256)
        return [
            pltpu.make_async_copy(
                buf.at[mat, :, lanes], out.at[mat, :, lanes], sems.at[kind, mat, part]
            )
            for kind, (buf, out) in enumerate(((buf_w, out_w), (buf_e, out_e), (buf_m, out_m)))
        ]

    rows = slice(CHIPS * FROWS, CHIPS * FROWS + MROWS)
    mine, other = own[rows], sib[rows]
    middle = pltpu.roll(mine + other, SIDE, 1)
    table = []
    for mat, rows in enumerate(
        (jnp.where(first, mine, other), middle, jnp.where(first, other, mine))
    ):
        rows = jnp.concatenate([rows[:, 0:COLS], rows[:, COLS : 2 * COLS]], axis=0)
        gram = outer(qt[mat], rows)
        rest = jnp.zeros((RANK, BLOCK - PAIR), jnp.float32)
        table.append(jnp.concatenate([gram, rows, rest], axis=1))
    table = jnp.stack(table)
    row = lax.broadcasted_iota(jnp.int32, table.shape, 1)
    small = table
    for step in range(0, RANK, 2):
        one = jnp.broadcast_to(table[:, :, step : step + 1], table.shape)
        two = jnp.broadcast_to(table[:, :, step + 1 : step + 2], table.shape)
        line = table[:, step : step + 1, :]
        pivot, cross = one[:, step : step + 1, :], two[:, step : step + 1, :]
        inverse = 1.0 / pivot
        ratio = one[:, step + 1 : step + 2, :] * inverse
        next_line = table[:, step + 1 : step + 2, :] - ratio * line
        next_pivot = two[:, step + 1 : step + 2, :] - ratio * cross
        next_scaled = next_line * (1.0 / next_pivot)
        scaled = (line - cross * next_scaled) * inverse
        here, below = row == step, row == step + 1
        small = jnp.where(here, line * lax.rsqrt(pivot), small)
        small = jnp.where(below, next_line * lax.rsqrt(next_pivot), small)
        rest = table - one * scaled - two * next_scaled
        table = jnp.where(here, scaled, jnp.where(below, next_scaled, rest))

    left = left_side(8)
    for block in range(BLOCKS):
        lanes = slice(block * BLOCK, (block + 1) * BLOCK)
        start = gather_slot(block) * FROWS
        mine, other = own[start : start + FROWS], sib[start : start + FROWS]
        low, high = jnp.where(first, mine, other), jnp.where(first, other, mine)
        low_half, high_half = low[RANK:FROWS], high[RANK:FROWS]
        half = jnp.concatenate(
            [
                jnp.where(left, low_half, swap_sides(high_half)),
                jnp.where(left, swap_sides(low_half), high_half),
            ],
            axis=0,
        )
        for mat, value in enumerate((low[0:RANK], half, high[0:RANK])):
            top, mid, last = split(value)
            for place, part in enumerate((top, mid, last, top, mid, top)):
                fac[mat, place * RANK : place * RANK + RANK, lanes] = part

    for mat in range(MATS):
        out_f[mat] = small[mat, :, RANK:PAIR] * (1.0 / islands)
        top, mid, last = split(table[mat, :, RANK:PAIR] * (1.0 / islands))
        parts = [x.astype(jnp.float32) for x in (top, top, top, mid, mid, last)]
        mixed = jnp.transpose(jnp.concatenate(parts, axis=0)).astype(jnp.bfloat16)
        for part, tiles in enumerate(PARTS):
            for tile in tiles:
                lanes = slice(tile * 256, (tile + 1) * 256)
                approx = jnp.dot(mixed, fac[mat, :, lanes], preferred_element_type=jnp.float32)
                wide = w[mat, :, lanes].astype(jnp.float32)
                momentum = 0.9 * mom[mat, :, lanes] + approx
                buf_e[mat, :, lanes] = drift[mat, :, lanes] - approx
                buf_m[mat, :, lanes] = momentum
                buf_w[mat, :, lanes] = (wide - 0.7 * (approx + 0.9 * momentum)).astype(
                    jnp.bfloat16
                )
            for copy in copies(mat, part):
                copy.start()
    for mat in range(MATS):
        for part in range(len(PARTS)):
            for copy in copies(mat, part):
                copy.wait()


def sibling(x):
    return lax.ppermute(x, "replica", [(i, i ^ 1) for i in range(2 * CHIPS)])


def exchange_z(x):
    groups = [[2 * chip_at(slot, core) + core for slot in range(CHIPS)] for core in range(2)]
    return lax.all_to_all(x, "replica", 0, 0, axis_index_groups=groups, tiled=True)


def exchange_mixed(x, line_core):
    lines = [
        [(2 * gather_chip(slot) + line_core) * 16 + place for slot in range(CHIPS)]
        for place in range(16)
    ]
    planes = [
        [(2 * chip + 1 - line_core) * 16 + (5 * slot) % 16 for slot in range(16)]
        for chip in range(CHIPS)
    ]
    return lax.all_to_all(
        x, ("replica", "fsdp"), 0, 0, axis_index_groups=lines + planes, tiled=True
    )


def local(weights, local_weights, carried_error, momentum, initial_factor):
    f32 = jnp.float32
    ids = (lax.axis_index("replica") & 1).astype(jnp.int32).reshape(1)
    shape = (MATS, COLS, WIDTH)
    arrays = (weights, local_weights[0], carried_error[0])
    send, ids_after = pl.pallas_call(
        send_kernel,
        out_shape=[pltpu.VMEM((CHIPS, SHARE, BLOCK), f32), pltpu.SMEM((1,), jnp.int32)],
        in_specs=[SMEM, HBM, HBM, HBM],
        out_specs=[VMEM, SMEM],
        scratch_shapes=[
            pltpu.VMEM((2, COLS, WIDTH), jnp.bfloat16),
            pltpu.VMEM((2, COLS, WIDTH), jnp.bfloat16),
            pltpu.VMEM((2, COLS, WIDTH), f32),
            pltpu.SemaphoreType.DMA((3, 2)),
        ],
        compiler_params=PACK_PARAMS,
        name="pack_send",
    )(ids, *arrays)
    got = sibling(send)
    keep, drift = pl.pallas_call(
        keep_kernel,
        out_shape=[pltpu.VMEM((CHIPS, SHARE, BLOCK), f32), pltpu.VMEM(shape, f32)],
        in_specs=[SMEM, HBM, HBM, HBM],
        out_specs=[VMEM] * 2,
        scratch_shapes=[
            pltpu.VMEM(shape, jnp.bfloat16),
            pltpu.VMEM(shape, jnp.bfloat16),
            pltpu.VMEM(shape, f32),
            pltpu.SemaphoreType.DMA((3, 3)),
        ],
        compiler_params=PACK_PARAMS,
        cost_estimate=pl.CostEstimate(
            flops=1_000_000, bytes_accessed=4_000_000, transcendentals=0
        ),
        name="pack_keep",
    )(ids_after, *arrays)
    qt = jnp.swapaxes(initial_factor, 1, 2)
    shares = exchange_z(keep + got)
    inner, factor = pl.pallas_call(
        factor_kernel,
        out_shape=[
            jax.ShapeDtypeStruct((MROWS, BLOCK), f32),
            jax.ShapeDtypeStruct((FROWS, BLOCK), f32),
        ],
        in_specs=[SMEM, VMEM, VMEM],
        out_specs=[VMEM, VMEM],
        compiler_params=PARAMS,
        name="factor",
    )(ids, qt, shares)

    arrivals = []
    for line_core in (0, 1):
        arrivals.append(
            exchange_mixed(
                jnp.broadcast_to(jnp.concatenate([factor, inner]), (CHIPS, GROWS, BLOCK)),
                line_core,
            )
        )
        inner = jnp.sum(arrivals[-1][:, FROWS:], axis=0)
    own = pl.pallas_call(
        choose_kernel,
        out_shape=pltpu.VMEM((CHIPS * FROWS + MROWS, BLOCK), f32),
        in_specs=[SMEM, VMEM, VMEM],
        out_specs=VMEM,
        compiler_params=PARAMS,
        name="choose",
    )(ids, *arrivals)
    sib = sibling(own)

    next_weights, next_error, next_momentum, following = pl.pallas_call(
        lambda *refs: final_kernel(lax.axis_size("replica"), *refs),
        out_shape=[
            jax.ShapeDtypeStruct(shape, jnp.bfloat16),
            jax.ShapeDtypeStruct(shape, f32),
            jax.ShapeDtypeStruct(shape, f32),
            jax.ShapeDtypeStruct((MATS, RANK, COLS), f32),
        ],
        in_specs=[SMEM] + [VMEM] * 6,
        out_specs=[HBM, HBM, HBM, VMEM],
        scratch_shapes=[
            pltpu.VMEM((MATS, 6 * RANK, WIDTH), jnp.bfloat16),
            pltpu.VMEM(shape, jnp.bfloat16),
            pltpu.VMEM(shape, f32),
            pltpu.VMEM(shape, f32),
            pltpu.SemaphoreType.DMA((3, 3, len(PARTS))),
        ],
        compiler_params=PARAMS,
        name="final",
    )(ids, qt, own, sib, weights, momentum, drift)
    return (next_weights, next_error[None], next_momentum, jnp.swapaxes(following, 1, 2))


def solution(mesh):
    return jax.shard_map(
        local,
        mesh=mesh,
        in_specs=(
            P(None, None, "fsdp"),
            P("replica", None, None, "fsdp"),
            P("replica", None, None, "fsdp"),
            P(None, None, "fsdp"),
            P(),
        ),
        out_specs=(
            P(None, None, "fsdp"),
            P("replica", None, None, "fsdp"),
            P(None, None, "fsdp"),
            P(),
        ),
        check_vma=False,
    )
```

```python
import jax
import jax.numpy as jnp
from jax import lax
from jax.experimental import pallas as pl
from jax.experimental.pallas import tpu as pltpu
from jax.sharding import PartitionSpec as P

CHIPS = 16
BLOCK = 128
SIDE = BLOCK // 2
BLOCKS = 14
WIDTH = BLOCK * BLOCKS
MATS = 3
COLS = 32
RANK = 16
SHARE = MATS * COLS // 2
FROWS = SHARE // 2
MROWS = 8
GROWS = FROWS + MROWS
PAIR = RANK + COLS
HIGHEST = lax.Precision.HIGHEST
VMEM = pl.BlockSpec(memory_space=pltpu.VMEM)
SMEM = pl.BlockSpec(memory_space=pltpu.SMEM)
HBM = pl.BlockSpec(memory_space=pl.ANY)
PARAMS = pltpu.CompilerParams(vmem_limit_bytes=32 * 1024 * 1024)
PACK_PARAMS = pltpu.CompilerParams(vmem_limit_bytes=56 * 1024 * 1024)


def slot_of(chip, core):
    return ((13 * (chip - 3)) & 15) ^ (8 * core)


def chip_at(slot, core):
    return (3 + 8 * core + 5 * slot) % CHIPS


def gather_slot(chip):
    return 2 * (chip & 7) + (chip >> 3)


def gather_chip(slot):
    return (slot >> 1) + 8 * (slot & 1)


def swap_sides(x):
    return pltpu.roll(x, SIDE, 1)


def left_side(rows):
    return lax.broadcasted_iota(jnp.int32, (rows, BLOCK), 1) < SIDE


def corrected(w, lw, ce, mat, lanes):
    return (
        w[mat, :, lanes].astype(jnp.float32)
        - lw[mat, :, lanes].astype(jnp.float32)
        + ce[mat, :, lanes]
    )


def half_block(value, core):
    left = left_side(16)
    top, bottom = value[0:16], value[16:32]
    first = jnp.where(left, top, swap_sides(bottom))
    second = jnp.where(left, swap_sides(top), bottom)
    return jnp.where(core == 0, first, second)


def send_kernel(ids, w_hbm, lw_hbm, ce_hbm, send, ids_out, w, lw, ce, sems):
    other = 1 - ids[0]
    ids_out[0] = ids[0]
    copies = [
        [
            pltpu.make_async_copy(src.at[mat], dst.at[place], sems.at[kind, place])
            for kind, (src, dst) in enumerate(((ce_hbm, ce), (w_hbm, w), (lw_hbm, lw)))
        ]
        for place, mat in enumerate((1, 2 * other))
    ]
    for group in copies:
        for copy in group:
            copy.start()
    for block in range(BLOCKS, CHIPS):
        send[slot_of(block, other)] = jnp.zeros((SHARE, BLOCK), jnp.float32)
    for place, rows in enumerate((slice(COLS, SHARE), slice(0, COLS))):
        for copy in copies[place]:
            copy.wait()
        for block in range(BLOCKS):
            lanes = slice(block * BLOCK, (block + 1) * BLOCK)
            value = corrected(w, lw, ce, place, lanes)
            send[slot_of(block, other), rows] = half_block(value, other) if place == 0 else value


def keep_kernel(ids, w_hbm, lw_hbm, ce_hbm, keep, drift, w, lw, ce, sems):
    core = ids[0]
    copies = [
        [
            pltpu.make_async_copy(src.at[mat], dst.at[mat], sems.at[kind, mat])
            for kind, (src, dst) in enumerate(((ce_hbm, ce), (w_hbm, w), (lw_hbm, lw)))
        ]
        for mat in range(MATS)
    ]
    for group in copies:
        for copy in group:
            copy.start()
    for block in range(BLOCKS, CHIPS):
        keep[slot_of(block, core)] = jnp.zeros((SHARE, BLOCK), jnp.float32)
    for mat in range(MATS):
        for copy in copies[mat]:
            copy.wait()
        for block in range(BLOCKS):
            lanes = slice(block * BLOCK, (block + 1) * BLOCK)
            drift[mat, :, lanes] = corrected(w, lw, ce, mat, lanes)
    for block in range(BLOCKS):
        lanes = slice(block * BLOCK, (block + 1) * BLOCK)
        keep[slot_of(block, core), 0:COLS] = drift[2 * core, :, lanes]
        keep[slot_of(block, core), COLS:SHARE] = half_block(drift[1, :, lanes], core)


def outer(a, b):
    return lax.dot_general(
        a, b, (((1,), (1,)), ((), ())), precision=HIGHEST, preferred_element_type=jnp.float32
    )


def factor_kernel(ids, qt, got, inner, factor):
    core = ids[0]
    total = jnp.sum(got[...], axis=0)
    left = left_side(16)
    whole = total[0:COLS]
    half = total[COLS:SHARE]
    half = jnp.concatenate(
        [jnp.where(left, half, 0.0), jnp.where(left, swap_sides(half), 0.0)], axis=0
    )
    whole_factor = jnp.dot(
        qt[2 * core], whole, precision=HIGHEST, preferred_element_type=jnp.float32
    )
    half_factor = jnp.dot(qt[1], half, precision=HIGHEST, preferred_element_type=jnp.float32)
    factor[0:RANK] = whole_factor
    factor[RANK:FROWS] = half_factor[0:8] + swap_sides(half_factor[8:16])
    whole, half = outer(whole_factor, whole), outer(half_factor, half)
    inner[...] = jnp.concatenate([whole[0:8], whole[8:16], half[0:8], half[8:16]], axis=1)


def choose_kernel(ids, one, two, out):
    out[CHIPS * FROWS :] = jnp.sum(two[:, FROWS:GROWS], axis=0)
    for core, arrived in enumerate((one, two)):

        @pl.when(ids[0] == core)
        def _():
            for slot in range(CHIPS):
                out[slot * FROWS : slot * FROWS + FROWS] = arrived[slot, 0:FROWS]


def split(x):
    high = x.astype(jnp.bfloat16)
    rest = x - high.astype(jnp.float32)
    middle = rest.astype(jnp.bfloat16)
    return high, middle, (rest - middle.astype(jnp.float32)).astype(jnp.bfloat16)


def final_kernel(
    islands, ids, qt, own, sib, w, mom, drift,
    out_w, out_e, out_m, out_f, fac, buf_w, buf_e, buf_m, sems,
):
    first = ids[0] == 0

    rows = slice(CHIPS * FROWS, CHIPS * FROWS + MROWS)
    mine, other = own[rows], sib[rows]
    middle = pltpu.roll(mine + other, SIDE, 1)
    table = []
    for mat, rows in enumerate(
        (jnp.where(first, mine, other), middle, jnp.where(first, other, mine))
    ):
        rows = jnp.concatenate([rows[:, 0:COLS], rows[:, COLS : 2 * COLS]], axis=0)
        gram = outer(qt[mat], rows)
        rest = jnp.zeros((RANK, BLOCK - PAIR), jnp.float32)
        table.append(jnp.concatenate([gram, rows, rest], axis=1))
    table = jnp.stack(table)
    row = lax.broadcasted_iota(jnp.int32, table.shape, 1)
    small = table
    for step in range(0, RANK, 2):
        one = jnp.broadcast_to(table[:, :, step : step + 1], table.shape)
        two = jnp.broadcast_to(table[:, :, step + 1 : step + 2], table.shape)
        line = table[:, step : step + 1, :]
        pivot, cross = one[:, step : step + 1, :], two[:, step : step + 1, :]
        inverse = 1.0 / pivot
        ratio = one[:, step + 1 : step + 2, :] * inverse
        next_line = table[:, step + 1 : step + 2, :] - ratio * line
        next_pivot = two[:, step + 1 : step + 2, :] - ratio * cross
        next_scaled = next_line * (1.0 / next_pivot)
        scaled = (line - cross * next_scaled) * inverse
        here, below = row == step, row == step + 1
        small = jnp.where(here, line * lax.rsqrt(pivot), small)
        small = jnp.where(below, next_line * lax.rsqrt(next_pivot), small)
        rest = table - one * scaled - two * next_scaled
        table = jnp.where(here, scaled, jnp.where(below, next_scaled, rest))

    left = left_side(8)
    for block in range(BLOCKS):
        lanes = slice(block * BLOCK, (block + 1) * BLOCK)
        start = gather_slot(block) * FROWS
        mine, other = own[start : start + FROWS], sib[start : start + FROWS]
        low, high = jnp.where(first, mine, other), jnp.where(first, other, mine)
        low_half, high_half = low[RANK:FROWS], high[RANK:FROWS]
        half = jnp.concatenate(
            [
                jnp.where(left, low_half, swap_sides(high_half)),
                jnp.where(left, swap_sides(low_half), high_half),
            ],
            axis=0,
        )
        for mat, value in enumerate((low[0:RANK], half, high[0:RANK])):
            top, mid, last = split(value)
            for place, part in enumerate((top, mid, last, top, mid, top)):
                fac[mat, place * RANK : place * RANK + RANK, lanes] = part

    for mat in range(MATS):
        out_f[mat] = small[mat, :, RANK:PAIR] * (1.0 / islands)
        top, mid, last = split(table[mat, :, RANK:PAIR] * (1.0 / islands))
        parts = [x.astype(jnp.float32) for x in (top, top, top, mid, mid, last)]
        mixed = jnp.transpose(jnp.concatenate(parts, axis=0)).astype(jnp.bfloat16)
        for tile in range(7):
            lanes = slice(tile * 256, (tile + 1) * 256)
            approx = jnp.dot(mixed, fac[mat, :, lanes], preferred_element_type=jnp.float32)
            wide = w[mat, :, lanes].astype(jnp.float32)
            momentum = 0.9 * mom[mat, :, lanes] + approx
            buf_e[mat, :, lanes] = drift[mat, :, lanes] - approx
            buf_m[mat, :, lanes] = momentum
            buf_w[mat, :, lanes] = (wide - 0.7 * (approx + 0.9 * momentum)).astype(jnp.bfloat16)
        for kind, (buf, out) in enumerate(((buf_w, out_w), (buf_e, out_e), (buf_m, out_m))):
            pltpu.make_async_copy(buf.at[mat], out.at[mat], sems.at[kind, mat]).start()
    for mat in range(MATS):
        for kind, (buf, out) in enumerate(((buf_w, out_w), (buf_e, out_e), (buf_m, out_m))):
            pltpu.make_async_copy(buf.at[mat], out.at[mat], sems.at[kind, mat]).wait()


def sibling(x):
    return lax.ppermute(x, "replica", [(i, i ^ 1) for i in range(2 * CHIPS)])


def exchange_z(x):
    groups = [[2 * chip_at(slot, core) + core for slot in range(CHIPS)] for core in range(2)]
    return lax.all_to_all(x, "replica", 0, 0, axis_index_groups=groups, tiled=True)


def exchange_mixed(x, line_core):
    lines = [
        [(2 * gather_chip(slot) + line_core) * 16 + place for slot in range(CHIPS)]
        for place in range(16)
    ]
    planes = [
        [(2 * chip + 1 - line_core) * 16 + (5 * slot) % 16 for slot in range(16)]
        for chip in range(CHIPS)
    ]
    return lax.all_to_all(
        x, ("replica", "fsdp"), 0, 0, axis_index_groups=lines + planes, tiled=True
    )


def local(weights, local_weights, carried_error, momentum, initial_factor):
    f32 = jnp.float32
    ids = (lax.axis_index("replica") & 1).astype(jnp.int32).reshape(1)
    shape = (MATS, COLS, WIDTH)
    arrays = (weights, local_weights[0], carried_error[0])
    send, ids_after = pl.pallas_call(
        send_kernel,
        out_shape=[pltpu.VMEM((CHIPS, SHARE, BLOCK), f32), pltpu.SMEM((1,), jnp.int32)],
        in_specs=[SMEM, HBM, HBM, HBM],
        out_specs=[VMEM, SMEM],
        scratch_shapes=[
            pltpu.VMEM((2, COLS, WIDTH), jnp.bfloat16),
            pltpu.VMEM((2, COLS, WIDTH), jnp.bfloat16),
            pltpu.VMEM((2, COLS, WIDTH), f32),
            pltpu.SemaphoreType.DMA((3, 2)),
        ],
        compiler_params=PACK_PARAMS,
        name="pack_send",
    )(ids, *arrays)
    got = sibling(send)
    keep, drift = pl.pallas_call(
        keep_kernel,
        out_shape=[pltpu.VMEM((CHIPS, SHARE, BLOCK), f32), pltpu.VMEM(shape, f32)],
        in_specs=[SMEM, HBM, HBM, HBM],
        out_specs=[VMEM] * 2,
        scratch_shapes=[
            pltpu.VMEM(shape, jnp.bfloat16),
            pltpu.VMEM(shape, jnp.bfloat16),
            pltpu.VMEM(shape, f32),
            pltpu.SemaphoreType.DMA((3, 3)),
        ],
        compiler_params=PACK_PARAMS,
        cost_estimate=pl.CostEstimate(
            flops=1_000_000, bytes_accessed=4_000_000, transcendentals=0
        ),
        name="pack_keep",
    )(ids_after, *arrays)
    qt = jnp.swapaxes(initial_factor, 1, 2)
    shares = exchange_z(keep + got)
    inner, factor = pl.pallas_call(
        factor_kernel,
        out_shape=[
            jax.ShapeDtypeStruct((MROWS, BLOCK), f32),
            jax.ShapeDtypeStruct((FROWS, BLOCK), f32),
        ],
        in_specs=[SMEM, VMEM, VMEM],
        out_specs=[VMEM, VMEM],
        compiler_params=PARAMS,
        name="factor",
    )(ids, qt, shares)

    arrivals = []
    for line_core in (0, 1):
        arrivals.append(
            exchange_mixed(
                jnp.broadcast_to(jnp.concatenate([factor, inner]), (CHIPS, GROWS, BLOCK)),
                line_core,
            )
        )
        inner = jnp.sum(arrivals[-1][:, FROWS:], axis=0)
    own = pl.pallas_call(
        choose_kernel,
        out_shape=pltpu.VMEM((CHIPS * FROWS + MROWS, BLOCK), f32),
        in_specs=[SMEM, VMEM, VMEM],
        out_specs=VMEM,
        compiler_params=PARAMS,
        name="choose",
    )(ids, *arrivals)
    sib = sibling(own)

    next_weights, next_error, next_momentum, following = pl.pallas_call(
        lambda *refs: final_kernel(lax.axis_size("replica"), *refs),
        out_shape=[
            jax.ShapeDtypeStruct(shape, jnp.bfloat16),
            jax.ShapeDtypeStruct(shape, f32),
            jax.ShapeDtypeStruct(shape, f32),
            jax.ShapeDtypeStruct((MATS, RANK, COLS), f32),
        ],
        in_specs=[SMEM] + [VMEM] * 6,
        out_specs=[HBM, HBM, HBM, VMEM],
        scratch_shapes=[
            pltpu.VMEM((MATS, 6 * RANK, WIDTH), jnp.bfloat16),
            pltpu.VMEM(shape, jnp.bfloat16),
            pltpu.VMEM(shape, f32),
            pltpu.VMEM(shape, f32),
            pltpu.SemaphoreType.DMA((3, 3)),
        ],
        compiler_params=PARAMS,
        name="final",
    )(ids, qt, own, sib, weights, momentum, drift)
    return (next_weights, next_error[None], next_momentum, jnp.swapaxes(following, 1, 2))


def solution(mesh):
    return jax.shard_map(
        local,
        mesh=mesh,
        in_specs=(
            P(None, None, "fsdp"),
            P("replica", None, None, "fsdp"),
            P("replica", None, None, "fsdp"),
            P(None, None, "fsdp"),
            P(),
        ),
        out_specs=(
            P(None, None, "fsdp"),
            P("replica", None, None, "fsdp"),
            P(None, None, "fsdp"),
            P(),
        ),
        check_vma=False,
    )
```

```python
import jax
import jax.numpy as jnp
from jax import lax
from jax.experimental import pallas as pl
from jax.experimental.pallas import tpu as pltpu
from jax.sharding import PartitionSpec as P

CHIPS = 16
BLOCK = 128
SIDE = BLOCK // 2
BLOCKS = 14
WIDTH = BLOCK * BLOCKS
MATS = 3
COLS = 32
RANK = 16
SHARE = MATS * COLS // 2
FROWS = SHARE // 2
MROWS = 8
GROWS = FROWS + MROWS
PAIR = RANK + COLS
HIGHEST = lax.Precision.HIGHEST
VMEM = pl.BlockSpec(memory_space=pltpu.VMEM)
SMEM = pl.BlockSpec(memory_space=pltpu.SMEM)
HBM = pl.BlockSpec(memory_space=pl.ANY)
PARAMS = pltpu.CompilerParams(vmem_limit_bytes=32 * 1024 * 1024)
PACK_PARAMS = pltpu.CompilerParams(vmem_limit_bytes=56 * 1024 * 1024)


def slot_of(chip, core):
    return ((3 * (chip - 13)) & 15) ^ (8 * core)


def chip_at(slot, core):
    return (13 + 8 * core + 11 * slot) % CHIPS


def gather_slot(chip):
    return (9 * chip) % CHIPS


def swap_sides(x):
    return pltpu.roll(x, SIDE, 1)


def left_side(rows):
    return lax.broadcasted_iota(jnp.int32, (rows, BLOCK), 1) < SIDE


def corrected(w, lw, ce, mat, lanes):
    return (
        w[mat, :, lanes].astype(jnp.float32)
        - lw[mat, :, lanes].astype(jnp.float32)
        + ce[mat, :, lanes]
    )


def half_block(value, core):
    left = left_side(16)
    top, bottom = value[0:16], value[16:32]
    first = jnp.where(left, top, swap_sides(bottom))
    second = jnp.where(left, swap_sides(top), bottom)
    return jnp.where(core == 0, first, second)


def send_kernel(ids, w_hbm, lw_hbm, ce_hbm, send, ids_out, w, lw, ce, sems):
    other = 1 - ids[0]
    ids_out[0] = ids[0]
    copies = [
        [
            pltpu.make_async_copy(src.at[mat], dst.at[place], sems.at[kind, place])
            for kind, (src, dst) in enumerate(((ce_hbm, ce), (w_hbm, w), (lw_hbm, lw)))
        ]
        for place, mat in enumerate((1, 2 * other))
    ]
    for group in copies:
        for copy in group:
            copy.start()
    for block in range(BLOCKS, CHIPS):
        send[slot_of(block, other)] = jnp.zeros((SHARE, BLOCK), jnp.float32)
    for place, rows in enumerate((slice(COLS, SHARE), slice(0, COLS))):
        for copy in copies[place]:
            copy.wait()
        for block in range(BLOCKS):
            lanes = slice(block * BLOCK, (block + 1) * BLOCK)
            value = corrected(w, lw, ce, place, lanes)
            send[slot_of(block, other), rows] = half_block(value, other) if place == 0 else value


def keep_kernel(ids, w_hbm, lw_hbm, ce_hbm, keep, drift, w, lw, ce, sems):
    core = ids[0]
    copies = [
        [
            pltpu.make_async_copy(src.at[mat], dst.at[mat], sems.at[kind, mat])
            for kind, (src, dst) in enumerate(((ce_hbm, ce), (w_hbm, w), (lw_hbm, lw)))
        ]
        for mat in range(MATS)
    ]
    for group in copies:
        for copy in group:
            copy.start()
    for block in range(BLOCKS, CHIPS):
        keep[slot_of(block, core)] = jnp.zeros((SHARE, BLOCK), jnp.float32)
    for mat in range(MATS):
        for copy in copies[mat]:
            copy.wait()
        for block in range(BLOCKS):
            lanes = slice(block * BLOCK, (block + 1) * BLOCK)
            drift[mat, :, lanes] = corrected(w, lw, ce, mat, lanes)
    for block in range(BLOCKS):
        lanes = slice(block * BLOCK, (block + 1) * BLOCK)
        keep[slot_of(block, core), 0:COLS] = drift[2 * core, :, lanes]
        keep[slot_of(block, core), COLS:SHARE] = half_block(drift[1, :, lanes], core)


def outer(a, b):
    return lax.dot_general(
        a, b, (((1,), (1,)), ((), ())), precision=HIGHEST, preferred_element_type=jnp.float32
    )


def factor_kernel(ids, qt, got, inner, factor):
    core = ids[0]
    total = jnp.sum(got[...], axis=0)
    left = left_side(16)
    whole = total[0:COLS]
    half = total[COLS:SHARE]
    half = jnp.concatenate(
        [jnp.where(left, half, 0.0), jnp.where(left, swap_sides(half), 0.0)], axis=0
    )
    whole_factor = jnp.dot(
        qt[2 * core], whole, precision=HIGHEST, preferred_element_type=jnp.float32
    )
    half_factor = jnp.dot(qt[1], half, precision=HIGHEST, preferred_element_type=jnp.float32)
    factor[0:RANK] = whole_factor
    factor[RANK:FROWS] = half_factor[0:8] + swap_sides(half_factor[8:16])
    whole, half = outer(whole_factor, whole), outer(half_factor, half)
    inner[...] = jnp.concatenate([whole[0:8], whole[8:16], half[0:8], half[8:16]], axis=1)


def choose_kernel(ids, one, two, out):
    out[CHIPS * FROWS :] = jnp.sum(two[:, FROWS:GROWS], axis=0)
    for core, arrived in enumerate((one, two)):

        @pl.when(ids[0] == core)
        def _():
            for slot in range(CHIPS):
                out[slot * FROWS : slot * FROWS + FROWS] = arrived[slot, 0:FROWS]


def split(x):
    high = x.astype(jnp.bfloat16)
    rest = x - high.astype(jnp.float32)
    middle = rest.astype(jnp.bfloat16)
    return high, middle, (rest - middle.astype(jnp.float32)).astype(jnp.bfloat16)


def final_kernel(
    islands, ids, qt, own, sib, w, mom, drift,
    out_w, out_e, out_m, out_f, fac, buf_w, buf_e, buf_m, sems,
):
    first = ids[0] == 0

    rows = slice(CHIPS * FROWS, CHIPS * FROWS + MROWS)
    mine, other = own[rows], sib[rows]
    middle = pltpu.roll(mine + other, SIDE, 1)
    table = []
    for mat, rows in enumerate(
        (jnp.where(first, mine, other), middle, jnp.where(first, other, mine))
    ):
        rows = jnp.concatenate([rows[:, 0:COLS], rows[:, COLS : 2 * COLS]], axis=0)
        gram = outer(qt[mat], rows)
        rest = jnp.zeros((RANK, BLOCK - PAIR), jnp.float32)
        table.append(jnp.concatenate([gram, rows, rest], axis=1))
    table = jnp.stack(table)
    row = lax.broadcasted_iota(jnp.int32, table.shape, 1)
    small = table
    for step in range(0, RANK, 2):
        one = jnp.broadcast_to(table[:, :, step : step + 1], table.shape)
        two = jnp.broadcast_to(table[:, :, step + 1 : step + 2], table.shape)
        line = table[:, step : step + 1, :]
        pivot, cross = one[:, step : step + 1, :], two[:, step : step + 1, :]
        inverse = 1.0 / pivot
        ratio = one[:, step + 1 : step + 2, :] * inverse
        next_line = table[:, step + 1 : step + 2, :] - ratio * line
        next_pivot = two[:, step + 1 : step + 2, :] - ratio * cross
        next_scaled = next_line * (1.0 / next_pivot)
        scaled = (line - cross * next_scaled) * inverse
        here, below = row == step, row == step + 1
        small = jnp.where(here, line * lax.rsqrt(pivot), small)
        small = jnp.where(below, next_line * lax.rsqrt(next_pivot), small)
        rest = table - one * scaled - two * next_scaled
        table = jnp.where(here, scaled, jnp.where(below, next_scaled, rest))

    left = left_side(8)
    for block in range(BLOCKS):
        lanes = slice(block * BLOCK, (block + 1) * BLOCK)
        start = gather_slot(block) * FROWS
        mine, other = own[start : start + FROWS], sib[start : start + FROWS]
        low, high = jnp.where(first, mine, other), jnp.where(first, other, mine)
        low_half, high_half = low[RANK:FROWS], high[RANK:FROWS]
        half = jnp.concatenate(
            [
                jnp.where(left, low_half, swap_sides(high_half)),
                jnp.where(left, swap_sides(low_half), high_half),
            ],
            axis=0,
        )
        for mat, value in enumerate((low[0:RANK], half, high[0:RANK])):
            top, mid, last = split(value)
            for place, part in enumerate((top, mid, last, top, mid, top)):
                fac[mat, place * RANK : place * RANK + RANK, lanes] = part

    for mat in range(MATS):
        out_f[mat] = small[mat, :, RANK:PAIR] * (1.0 / islands)
        top, mid, last = split(table[mat, :, RANK:PAIR] * (1.0 / islands))
        parts = [x.astype(jnp.float32) for x in (top, top, top, mid, mid, last)]
        mixed = jnp.transpose(jnp.concatenate(parts, axis=0)).astype(jnp.bfloat16)
        for tile in range(7):
            lanes = slice(tile * 256, (tile + 1) * 256)
            approx = jnp.dot(mixed, fac[mat, :, lanes], preferred_element_type=jnp.float32)
            wide = w[mat, :, lanes].astype(jnp.float32)
            momentum = 0.9 * mom[mat, :, lanes] + approx
            buf_e[mat, :, lanes] = drift[mat, :, lanes] - approx
            buf_m[mat, :, lanes] = momentum
            buf_w[mat, :, lanes] = (wide - 0.7 * (approx + 0.9 * momentum)).astype(jnp.bfloat16)
        for kind, (buf, out) in enumerate(((buf_w, out_w), (buf_e, out_e), (buf_m, out_m))):
            pltpu.make_async_copy(buf.at[mat], out.at[mat], sems.at[kind, mat]).start()
    for mat in range(MATS):
        for kind, (buf, out) in enumerate(((buf_w, out_w), (buf_e, out_e), (buf_m, out_m))):
            pltpu.make_async_copy(buf.at[mat], out.at[mat], sems.at[kind, mat]).wait()


def sibling(x):
    return lax.ppermute(x, "replica", [(i, i ^ 1) for i in range(2 * CHIPS)])


def exchange_z(x):
    groups = [[2 * chip_at(slot, core) + core for slot in range(CHIPS)] for core in range(2)]
    return lax.all_to_all(x, "replica", 0, 0, axis_index_groups=groups, tiled=True)


def exchange_mixed(x, line_core):
    lines = [
        [(2 * gather_slot(slot) + line_core) * 16 + place for slot in range(CHIPS)]
        for place in range(16)
    ]
    planes = [
        [(2 * chip + 1 - line_core) * 16 + (5 * slot) % 16 for slot in range(16)]
        for chip in range(CHIPS)
    ]
    return lax.all_to_all(
        x, ("replica", "fsdp"), 0, 0, axis_index_groups=lines + planes, tiled=True
    )


def local(weights, local_weights, carried_error, momentum, initial_factor):
    f32 = jnp.float32
    ids = (lax.axis_index("replica") & 1).astype(jnp.int32).reshape(1)
    shape = (MATS, COLS, WIDTH)
    arrays = (weights, local_weights[0], carried_error[0])
    send, ids_after = pl.pallas_call(
        send_kernel,
        out_shape=[pltpu.VMEM((CHIPS, SHARE, BLOCK), f32), pltpu.SMEM((1,), jnp.int32)],
        in_specs=[SMEM, HBM, HBM, HBM],
        out_specs=[VMEM, SMEM],
        scratch_shapes=[
            pltpu.VMEM((2, COLS, WIDTH), jnp.bfloat16),
            pltpu.VMEM((2, COLS, WIDTH), jnp.bfloat16),
            pltpu.VMEM((2, COLS, WIDTH), f32),
            pltpu.SemaphoreType.DMA((3, 2)),
        ],
        compiler_params=PACK_PARAMS,
        name="pack_send",
    )(ids, *arrays)
    got = sibling(send)
    keep, drift = pl.pallas_call(
        keep_kernel,
        out_shape=[pltpu.VMEM((CHIPS, SHARE, BLOCK), f32), pltpu.VMEM(shape, f32)],
        in_specs=[SMEM, HBM, HBM, HBM],
        out_specs=[VMEM] * 2,
        scratch_shapes=[
            pltpu.VMEM(shape, jnp.bfloat16),
            pltpu.VMEM(shape, jnp.bfloat16),
            pltpu.VMEM(shape, f32),
            pltpu.SemaphoreType.DMA((3, 3)),
        ],
        compiler_params=PACK_PARAMS,
        cost_estimate=pl.CostEstimate(
            flops=1_000_000, bytes_accessed=4_000_000, transcendentals=0
        ),
        name="pack_keep",
    )(ids_after, *arrays)
    qt = jnp.swapaxes(initial_factor, 1, 2)
    shares = exchange_z(keep + got)
    inner, factor = pl.pallas_call(
        factor_kernel,
        out_shape=[
            jax.ShapeDtypeStruct((MROWS, BLOCK), f32),
            jax.ShapeDtypeStruct((FROWS, BLOCK), f32),
        ],
        in_specs=[SMEM, VMEM, VMEM],
        out_specs=[VMEM, VMEM],
        compiler_params=PARAMS,
        name="factor",
    )(ids, qt, shares)

    arrivals = []
    for line_core in (0, 1):
        arrivals.append(
            exchange_mixed(
                jnp.broadcast_to(jnp.concatenate([factor, inner]), (CHIPS, GROWS, BLOCK)),
                line_core,
            )
        )
        inner = jnp.sum(arrivals[-1][:, FROWS:], axis=0)
    own = pl.pallas_call(
        choose_kernel,
        out_shape=pltpu.VMEM((CHIPS * FROWS + MROWS, BLOCK), f32),
        in_specs=[SMEM, VMEM, VMEM],
        out_specs=VMEM,
        compiler_params=PARAMS,
        name="choose",
    )(ids, *arrivals)
    sib = sibling(own)

    next_weights, next_error, next_momentum, following = pl.pallas_call(
        lambda *refs: final_kernel(lax.axis_size("replica"), *refs),
        out_shape=[
            jax.ShapeDtypeStruct(shape, jnp.bfloat16),
            jax.ShapeDtypeStruct(shape, f32),
            jax.ShapeDtypeStruct(shape, f32),
            jax.ShapeDtypeStruct((MATS, RANK, COLS), f32),
        ],
        in_specs=[SMEM] + [VMEM] * 6,
        out_specs=[HBM, HBM, HBM, VMEM],
        scratch_shapes=[
            pltpu.VMEM((MATS, 6 * RANK, WIDTH), jnp.bfloat16),
            pltpu.VMEM(shape, jnp.bfloat16),
            pltpu.VMEM(shape, f32),
            pltpu.VMEM(shape, f32),
            pltpu.SemaphoreType.DMA((3, 3)),
        ],
        compiler_params=PARAMS,
        name="final",
    )(ids, qt, own, sib, weights, momentum, drift)
    return (next_weights, next_error[None], next_momentum, jnp.swapaxes(following, 1, 2))


def solution(mesh):
    return jax.shard_map(
        local,
        mesh=mesh,
        in_specs=(
            P(None, None, "fsdp"),
            P("replica", None, None, "fsdp"),
            P("replica", None, None, "fsdp"),
            P(None, None, "fsdp"),
            P(),
        ),
        out_specs=(
            P(None, None, "fsdp"),
            P("replica", None, None, "fsdp"),
            P(None, None, "fsdp"),
            P(),
        ),
        check_vma=False,
    )
```

```python
import jax
import jax.numpy as jnp
from jax import lax
from jax.experimental import pallas as pl
from jax.experimental.pallas import tpu as pltpu
from jax.sharding import PartitionSpec as P

CHIPS = 16
BLOCK = 128
SIDE = BLOCK // 2
BLOCKS = 14
WIDTH = BLOCK * BLOCKS
MATS = 3
COLS = 32
RANK = 16
SHARE = MATS * COLS // 2
FROWS = SHARE // 2
MROWS = 8
GROWS = FROWS + MROWS
PAIR = RANK + COLS
HIGHEST = lax.Precision.HIGHEST
VMEM = pl.BlockSpec(memory_space=pltpu.VMEM)
SMEM = pl.BlockSpec(memory_space=pltpu.SMEM)
HBM = pl.BlockSpec(memory_space=pl.ANY)
PARAMS = pltpu.CompilerParams(vmem_limit_bytes=32 * 1024 * 1024)
PACK_PARAMS = pltpu.CompilerParams(vmem_limit_bytes=56 * 1024 * 1024)


def slot_of(chip, core):
    return ((3 * (chip - 5)) & 15) ^ (8 * core)


def chip_at(slot, core):
    return (5 + 8 * core + 11 * slot) % CHIPS


def gather_slot(chip):
    return (9 * chip) % CHIPS


def swap_sides(x):
    return pltpu.roll(x, SIDE, 1)


def left_side(rows):
    return lax.broadcasted_iota(jnp.int32, (rows, BLOCK), 1) < SIDE


def corrected(w, lw, ce, mat, lanes):
    return (
        w[mat, :, lanes].astype(jnp.float32)
        - lw[mat, :, lanes].astype(jnp.float32)
        + ce[mat, :, lanes]
    )


def half_block(value, core):
    left = left_side(16)
    top, bottom = value[0:16], value[16:32]
    first = jnp.where(left, top, swap_sides(bottom))
    second = jnp.where(left, swap_sides(top), bottom)
    return jnp.where(core == 0, first, second)


def send_kernel(ids, w_hbm, lw_hbm, ce_hbm, send, ids_out, w, lw, ce, sems):
    other = 1 - ids[0]
    ids_out[0] = ids[0]
    copies = [
        [
            pltpu.make_async_copy(src.at[mat], dst.at[place], sems.at[kind, place])
            for kind, (src, dst) in enumerate(((ce_hbm, ce), (w_hbm, w), (lw_hbm, lw)))
        ]
        for place, mat in enumerate((1, 2 * other))
    ]
    for group in copies:
        for copy in group:
            copy.start()
    for block in range(BLOCKS, CHIPS):
        send[slot_of(block, other)] = jnp.zeros((SHARE, BLOCK), jnp.float32)
    for place, rows in enumerate((slice(COLS, SHARE), slice(0, COLS))):
        for copy in copies[place]:
            copy.wait()
        for block in range(BLOCKS):
            lanes = slice(block * BLOCK, (block + 1) * BLOCK)
            value = corrected(w, lw, ce, place, lanes)
            send[slot_of(block, other), rows] = half_block(value, other) if place == 0 else value


def keep_kernel(ids, w_hbm, lw_hbm, ce_hbm, keep, drift, w, lw, ce, sems):
    core = ids[0]
    copies = [
        [
            pltpu.make_async_copy(src.at[mat], dst.at[mat], sems.at[kind, mat])
            for kind, (src, dst) in enumerate(((ce_hbm, ce), (w_hbm, w), (lw_hbm, lw)))
        ]
        for mat in range(MATS)
    ]
    for group in copies:
        for copy in group:
            copy.start()
    for block in range(BLOCKS, CHIPS):
        keep[slot_of(block, core)] = jnp.zeros((SHARE, BLOCK), jnp.float32)
    for mat in range(MATS):
        for copy in copies[mat]:
            copy.wait()
        for block in range(BLOCKS):
            lanes = slice(block * BLOCK, (block + 1) * BLOCK)
            drift[mat, :, lanes] = corrected(w, lw, ce, mat, lanes)
    for block in range(BLOCKS):
        lanes = slice(block * BLOCK, (block + 1) * BLOCK)
        keep[slot_of(block, core), 0:COLS] = drift[2 * core, :, lanes]
        keep[slot_of(block, core), COLS:SHARE] = half_block(drift[1, :, lanes], core)


def outer(a, b):
    return lax.dot_general(
        a, b, (((1,), (1,)), ((), ())), precision=HIGHEST, preferred_element_type=jnp.float32
    )


def factor_kernel(ids, qt, got, inner, factor):
    core = ids[0]
    total = jnp.sum(got[...], axis=0)
    left = left_side(16)
    whole = total[0:COLS]
    half = total[COLS:SHARE]
    half = jnp.concatenate(
        [jnp.where(left, half, 0.0), jnp.where(left, swap_sides(half), 0.0)], axis=0
    )
    whole_factor = jnp.dot(
        qt[2 * core], whole, precision=HIGHEST, preferred_element_type=jnp.float32
    )
    half_factor = jnp.dot(qt[1], half, precision=HIGHEST, preferred_element_type=jnp.float32)
    factor[0:RANK] = whole_factor
    factor[RANK:FROWS] = half_factor[0:8] + swap_sides(half_factor[8:16])
    whole, half = outer(whole_factor, whole), outer(half_factor, half)
    inner[...] = jnp.concatenate([whole[0:8], whole[8:16], half[0:8], half[8:16]], axis=1)


def choose_kernel(ids, one, two, out):
    out[CHIPS * FROWS :] = jnp.sum(two[:, FROWS:GROWS], axis=0)
    for core, arrived in enumerate((one, two)):

        @pl.when(ids[0] == core)
        def _():
            for slot in range(CHIPS):
                out[slot * FROWS : slot * FROWS + FROWS] = arrived[slot, 0:FROWS]


def split(x):
    high = x.astype(jnp.bfloat16)
    rest = x - high.astype(jnp.float32)
    middle = rest.astype(jnp.bfloat16)
    return high, middle, (rest - middle.astype(jnp.float32)).astype(jnp.bfloat16)


def final_kernel(
    islands, ids, qt, own, sib, w, mom, drift,
    out_w, out_e, out_m, out_f, fac, buf_w, buf_e, buf_m, sems,
):
    first = ids[0] == 0

    rows = slice(CHIPS * FROWS, CHIPS * FROWS + MROWS)
    mine, other = own[rows], sib[rows]
    middle = pltpu.roll(mine + other, SIDE, 1)
    table = []
    for mat, rows in enumerate(
        (jnp.where(first, mine, other), middle, jnp.where(first, other, mine))
    ):
        rows = jnp.concatenate([rows[:, 0:COLS], rows[:, COLS : 2 * COLS]], axis=0)
        gram = outer(qt[mat], rows)
        rest = jnp.zeros((RANK, BLOCK - PAIR), jnp.float32)
        table.append(jnp.concatenate([gram, rows, rest], axis=1))
    table = jnp.stack(table)
    row = lax.broadcasted_iota(jnp.int32, table.shape, 1)
    small = table
    for step in range(0, RANK, 2):
        one = jnp.broadcast_to(table[:, :, step : step + 1], table.shape)
        two = jnp.broadcast_to(table[:, :, step + 1 : step + 2], table.shape)
        line = table[:, step : step + 1, :]
        pivot, cross = one[:, step : step + 1, :], two[:, step : step + 1, :]
        inverse = 1.0 / pivot
        ratio = one[:, step + 1 : step + 2, :] * inverse
        next_line = table[:, step + 1 : step + 2, :] - ratio * line
        next_pivot = two[:, step + 1 : step + 2, :] - ratio * cross
        next_scaled = next_line * (1.0 / next_pivot)
        scaled = (line - cross * next_scaled) * inverse
        here, below = row == step, row == step + 1
        small = jnp.where(here, line * lax.rsqrt(pivot), small)
        small = jnp.where(below, next_line * lax.rsqrt(next_pivot), small)
        rest = table - one * scaled - two * next_scaled
        table = jnp.where(here, scaled, jnp.where(below, next_scaled, rest))

    left = left_side(8)
    for block in range(BLOCKS):
        lanes = slice(block * BLOCK, (block + 1) * BLOCK)
        start = gather_slot(block) * FROWS
        mine, other = own[start : start + FROWS], sib[start : start + FROWS]
        low, high = jnp.where(first, mine, other), jnp.where(first, other, mine)
        low_half, high_half = low[RANK:FROWS], high[RANK:FROWS]
        half = jnp.concatenate(
            [
                jnp.where(left, low_half, swap_sides(high_half)),
                jnp.where(left, swap_sides(low_half), high_half),
            ],
            axis=0,
        )
        for mat, value in enumerate((low[0:RANK], half, high[0:RANK])):
            top, mid, last = split(value)
            for place, part in enumerate((top, mid, last, top, mid, top)):
                fac[mat, place * RANK : place * RANK + RANK, lanes] = part

    for mat in range(MATS):
        out_f[mat] = small[mat, :, RANK:PAIR] * (1.0 / islands)
        top, mid, last = split(table[mat, :, RANK:PAIR] * (1.0 / islands))
        parts = [x.astype(jnp.float32) for x in (top, top, top, mid, mid, last)]
        mixed = jnp.transpose(jnp.concatenate(parts, axis=0)).astype(jnp.bfloat16)
        for tile in range(7):
            lanes = slice(tile * 256, (tile + 1) * 256)
            approx = jnp.dot(mixed, fac[mat, :, lanes], preferred_element_type=jnp.float32)
            wide = w[mat, :, lanes].astype(jnp.float32)
            momentum = 0.9 * mom[mat, :, lanes] + approx
            buf_e[mat, :, lanes] = drift[mat, :, lanes] - approx
            buf_m[mat, :, lanes] = momentum
            buf_w[mat, :, lanes] = (wide - 0.7 * (approx + 0.9 * momentum)).astype(jnp.bfloat16)
        for kind, (buf, out) in enumerate(((buf_w, out_w), (buf_e, out_e), (buf_m, out_m))):
            pltpu.make_async_copy(buf.at[mat], out.at[mat], sems.at[kind, mat]).start()
    for mat in range(MATS):
        for kind, (buf, out) in enumerate(((buf_w, out_w), (buf_e, out_e), (buf_m, out_m))):
            pltpu.make_async_copy(buf.at[mat], out.at[mat], sems.at[kind, mat]).wait()


def sibling(x):
    return lax.ppermute(x, "replica", [(i, i ^ 1) for i in range(2 * CHIPS)])


def exchange_z(x):
    groups = [[2 * chip_at(slot, core) + core for slot in range(CHIPS)] for core in range(2)]
    return lax.all_to_all(x, "replica", 0, 0, axis_index_groups=groups, tiled=True)


def exchange_mixed(x, line_core):
    lines = [
        [(2 * gather_slot(slot) + line_core) * 16 + place for slot in range(CHIPS)]
        for place in range(16)
    ]
    planes = [
        [(2 * chip + 1 - line_core) * 16 + (5 * slot) % 16 for slot in range(16)]
        for chip in range(CHIPS)
    ]
    return lax.all_to_all(
        x, ("replica", "fsdp"), 0, 0, axis_index_groups=lines + planes, tiled=True
    )


def local(weights, local_weights, carried_error, momentum, initial_factor):
    f32 = jnp.float32
    ids = (lax.axis_index("replica") & 1).astype(jnp.int32).reshape(1)
    shape = (MATS, COLS, WIDTH)
    arrays = (weights, local_weights[0], carried_error[0])
    send, ids_after = pl.pallas_call(
        send_kernel,
        out_shape=[pltpu.VMEM((CHIPS, SHARE, BLOCK), f32), pltpu.SMEM((1,), jnp.int32)],
        in_specs=[SMEM, HBM, HBM, HBM],
        out_specs=[VMEM, SMEM],
        scratch_shapes=[
            pltpu.VMEM((2, COLS, WIDTH), jnp.bfloat16),
            pltpu.VMEM((2, COLS, WIDTH), jnp.bfloat16),
            pltpu.VMEM((2, COLS, WIDTH), f32),
            pltpu.SemaphoreType.DMA((3, 2)),
        ],
        compiler_params=PACK_PARAMS,
        name="pack_send",
    )(ids, *arrays)
    got = sibling(send)
    keep, drift = pl.pallas_call(
        keep_kernel,
        out_shape=[pltpu.VMEM((CHIPS, SHARE, BLOCK), f32), pltpu.VMEM(shape, f32)],
        in_specs=[SMEM, HBM, HBM, HBM],
        out_specs=[VMEM] * 2,
        scratch_shapes=[
            pltpu.VMEM(shape, jnp.bfloat16),
            pltpu.VMEM(shape, jnp.bfloat16),
            pltpu.VMEM(shape, f32),
            pltpu.SemaphoreType.DMA((3, 3)),
        ],
        compiler_params=PACK_PARAMS,
        cost_estimate=pl.CostEstimate(
            flops=1_000_000, bytes_accessed=4_000_000, transcendentals=0
        ),
        name="pack_keep",
    )(ids_after, *arrays)
    qt = jnp.swapaxes(initial_factor, 1, 2)
    shares = exchange_z(keep + got)
    inner, factor = pl.pallas_call(
        factor_kernel,
        out_shape=[
            jax.ShapeDtypeStruct((MROWS, BLOCK), f32),
            jax.ShapeDtypeStruct((FROWS, BLOCK), f32),
        ],
        in_specs=[SMEM, VMEM, VMEM],
        out_specs=[VMEM, VMEM],
        compiler_params=PARAMS,
        name="factor",
    )(ids, qt, shares)

    arrivals = []
    for line_core in (0, 1):
        arrivals.append(
            exchange_mixed(
                jnp.broadcast_to(jnp.concatenate([factor, inner]), (CHIPS, GROWS, BLOCK)),
                line_core,
            )
        )
        inner = jnp.sum(arrivals[-1][:, FROWS:], axis=0)
    own = pl.pallas_call(
        choose_kernel,
        out_shape=pltpu.VMEM((CHIPS * FROWS + MROWS, BLOCK), f32),
        in_specs=[SMEM, VMEM, VMEM],
        out_specs=VMEM,
        compiler_params=PARAMS,
        name="choose",
    )(ids, *arrivals)
    sib = sibling(own)

    next_weights, next_error, next_momentum, following = pl.pallas_call(
        lambda *refs: final_kernel(lax.axis_size("replica"), *refs),
        out_shape=[
            jax.ShapeDtypeStruct(shape, jnp.bfloat16),
            jax.ShapeDtypeStruct(shape, f32),
            jax.ShapeDtypeStruct(shape, f32),
            jax.ShapeDtypeStruct((MATS, RANK, COLS), f32),
        ],
        in_specs=[SMEM] + [VMEM] * 6,
        out_specs=[HBM, HBM, HBM, VMEM],
        scratch_shapes=[
            pltpu.VMEM((MATS, 6 * RANK, WIDTH), jnp.bfloat16),
            pltpu.VMEM(shape, jnp.bfloat16),
            pltpu.VMEM(shape, f32),
            pltpu.VMEM(shape, f32),
            pltpu.SemaphoreType.DMA((3, 3)),
        ],
        compiler_params=PARAMS,
        name="final",
    )(ids, qt, own, sib, weights, momentum, drift)
    return (next_weights, next_error[None], next_momentum, jnp.swapaxes(following, 1, 2))


def solution(mesh):
    return jax.shard_map(
        local,
        mesh=mesh,
        in_specs=(
            P(None, None, "fsdp"),
            P("replica", None, None, "fsdp"),
            P("replica", None, None, "fsdp"),
            P(None, None, "fsdp"),
            P(),
        ),
        out_specs=(
            P(None, None, "fsdp"),
            P("replica", None, None, "fsdp"),
            P(None, None, "fsdp"),
            P(),
        ),
        check_vma=False,
    )
```
